32 devices in a mesh: section: 4 (over x, core), dp: 4 (over z), tensor: 2 (over y).
Axes of the slice: x: 2, y: 2, z: 4, core: 2. Of those that a mesh axis runs over, the one named last changes fastest.
Arguments:
- tokens: bfloat16 [16384, 512], P('dp'), may hold values from -6 to 6
- attn_gain: float32 [2, 512], replicated, may hold values from 0.5 to 1.5
- attention_input_weight: bfloat16 [2, 512, 2048], P(None, None, 'tensor'), may hold values from -0.44194174 to 0.44194174, as said below
- attn_out: bfloat16 [2, 512, 512], P(None, 'tensor'), may hold values from -1 to 1
- ffn_gain: float32 [2, 512], replicated, may hold values from 0.5 to 1.5
- ffn_in: bfloat16 [2, 512, 2048], P(None, None, 'tensor'), may hold values from -0.25 to 0.25
- ffn_out: bfloat16 [2, 2048, 512], P(None, 'tensor'), may hold values from -0.25 to 0.25
- cotangent: bfloat16 [16384, 512], P('dp'), may hold values from -6 to 6
Outputs:
- output: bfloat16 [16384, 512], P('dp', 'section')
- input_grad: bfloat16 [16384, 512], P('dp', 'section')
- attn_in_grad: float32 [2, 512, 2048], P(None, None, 'tensor')
- attn_out_grad: float32 [2, 512, 512], P(None, 'tensor')
- attn_gain_grad: float32 [2, 512], replicated
- ffn_in_grad: float32 [2, 512, 2048], P(None, None, 'tensor')
- ffn_out_grad: float32 [2, 2048, 512], P(None, 'tensor')
- ffn_gain_grad: float32 [2, 512], replicated
- slot_mean: float32 [2, 512], P(None, 'tensor')
The draws below stay inside these ranges and needn't reach their ends.
Inputs may be any that keep to these rules, and one draw needn't show every extreme that they name: Entries of attention_input_weight are at most 10 / sqrt(512) in magnitude.
All inputs are finite; a program needn't handle non-finite values.
Results may differ from the reference program's by a relative error of at most 0.015.
Values may be sent and summed in bfloat16 or wider, within the bound.
A program may use at most 192 MiB of HBM per device.

```python
import jax
import jax.numpy as jnp
from jax import lax

D = 512
HEADS = 8
HEAD_SIZE = 64
MEMORY_SLOTS = 64
FF = 2048
LAYERS = 2
SPAN = 1024
BLOCK = 512
TOKENS = 16384


control_boost = 2.5


def draw_attention_input_weight(key, part):
    key = jax.random.fold_in(key, 11)
    per_head_width = 3 * HEAD_SIZE + MEMORY_SLOTS
    full_shape = (LAYERS, D, HEADS * per_head_width)
    drawn_vals = jnp.clip(jax.random.normal(key, full_shape, jnp.float32), -4.0, 4.0)
    column = jnp.arange(HEADS * per_head_width) % per_head_width
    col_scale = jnp.where(column >= 3 * HEAD_SIZE, control_boost, 1.0) * D ** (-0.5)
    return (drawn_vals * col_scale).astype(jnp.bfloat16)


def shard_levels(key, shape, cuts, smallest, largest):
    factor_of = 1.0
    for position, blocks in cuts:
        heights = jax.random.uniform(jax.random.fold_in(jax.random.fold_in(key, 6), position), (blocks,), jnp.float32, smallest / len(cuts), largest / len(cuts))
        factor_of = factor_of * jnp.repeat(jnp.exp(heights), shape[position] // blocks).reshape((-1,) + (1,) * (len(shape) - 1 - position))
    return factor_of


def scatter_about(own_key, shape, scale, most, cuts=(), held_as=jnp.bfloat16):
    level = shard_levels(own_key, shape, cuts, -0.22, 0.18) if cuts else 1.0
    array = jax.random.normal(own_key, shape, jnp.float32) * scale * level
    return jnp.minimum(jnp.maximum(array, -most), most).astype(held_as)


def setup_inputs(seed: int = 0) -> dict:
    key_of = jax.random.split(jax.random.key(seed), 9)
    tokens = scatter_about(key_of[0], (TOKENS, D), 1.0, 6.0, ((0, 4),))
    attn_gain = jnp.clip(1.0 + 0.1 * jax.random.normal(key_of[1], (LAYERS, D), jnp.float32), 0.5, 1.5)
    attention_input_weight = draw_attention_input_weight(jax.random.fold_in(key_of[8], 71), 0)
    attn_out = scatter_about(key_of[3], (LAYERS, HEADS * HEAD_SIZE, D), (HEADS * HEAD_SIZE // 16) ** -0.5, 1.0, ((1, 2),))
    ffn_gain = jnp.clip(1.0 + 0.1 * jax.random.normal(key_of[4], (LAYERS, D), jnp.float32), 0.5, 1.5)
    ffn_in = scatter_about(key_of[5], (LAYERS, D, FF), D ** -0.5, 0.25, ((2, 2),))
    ffn_out = scatter_about(key_of[6], (LAYERS, FF, D), (FF // 4) ** -0.5, 0.25, ((1, 2),))
    cotangent = scatter_about(key_of[7], (TOKENS, D), 1.0, 6.0, ((0, 4),))
    return dict(tokens=tokens, attn_gain=attn_gain, attention_input_weight=attention_input_weight, attn_out=attn_out, ffn_gain=ffn_gain, ffn_in=ffn_in, ffn_out=ffn_out, cotangent=cotangent)


@jax.custom_vjp
def low(v):
    return lax.optimization_barrier(v.astype(jnp.bfloat16)).astype(jnp.float32)

@jax.custom_vjp
def low_back(v):
    return v

def low_keep(v):
    return (low(v), None)

def low_pass(kept, grad):
    return (grad,)

def back_keep(v):
    return (v, None)

def back_low(kept, grad):
    return (low(grad),)
low.defvjp(low_keep, low_pass)
low_back.defvjp(back_keep, back_low)
highest = lax.Precision.HIGHEST
norm_eps = 1e-05

def rms_scale(hidden, gain):
    mean_sq = lax.optimization_barrier(jnp.mean(hidden * hidden, axis=-1, keepdims=True))
    return hidden * lax.rsqrt(mean_sq + norm_eps) * gain

def slot_block(carried, pieces):
    state_keys, state_values, slot_total = carried
    queries, keys_in, values_in, control = pieces
    sequence_length = queries.shape[0]
    causal = (jnp.arange(sequence_length)[:, None] >= jnp.arange(sequence_length)[None, :]).astype(jnp.float32)
    running = slot_total[None] + jnp.einsum('ts,shn->thn', causal, control, precision=highest)
    paired = jnp.einsum('thd,shd->hts', queries, keys_in, precision=highest) * causal[None]
    numerator = jnp.einsum('thd,hnd->thn', queries, state_keys, precision=highest) + jnp.einsum('hts,shn->thn', paired, control, precision=highest)
    scores = numerator / running * queries.shape[-1] ** (-0.5)
    row_max = lax.optimization_barrier(jnp.max(scores, axis=-1, keepdims=True))
    shifted = jnp.exp(scores - row_max)
    attend = shifted / lax.optimization_barrier(jnp.sum(shifted, axis=-1, keepdims=True))
    shares = attend / running
    spread = jnp.einsum('thn,shn->hts', shares, control, precision=highest) * causal[None]
    mixed_rows = jnp.einsum('thn,hnd->thd', shares, state_values, precision=highest) + jnp.einsum('hts,shd->thd', spread, values_in, precision=highest)
    state_keys = state_keys + jnp.einsum('shn,shd->hnd', control, keys_in, precision=highest)
    state_values = state_values + jnp.einsum('shn,shd->hnd', control, values_in, precision=highest)
    slot_total = slot_total + lax.optimization_barrier(jnp.sum(control, axis=0))
    log_mass = lax.optimization_barrier(jnp.sum(jnp.log(running), axis=0))
    return ((state_keys, state_values, slot_total), (mixed_rows, log_mass))

def slot_attention(projected_rows):
    sequence_length = projected_rows.shape[0]
    grouped_by_head = projected_rows.reshape(sequence_length, -1, 3 * HEAD_SIZE + MEMORY_SLOTS)
    count_of_heads = grouped_by_head.shape[1]
    blocks = sequence_length // BLOCK

    def to_blocks(source):
        return source.reshape(blocks, BLOCK, count_of_heads, source.shape[-1])
    queries = grouped_by_head[:, :, :HEAD_SIZE]
    keys_in = grouped_by_head[:, :, HEAD_SIZE:2 * HEAD_SIZE]
    values_in = grouped_by_head[:, :, 2 * HEAD_SIZE:3 * HEAD_SIZE]
    control = jnp.exp(grouped_by_head[:, :, 3 * HEAD_SIZE:])
    initial_state = (jnp.zeros((count_of_heads, MEMORY_SLOTS, HEAD_SIZE), jnp.float32), jnp.zeros((count_of_heads, MEMORY_SLOTS, HEAD_SIZE), jnp.float32), jnp.zeros((count_of_heads, MEMORY_SLOTS), jnp.float32))
    _, (mixed_rows, log_mass) = lax.scan(jax.checkpoint(slot_block), initial_state, (to_blocks(queries), to_blocks(keys_in), to_blocks(values_in), to_blocks(control)))
    return (mixed_rows.reshape(sequence_length, count_of_heads * HEAD_SIZE), lax.optimization_barrier(jnp.sum(log_mass, axis=0)).reshape(-1))

def attention(hidden, gain, weight_in, weight_out):
    normed = low(rms_scale(hidden, gain))
    projected_rows = low_back(jnp.dot(normed, weight_in, precision=highest))
    grouped_by_head = projected_rows.reshape(-1, SPAN, projected_rows.shape[-1])
    mixed_rows, log_mass = lax.map(slot_attention, grouped_by_head)
    mixed_rows = low_back(low(mixed_rows.reshape(-1, mixed_rows.shape[-1])))
    return (jnp.dot(mixed_rows, weight_out, precision=highest), lax.optimization_barrier(jnp.sum(log_mass, axis=0)))

def feed_forward(hidden, gain, weight_in, weight_out):
    normed = low(rms_scale(hidden, gain))
    before = low_back(jnp.dot(normed, weight_in, precision=highest))
    activated = low(jax.nn.gelu(before))
    return jnp.dot(activated, weight_out, precision=highest)

def forward(tokens, attn_gain, attention_input_weight, attn_out, ffn_gain, ffn_in, ffn_out):
    hidden = low_back(tokens)
    slot_marks = []
    for layer_index in range(LAYERS):
        branch, log_mass = attention(hidden, attn_gain[layer_index], attention_input_weight[layer_index], attn_out[layer_index])
        hidden = low_back(low(hidden + branch))
        hidden = low_back(low(hidden + feed_forward(hidden, ffn_gain[layer_index], ffn_in[layer_index], ffn_out[layer_index])))
        slot_marks.append(log_mass)
    return (hidden, jnp.stack(slot_marks))

def reference(tokens, attn_gain, attention_input_weight, attn_out, ffn_gain, ffn_in, ffn_out, cotangent):
    output_rows, pullback, slot_marks = jax.vjp(forward, tokens.astype(jnp.float32), attn_gain.astype(jnp.float32), attention_input_weight.astype(jnp.float32), attn_out.astype(jnp.float32), ffn_gain.astype(jnp.float32), ffn_in.astype(jnp.float32), ffn_out.astype(jnp.float32), has_aux=True)
    gradients = pullback(cotangent.astype(jnp.float32))
    slot_mean = slot_marks / (tokens.shape[0] * 1.0)
    return (output_rows.astype(jnp.bfloat16), gradients[0].astype(jnp.bfloat16), gradients[2], gradients[3], gradients[1], gradients[5], gradients[6], gradients[4], slot_mean)
```

```python
import types

import jax
import jax.numpy as jnp
from jax import lax
from jax.experimental import pallas as pl
from jax.experimental.pallas import tpu as pltpu
from jax.sharding import PartitionSpec as P

HEAD_SIZE = 64
MEMORY_SLOTS = 64
SPAN = 1024
NORM_EPS = 1e-05
MESH = pl.DeviceIdType.MESH
F32 = jnp.float32
BF16 = jnp.bfloat16
HALF = SPAN // 2
BLK = 256
WI, WO, F1, F2 = KINDS = range(4)
TO_Y, TO_X, TO_C0, TO_C1 = range(4)
CO, YO, CW, XS, AX, AC, OWN, ZS = range(8)
POINTS = 11


def nn(a, b):
    return lax.dot_general(a, b, (((1,), (0,)), ((), ())), preferred_element_type=F32)


def nt(a, b):
    return lax.dot_general(a, b, (((1,), (1,)), ((), ())), preferred_element_type=F32)


def loop(n, body):
    def step(i, carry):
        body(i)
        return carry

    lax.fori_loop(0, n, step, 0)


def make_kernel(layers, dims, n_dp, dp_inside):
    width = dims[WI][0]
    heads = dims[WI][1] // (3 * HEAD_SIZE + MEMORY_SLOTS)
    nz = n_dp - 1 if dp_inside else 0
    shards = n_dp if dp_inside else 1
    tiles = 2 * dims[F2][0] // 512
    half_tiles = tiles // 2
    core_rows = [rows // 2 for rows, _ in dims]

    def kernel(*refs):
        tok, ag, fg, cot, *rest = refs
        hbm, (out, ig, *grad), small = rest[:4], rest[4:10], rest[10]
        r = types.SimpleNamespace(**jax.tree.unflatten(layout, rest[11:]))
        s = lax.axis_index("section")
        z = lax.axis_index("dp")
        y = lax.axis_index("tensor")
        c = lax.rem(s, 2)
        x = s // 2
        oc, ox, oy = 1 - c, 1 - x, 1 - y
        dev_core = (x * 2 + oc, z, y)
        dev_x = (ox * 2 + c, z, y)
        dev_y = (s, z, oy)

        def dev_z(k):
            return (s, lax.rem(z + k, n_dp), y)

        group = [
            (ds, dy, (lax.rem(s + ds, 4), z, lax.rem(y + dy, 2)))
            for ds in range(4)
            for dy in range(2)
            if ds or dy
        ]

        barrier = pltpu.get_barrier_semaphore()
        everyone = [d for _, _, d in group] + [dev_z(k) for k in range(1, nz + 1)]
        for d in everyone:
            pl.semaphore_signal(barrier, inc=1, device_id=d, device_id_type=MESH)

        row0 = pl.multiple_of((2 * x + y) * SPAN + c * HALF, HALF)

        def load(i, src, dst):
            return pltpu.make_async_copy(src, dst, r.ld_sem.at[i])

        tok_ld = load(0, tok.at[pl.ds(row0, HALF), :], r.h.at[0])
        cot_ld = load(1, cot.at[pl.ds(row0, HALF), :], r.g)
        w_ld = {}
        order = [(k, l) for l in range(layers) for k in KINDS]
        for i, (k, l) in enumerate(order):
            w_ld[i] = load(2 + i, hbm[k].at[l], r.v[k].at[l, y])

        tok_ld.start()
        w_ld[0].start()
        w_ld[1].start()

        def w_copy(i, stage):
            k, l = order[i]
            rows = dims[k][0] // 4
            mine = pl.ds(pl.multiple_of((2 * x + c) * rows, rows), rows)
            far = pl.ds(pl.multiple_of((2 * ox + c) * rows, rows), rows)
            v = r.v[k]
            src, dst, dev = {
                TO_Y: (hbm[k].at[l, mine, :], v.at[l, y, mine, :], dev_y),
                TO_X: (v.at[l, oy, mine, :], v.at[l, oy, mine, :], dev_x),
                TO_C0: (v.at[l, oy, mine, :], v.at[l, oy, mine, :], dev_core),
                TO_C1: (v.at[l, oy, far, :], v.at[l, oy, far, :], dev_core),
            }[stage]
            at = i * 4 + stage
            return pltpu.make_async_remote_copy(
                src_ref=src,
                dst_ref=dst,
                send_sem=r.w_send.at[at],
                recv_sem=r.w_recv.at[at],
                device_id=dev,
                device_id_type=MESH,
            )

        def wy(i):
            w_copy(i, TO_Y).start()

        def wx(i):
            w_copy(i, TO_Y).wait_recv()
            w_copy(i, TO_X).start()
            w_copy(i, TO_C0).start()

        def wc(i):
            w_copy(i, TO_X).wait_recv()
            w_copy(i, TO_C1).start()

        def wd(i):
            w_copy(i, TO_C0).wait_recv()
            w_copy(i, TO_C1).wait_recv()

        def w_end(i):
            for stage in range(4):
                w_copy(i, stage).wait_send()

        pl.semaphore_wait(barrier, len(everyone))
        wy(0)
        wy(1)
        for i in range(2, len(order)):
            w_ld[i].start()
        cot_ld.start()

        tri_s = lax.broadcasted_iota(jnp.int32, (BLK, BLK), 0)
        tri_t = lax.broadcasted_iota(jnp.int32, (BLK, BLK), 1)
        r.tri[...] = jnp.where(tri_s <= tri_t, 1.0, 0.0).astype(BF16)
        r.state_in[2 * layers] = jnp.zeros(r.state_in.shape[1:], BF16)

        def masked(v, on):
            if not on:
                return v.astype(BF16)
            keep = lax.broadcasted_iota(jnp.int32, (BLK, BLK), 0) <= lax.broadcasted_iota(
                jnp.int32, (BLK, BLK), 1
            )
            return jnp.where(keep, v, 0.0).astype(BF16)

        def blocks(tb):
            return [(b, b == tb) for b in range(tb + 1)]

        def state_copy(slot, buf):
            return pltpu.make_async_remote_copy(
                src_ref=r.state_out.at[buf],
                dst_ref=r.state_in.at[slot],
                send_sem=r.st_send.at[slot],
                recv_sem=r.st_recv.at[slot],
                device_id=dev_core,
                device_id_type=MESH,
            )

        def state_send(slot, buf, from_core):
            @pl.when(c == from_core)
            def _():
                state_copy(slot, buf).start()

        def state_recv(slot, buf, from_core):
            @pl.when(c != from_core)
            def _():
                state_copy(slot, buf).wait_recv()

        def state_sent(slot, buf, from_core):
            @pl.when(c == from_core)
            def _():
                state_copy(slot, buf).wait_send()

        def rms(sub, gain):
            h = r.h[sub].astype(F32)
            scale = lax.rsqrt(jnp.mean(h * h, axis=1, keepdims=True) + NORM_EPS)
            normed = (h * scale * gain).astype(BF16)
            r.nrm[...] = normed
            r.nT[sub] = normed.T

        def rms_back(sub, gain, dn, gain_row):
            h = r.h[sub].astype(F32)
            scale = lax.rsqrt(jnp.mean(h * h, axis=1, keepdims=True) + NORM_EPS)
            a = dn * gain
            hs = h * scale
            r.sm[0, pl.ds(gain_row, 1), :] = jnp.sum(dn * hs, axis=0, keepdims=True)
            dh = scale * (a - hs * jnp.mean(hs * a, axis=1, keepdims=True))
            r.g[...] = (r.g[...].astype(F32) + dh).astype(BF16)

        def project(l, half):
            def head(i):
                hd = half * heads + i
                cols = pl.ds(pl.multiple_of(i * 256, 256), 256)
                p = nn(r.nrm[...], r.v[WI][l, half, :, cols])
                lane = lax.broadcasted_iota(jnp.int32, (HALF, 128), 1)
                hi = p[:, 128:]
                hi = jnp.where(lane >= 64, jnp.exp(hi), hi)
                pb = jnp.concatenate([p[:, :128], hi], axis=1).astype(BF16)
                r.pj[l, hd] = pb
                pt = pb.T
                r.pjT[l, hd] = pt
                kv = pt[64:192]
                e = pt[192:256]
                buf = r.state_out.at[0]
                buf[i, 0:64, :] = nt(e, kv).astype(BF16)
                buf[i, 64:192, 0:64] = nt(kv, e).astype(BF16)
                buf[i, 192:256, :] = nn(e, jnp.ones((HALF, 128), BF16)).astype(BF16)

            loop(heads, head)

        def attend(l, half, slot):
            def head(i):
                hd = half * heads + i
                q = r.pjT[l, hd, 0:64, :]
                v = r.pjT[l, hd, 128:192, :]
                e = r.pjT[l, hd, 192:256, :]
                sk = r.state_in[slot, i, 0:64, 0:64]
                svt = r.state_in[slot, i, 128:192, 0:64]
                before = r.state_in[slot, i, 192:256, 0:1].astype(F32)
                zero = jnp.zeros((64, BLK), BF16)
                log_sum = jnp.zeros((64, 1), F32)
                for tb in range(2):
                    ts = slice(tb * BLK, (tb + 1) * BLK)
                    qt = q[:, ts]
                    rq = jnp.concatenate([zero, qt], axis=0)
                    num = nn(sk, qt)
                    for b, on in blocks(tb):
                        bs = slice(b * BLK, (b + 1) * BLK)
                        at = masked(nn(r.pj[l, hd, bs, 0:128], rq), on)
                        num = num + nn(e[:, bs], at)
                    zt = nn(e[:, ts], r.tri[...]) + before
                    before = zt[:, BLK - 1 : BLK]
                    rz = 1.0 / zt
                    sc = num * rz * 0.125
                    ex = jnp.exp(sc - jnp.max(sc, axis=0, keepdims=True))
                    p = ex * (1.0 / jnp.sum(ex, axis=0, keepdims=True))
                    w = (p * rz).astype(BF16)
                    r.rz[l, hd, :, ts] = rz
                    r.pr[l, hd, :, ts] = p.astype(BF16)
                    r.sc[l, hd, :, ts] = sc.astype(BF16)
                    log_sum = log_sum + jnp.sum(jnp.log(zt), axis=1, keepdims=True)
                    rw = jnp.concatenate([zero, w], axis=0)
                    o = nn(svt, w)
                    for b, on in blocks(tb):
                        bs = slice(b * BLK, (b + 1) * BLK)
                        gt = masked(nn(r.pj[l, hd, bs, 128:256], rw), on)
                        o = o + nn(v[:, bs], gt)
                    r.mixT[l, hd, :, ts] = o.astype(BF16)
                r.lm[l, hd] = jnp.broadcast_to(log_sum, (64, 128))

            loop(heads, head)

        def attn_out(l):
            mixed = r.mixT[l].reshape(2 * heads * 64, HALF).T
            wo = r.v[WO][l].reshape(2 * dims[WO][0], width)
            r.h[2 * l + 1] = (r.h[2 * l].astype(F32) + nn(mixed, wo)).astype(BF16)

        def tile_of(i, first):
            j = lax.rem(first * half_tiles + i, tiles)
            return j, j // half_tiles, pl.ds(pl.multiple_of(lax.rem(j, half_tiles) * 512, 512), 512)

        def ffn(l, lo, hi):
            k = 0.7978845608028654

            def tile(i):
                j, half, at = tile_of(i + lo, y)
                w1 = r.v[F1][l, half, :, at]
                w2 = r.v[F2][l, half, at, :]
                for tb in range(2):
                    ts = slice(tb * BLK, (tb + 1) * BLK)
                    b = nn(r.nrm[ts, :], w1)
                    bb = b * b
                    th = jnp.tanh(k * b * (1.0 + 0.044715 * bb))
                    hp = 0.5 * (1.0 + th)
                    act = (b * hp).astype(BF16)
                    slope = hp + (0.5 * k) * b * (1.0 - th * th) * (1.0 + 0.134145 * bb)
                    r.gp[l, j, ts, :] = slope.astype(BF16)
                    r.actT[l, j, :, ts] = act.T
                    r.acc[ts, :] = r.acc[ts, :] + nn(act, w2)

            loop(hi - lo, tile)

        def ffn_back(l, lo, hi):
            def tile(i):
                j, half, at = tile_of(i + lo, oy)
                w1 = r.v[F1][l, half, :, at]
                w2 = r.v[F2][l, half, at, :]
                for tb in range(2):
                    ts = slice(tb * BLK, (tb + 1) * BLK)
                    db = (nt(r.g[ts, :], w2) * r.gp[l, j, ts, :].astype(F32)).astype(BF16)
                    r.nrm[ts, :] = db
                    r.acc[ts, :] = r.acc[ts, :] + nt(db, w1)
                r.v[F2][l, half, at, :] = nn(r.actT[l, j], r.g[...]).astype(BF16)
                r.v[F1][l, half, :, at] = nn(r.nT[2 * l + 1], r.nrm[...]).astype(BF16)

            loop(hi - lo, tile)

        def mixed_back(l):
            wo = r.v[WO][l].reshape(2 * dims[WO][0], width)
            r.dmT[...] = nt(wo, r.g[...]).astype(BF16).reshape(r.dmT.shape)

        def attn_out_grad(l):
            mixed = r.mixT[l].reshape(2 * heads * 64, HALF)
            r.v[WO][l] = nn(mixed, r.g[...]).astype(BF16).reshape(r.v[WO].shape[1:])

        def attend_back(l, half, slot):
            def head(i):
                hd = half * heads + i
                q = r.pjT[l, hd, 0:64, :]
                kt = r.pjT[l, hd, 64:128, :]
                e = r.pjT[l, hd, 192:256, :]
                do = r.dmT[hd]
                skv = r.state_in[slot, i, 0:64, :]
                skt = r.state_in[slot, i, 64:128, 0:64]
                zero = jnp.zeros((64, BLK), BF16)
                none = jnp.zeros((64, BLK), F32)
                dv, dk, de = [none, none], [none, none], [none, none]
                dzs, dns, ws = [], [], []
                for tb in range(2):
                    ts = slice(tb * BLK, (tb + 1) * BLK)
                    dot, qt = do[:, ts], q[:, ts]
                    rd = jnp.concatenate([dot, zero], axis=0)
                    rz = r.rz[l, hd, :, ts]
                    p = r.pr[l, hd, :, ts].astype(F32)
                    sc = r.sc[l, hd, :, ts].astype(F32)
                    w = p * rz
                    wb = w.astype(BF16)
                    dw = nn(skv, jnp.concatenate([zero, dot], axis=0))
                    dgs = []
                    for b, on in blocks(tb):
                        bs = slice(b * BLK, (b + 1) * BLK)
                        dg = masked(nn(r.pj[l, hd, bs, 128:256], rd), on)
                        dw = dw + nn(e[:, bs], dg)
                        dgs.append(dg)
                    dp = dw * rz
                    ds = p * (dp - jnp.sum(p * dp, axis=0, keepdims=True))
                    dnb = (ds * rz * 0.125).astype(BF16)
                    dzs.append((-(dw * w + ds * sc) * rz).astype(BF16))
                    dns.append(dnb)
                    ws.append(wb)
                    rw = jnp.concatenate([zero, wb], axis=0)
                    rn = jnp.concatenate([zero, dnb], axis=0)
                    rq = jnp.concatenate([zero, qt], axis=0)
                    dq = nn(skt, dnb)
                    for b, on in blocks(tb):
                        bs = slice(b * BLK, (b + 1) * BLK)
                        qk = r.pj[l, hd, bs, 0:128]
                        ve = r.pj[l, hd, bs, 128:256]
                        at = masked(nn(qk, rq), on)
                        gt = masked(nn(ve, rw), on)
                        da = masked(nn(ve, rn), on)
                        dv[b] = dv[b] + nt(dot, gt)
                        de[b] = de[b] + nt(wb, dgs[b]) + nt(dnb, at)
                        dk[b] = dk[b] + nt(qt, da)
                        dq = dq + nn(kt[:, bs], da)
                    r.dpT[hd, 0:64, ts] = dq.astype(BF16)
                tri = r.tri[...]
                rev1 = nt(dzs[1], tri)
                rev0 = nt(dzs[0], tri) + rev1[:, 0:1]
                tmp = r.tmp.at[i]
                for b, rev in enumerate((rev0, rev1)):
                    bs = slice(b * BLK, (b + 1) * BLK)
                    tmp[0:64, bs] = dk[b]
                    tmp[64:128, bs] = dv[b]
                    tmp[128:192, bs] = de[b] + rev
                dn_all = jnp.concatenate(dns, axis=1)
                w_all = jnp.concatenate(ws, axis=1)
                buf = r.state_out.at[1]
                buf[i, 0:64, :] = jnp.concatenate([nt(dn_all, q), nt(w_all, do)], axis=1).astype(
                    BF16
                )
                buf[i, 64:128, 0:64] = nt(q, dn_all).astype(BF16)
                buf[i, 128:192, 0:64] = nt(do, w_all).astype(BF16)
                buf[i, 192:256, :] = jnp.broadcast_to(rev0[:, 0:1], (64, 128)).astype(BF16)

            loop(heads, head)

        def project_back(l, half, slot):
            def head(i):
                hd = half * heads + i
                kv = r.pjT[l, hd, 64:192, :]
                e = r.pjT[l, hd, 192:256, :]
                sin = r.state_in.at[slot]
                dkv = r.tmp[i, 0:128, :] + nn(sin[i, 64:192, 0:64], e)
                de = r.tmp[i, 128:192, :] + nn(sin[i, 0:64, :], kv)
                de = (de + sin[i, 192:256, 0:1].astype(F32)) * e.astype(F32)
                r.dpT[hd, 64:192, :] = dkv.astype(BF16)
                r.dpT[hd, 192:256, :] = de.astype(BF16)
                cols = pl.ds(pl.multiple_of(i * 256, 256), 256)
                dp = r.dpT[hd]
                r.acc[...] = r.acc[...] + nn(r.v[WI][l, half, :, cols], dp)
                r.v[WI][l, half, :, cols] = nt(r.nT[2 * l], dp).astype(BF16)

            loop(heads, head)

        def out_copies(src, dst, base):
            copies = []
            for ds, dy, dev in group:
                cols = pl.ds(pl.multiple_of(dev[0] * 128, 128), 128)
                copies.append(
                    pltpu.make_async_remote_copy(
                        src_ref=src.at[:, cols],
                        dst_ref=dst.at[pl.ds(row0, HALF), :],
                        send_sem=r.o_send.at[base + 2 * ds + dy],
                        recv_sem=r.o_recv.at[base + 2 * ds + dy],
                        device_id=dev,
                        device_id_type=MESH,
                    )
                )
            own = pltpu.make_async_copy(
                src.at[:, pl.ds(pl.multiple_of(s * 128, 128), 128)],
                dst.at[pl.ds(row0, HALF), :],
                r.o_send.at[base],
            )
            return copies, own

        def out_start(*which):
            copies, own = out_copies(*which)
            for copy in copies:
                copy.start()
            own.start()

        def out_wait(*which):
            copies, own = out_copies(*which)
            for copy in copies:
                copy.wait()
            own.wait()

        n_stage = ZS + 2 * nz

        def g_copy(k, l, stage):
            rows = core_rows[k]
            xr = rows // 2
            zr = xr // shards
            part = r.v[k].at[l]
            full = grad[k].at[l]
            at = (k * layers + l) * n_stage + stage
            sems = dict(send_sem=r.g_send.at[at], recv_sem=r.g_recv.at[at])

            def rng(start, size):
                return pl.ds(pl.multiple_of(start, size), size)

            own_rows = rng(c * rows + x * xr + z * zr, zr) if shards > 1 else rng(c * rows + x * xr, xr)
            if stage == OWN:
                return pltpu.make_async_copy(
                    r.fin[k].at[l], full.at[own_rows, :], r.g_send.at[at]
                )
            if stage == CO:
                src, dst, dev = part.at[oy, rng(oc * rows, rows), :], r.cr[k].at[0], dev_core
            elif stage == CW:
                src, dst, dev = part.at[y, rng(oc * rows, rows), :], r.cr[k].at[1], dev_core
            elif stage == YO:
                src, dst, dev = part.at[oy, rng(c * rows, rows), :], r.yr[k].at[l], dev_y
            elif stage == XS:
                src = part.at[y, rng(c * rows + ox * xr, xr), :]
                dst, dev = r.xr[k].at[l], dev_x
            elif stage == AX:
                span = rng(c * rows + x * xr, xr)
                src, dst, dev = full.at[span, :], full.at[span, :], dev_x
            elif stage == AC:
                span = rng(c * rows, rows)
                src, dst, dev = full.at[span, :], full.at[span, :], dev_core
            elif stage < ZS + nz:
                step = stage - ZS + 1
                dev = dev_z(step)
                src = part.at[y, rng(c * rows + x * xr + dev[1] * zr, zr), :]
                dst = r.zr[k].at[l, step - 1]
            else:
                step = stage - ZS - nz + 1
                dev = dev_z(step)
                src, dst = r.fin[k].at[l], full.at[own_rows, :]
            return pltpu.make_async_remote_copy(
                src_ref=src, dst_ref=dst, device_id=dev, device_id_type=MESH, **sems
            )

        def add_rows(k, total, dst, start, sources):
            cut = min(total, 32768 // dims[k][1])

            def rows_step(i):
                rows = pl.ds(pl.multiple_of(start + i * cut, 16), cut)
                value = dst[0][rows, :].astype(F32)
                here = pl.ds(pl.multiple_of(i * cut, 16), cut)
                for source in sources:
                    value = value + source[here, :].astype(F32)
                if dst[1] is None:
                    dst[0][rows, :] = value.astype(BF16)
                else:
                    dst[1][here, :] = value.astype(BF16)

            loop(total // cut, rows_step)

        def event(k, l, e):
            rows = core_rows[k]
            xr = rows // 2
            zr = xr // shards
            part = r.v[k].at[l]
            if e == 0:
                g_copy(k, l, CO).start()
            elif e == 1:
                g_copy(k, l, CO).wait_recv()
                add_rows(k, rows, (part.at[oy], None), c * rows, [r.cr[k].at[0]])
                g_copy(k, l, YO).start()
            elif e == 2:
                g_copy(k, l, CW).start()
            elif e == 3:
                g_copy(k, l, CW).wait_recv()
                g_copy(k, l, YO).wait_recv()
                add_rows(
                    k,
                    rows,
                    (part.at[y], None),
                    c * rows,
                    [r.cr[k].at[1], r.yr[k].at[l]],
                )
                g_copy(k, l, XS).start()
            elif e == 4:
                g_copy(k, l, XS).wait_recv()
                if nz:
                    add_rows(k, xr, (part.at[y], None), c * rows + x * xr, [r.xr[k].at[l]])
                    for step in range(1, nz + 1):
                        g_copy(k, l, ZS + step - 1).start()
            elif e == 5:
                sources = [r.zr[k].at[l, step - 1] for step in range(1, nz + 1)]
                for step in range(1, nz + 1):
                    g_copy(k, l, ZS + step - 1).wait_recv()
                start = c * rows + x * xr + (z * zr if nz else 0)
                if not nz:
                    sources = [r.xr[k].at[l]]
                add_rows(k, zr, (part.at[y], r.fin[k].at[l]), start, sources)
                for step in range(1, nz + 1):
                    g_copy(k, l, ZS + nz + step - 1).start()
                g_copy(k, l, OWN).start()
            elif e == 6:
                for step in range(1, nz + 1):
                    g_copy(k, l, ZS + nz + step - 1).wait_recv()
                g_copy(k, l, OWN).wait()
                g_copy(k, l, AX).start()
            elif e == 7:
                g_copy(k, l, AX).wait_recv()
                g_copy(k, l, AC).start()
            elif e == 8:
                g_copy(k, l, AC).wait_recv()
                for stage in range(n_stage):
                    if stage != OWN:
                        g_copy(k, l, stage).wait_send()

        def small_copy(step):
            dev = [dev_core, dev_y, dev_x][step] if step < 3 else dev_z(step - 2)
            return pltpu.make_async_remote_copy(
                src_ref=r.sm.at[min(step, 3)],
                dst_ref=r.smr.at[step],
                send_sem=r.s_send.at[step],
                recv_sem=r.s_recv.at[step],
                device_id=dev,
                device_id_type=MESH,
            )

        def small_sum(step):
            if step < 3:
                small_copy(step).wait_recv()
                r.sm[step + 1] = r.sm[step] + r.smr[step]
            else:
                total = r.sm[3]
                for k in range(nz):
                    small_copy(3 + k).wait_recv()
                    total = total + r.smr[3 + k]
                small[...] = total

        tok_ld.wait()
        for l in range(layers):
            w0 = l * 4
            if l == 0:
                r.sm[0] = jnp.zeros(r.sm.shape[1:], F32)
            rms(2 * l, ag[pl.ds(l, 1), :])
            for turn in range(2):
                half = y if turn == 0 else oy
                slot = 2 * l + turn
                use = jnp.where(c == 1, slot, 2 * layers)
                if turn == 0:
                    w_ld[w0].wait()
                else:
                    wc(w0)
                    wx(w0 + 1)
                    wy(w0 + 3)
                    wd(w0)
                if slot:
                    state_sent(slot - 1, 0, 0)
                project(l, half)
                state_send(slot, 0, 0)
                if turn == 0:
                    wx(w0)
                    wy(w0 + 2)
                else:
                    wc(w0 + 1)
                    wx(w0 + 2)
                state_recv(slot, 0, 0)
                attend(l, half, use)
            wd(w0 + 1)
            w_ld[w0 + 1].wait()
            attn_out(l)
            wc(w0 + 2)
            wx(w0 + 3)
            if l + 1 < layers:
                wy(w0 + 4)
                wy(w0 + 5)
            rms(2 * l + 1, fg[pl.ds(l, 1), :])
            w_ld[w0 + 2].wait()
            w_ld[w0 + 3].wait()
            r.acc[...] = r.h[2 * l + 1].astype(F32)
            ffn(l, 0, half_tiles)
            wc(w0 + 3)
            wd(w0 + 2)
            wd(w0 + 3)
            ffn(l, half_tiles, tiles)
            r.h[2 * l + 2] = r.acc[...].astype(BF16)
        out_start(r.h.at[2 * layers], out, 0)
        for i in range(len(order)):
            w_end(i)
        state_sent(2 * layers - 1, 0, 0)
        cot_ld.wait()
        for l in range(layers):
            lm = r.lm[l].reshape(2 * heads * 64, 128).T
            r.sm[0, pl.ds(2 * layers + l, 1), :] = lm[0:1, :]

        plan = {
            F1: (1, 2, 3, 5, 7, 8, 9, 10, 12),
            F2: (1, 2, 3, 5, 7, 8, 9, 10, 12),
            WO: (5, 6, 5, 7, 8, 9, 10, 11, 12),
            WI: (7, 8, 9, 10, 11, 12, 13, 14, 15),
        }
        events = {}
        for l in range(layers):
            for k in (F1, F2, WO, WI):
                for e, point in enumerate(plan[k]):
                    events.setdefault((layers - 1 - l) * POINTS + point, []).append((k, l, e))

        def at_point(l, point):
            for k, kl, e in events.pop((layers - 1 - l) * POINTS + point, []):
                event(k, kl, e)

        for l in reversed(range(layers)):
            r.acc[...] = jnp.zeros(r.acc.shape, F32)
            quarter = half_tiles // 2
            for part in range(4):
                ffn_back(l, part * quarter, (part + 1) * quarter)
                at_point(l, part)
            if l == layers - 1:
                out_wait(r.h.at[2 * layers], out, 0)
            rms_back(2 * l + 1, fg[pl.ds(l, 1), :], r.acc[...], 2 * l + 1)
            at_point(l, 4)
            mixed_back(l)
            attn_out_grad(l)
            at_point(l, 5)
            r.acc[...] = jnp.zeros(r.acc.shape, F32)
            for turn in range(2):
                half = oy if turn == 0 else y
                fwd_slot = jnp.where(c == 1, 2 * l + 1 - turn, 2 * layers)
                slot = 2 * l + turn
                use = jnp.where(c == 0, slot, 2 * layers)
                if not (turn == 0 and l == layers - 1):
                    prev = 2 * l if turn == 1 else 2 * (l + 1) + 1
                    state_sent(prev, 1, 1)
                attend_back(l, half, fwd_slot)
                state_send(slot, 1, 1)
                at_point(l, 6 if turn == 0 else 8)
                state_recv(slot, 1, 1)
                project_back(l, half, use)
                at_point(l, 7 if turn == 0 else 9)
            rms_back(2 * l, ag[pl.ds(l, 1), :], r.acc[...].T, 2 * l)
            if l == 0:
                out_start(r.g, ig, 8)
                small_copy(0).start()
            at_point(l, 10)
        state_sent(1, 1, 1)
        tail = [e for point in sorted(events) for e in events[point]]
        small_sum(0)
        small_copy(1).start()
        for i, (k, l, e) in enumerate(tail):
            event(k, l, e)
            if i == 0:
                small_sum(1)
                small_copy(2).start()
            if i == 1:
                small_sum(2)
                for k2 in range(nz):
                    small_copy(3 + k2).start()
            if i == 2:
                small_sum(3)
        for step in range(3 + nz):
            small_copy(step).wait_send()
        out_wait(r.g, ig, 8)

    L = layers
    nzb = max(nz, 1)
    n_sem = 4 * L * (7 + 2 * nz)
    scratch = dict(
        v=[pltpu.VMEM((L, 2, *dims[k]), BF16) for k in KINDS],
        h=pltpu.VMEM((2 * L + 1, HALF, width), BF16),
        nT=pltpu.VMEM((2 * L, width, HALF), BF16),
        nrm=pltpu.VMEM((HALF, width), BF16),
        g=pltpu.VMEM((HALF, width), BF16),
        pj=pltpu.VMEM((L, 2 * heads, HALF, 256), BF16),
        pjT=pltpu.VMEM((L, 2 * heads, 256, HALF), BF16),
        rz=pltpu.VMEM((L, 2 * heads, 64, HALF), F32),
        pr=pltpu.VMEM((L, 2 * heads, 64, HALF), BF16),
        sc=pltpu.VMEM((L, 2 * heads, 64, HALF), BF16),
        mixT=pltpu.VMEM((L, 2 * heads, 64, HALF), BF16),
        lm=pltpu.VMEM((L, 2 * heads, 64, 128), F32),
        gp=pltpu.VMEM((L, tiles, HALF, 512), BF16),
        actT=pltpu.VMEM((L, tiles, 512, HALF), BF16),
        acc=pltpu.VMEM((HALF, width), F32),
        dmT=pltpu.VMEM((2 * heads, 64, HALF), BF16),
        dpT=pltpu.VMEM((2 * heads, 256, HALF), BF16),
        tmp=pltpu.VMEM((heads, 192, HALF), F32),
        tri=pltpu.VMEM((BLK, BLK), BF16),
        state_out=pltpu.VMEM((2, heads, 256, 128), BF16),
        state_in=pltpu.VMEM((2 * L + 1, heads, 256, 128), BF16),
        sm=pltpu.VMEM((4, 8, width), F32),
        smr=pltpu.VMEM((3 + nzb, 8, width), F32),
        cr=[pltpu.VMEM((2, core_rows[k], dims[k][1]), BF16) for k in KINDS],
        yr=[pltpu.VMEM((L, core_rows[k], dims[k][1]), BF16) for k in KINDS],
        xr=[pltpu.VMEM((L, core_rows[k] // 2, dims[k][1]), BF16) for k in KINDS],
        zr=[pltpu.VMEM((L, nzb, core_rows[k] // 2 // shards, dims[k][1]), BF16) for k in KINDS],
        fin=[pltpu.VMEM((L, core_rows[k] // 2 // shards, dims[k][1]), BF16) for k in KINDS],
        ld_sem=pltpu.SemaphoreType.DMA((2 + 4 * L,)),
        w_send=pltpu.SemaphoreType.DMA((16 * L,)),
        w_recv=pltpu.SemaphoreType.DMA((16 * L,)),
        st_send=pltpu.SemaphoreType.DMA((2 * L,)),
        st_recv=pltpu.SemaphoreType.DMA((2 * L,)),
        o_send=pltpu.SemaphoreType.DMA((16,)),
        o_recv=pltpu.SemaphoreType.DMA((16,)),
        g_send=pltpu.SemaphoreType.DMA((n_sem,)),
        g_recv=pltpu.SemaphoreType.DMA((n_sem,)),
        s_send=pltpu.SemaphoreType.DMA((3 + nzb,)),
        s_recv=pltpu.SemaphoreType.DMA((3 + nzb,)),
    )
    flat, layout = jax.tree.flatten(scratch)
    return kernel, flat


def solution(mesh):
    n_dp = mesh.shape["dp"]
    dp_inside = n_dp in (2, 4)

    def local(tokens, attn_gain, w_in, w_out, ffn_gain, ffn_in, ffn_out, cotangent):
        layers, width = attn_gain.shape
        arrays = (w_in, w_out, ffn_in, ffn_out)
        dims = [v.shape[1:] for v in arrays]
        kernel, scratch = make_kernel(layers, dims, n_dp, dp_inside)
        anyspace = pl.BlockSpec(memory_space=pl.ANY)
        vmem = pl.BlockSpec(memory_space=pltpu.VMEM)
        edge = jax.ShapeDtypeStruct((tokens.shape[0], width // 4), BF16)
        results = pl.pallas_call(
            kernel,
            out_shape=[edge, edge]
            + [jax.ShapeDtypeStruct(v.shape, BF16) for v in arrays]
            + [jax.ShapeDtypeStruct((8, width), F32)],
            in_specs=[anyspace, vmem, vmem] + [anyspace] * 5,
            out_specs=[anyspace] * 6 + [vmem],
            scratch_shapes=scratch,
            compiler_params=pltpu.CompilerParams(
                collective_id=0, has_side_effects=True, vmem_limit_bytes=63 * 1024 * 1024
            ),
        )(tokens, attn_gain, ffn_gain, cotangent, *arrays)
        out, ig, *grads, small = results
        if not dp_inside and n_dp > 1:
            grads = [lax.psum(v, "dp") for v in grads]
            small = lax.psum(small, "dp")
        grads = [v.astype(F32) for v in grads]
        own = w_in.shape[2] // (3 * HEAD_SIZE + MEMORY_SLOTS) * MEMORY_SLOTS
        mass = lax.dynamic_slice_in_dim(
            small[2 * layers : 3 * layers], lax.axis_index("tensor") * own, own, 1
        )
        count = tokens.shape[0] * n_dp * 1.0
        return (
            out,
            ig,
            grads[0],
            grads[1],
            small[0 : 2 * layers : 2],
            grads[2],
            grads[3],
            small[1 : 2 * layers : 2],
            mass / count,
        )

    placed = (
        P("dp", None),
        P(),
        P(None, None, "tensor"),
        P(None, "tensor", None),
        P(),
        P(None, None, "tensor"),
        P(None, "tensor", None),
        P("dp", None),
    )
    return jax.shard_map(
        local,
        mesh=mesh,
        in_specs=placed,
        out_specs=(
            P("dp", "section"),
            P("dp", "section"),
            P(None, None, "tensor"),
            P(None, "tensor", None),
            P(),
            P(None, None, "tensor"),
            P(None, "tensor", None),
            P(),
            P(None, "tensor"),
        ),
        check_vma=False,
    )
```

```python
import types

import jax
import jax.numpy as jnp
from jax import lax
from jax.experimental import pallas as pl
from jax.experimental.pallas import tpu as pltpu
from jax.sharding import PartitionSpec as P

HEAD_SIZE = 64
MEMORY_SLOTS = 64
SPAN = 1024
NORM_EPS = 1e-05
MESH = pl.DeviceIdType.MESH
F32 = jnp.float32
BF16 = jnp.bfloat16
HALF = SPAN // 2
BLK = 256
WI, WO, F1, F2 = KINDS = range(4)
TO_Y, TO_X, TO_C0, TO_C1 = range(4)
CO, YO, CW, XS, AX, AC, OWN, ZS = range(8)
ITEMS = ((WI, 0), (WI, 1), (WO, 0), (F1, 0), (F2, 0), (F1, 1), (F2, 1))
TILES = ((F2, 0), (F1, 0), (F2, 1), (F1, 1), (WO, 0), (WI, 0), (WI, 1))
FORWARD = (
    (0, 4, 8),
    (),
    (),
    (1, 12, 5, 16, 9, 20, 2, 13, 24, 3, 6, 17, 28, 10, 7),
    (21, 32),
    (14, 25, 36, 18, 11),
    (),
    (22, 29, 40, 33, 44, 15, 19),
    (26, 37, 48, 23, 27),
    (),
    (),
    (30, 41, 52),
    (34, 38, 45, 49, 31, 42, 35),
    (53,),
    (46, 39),
    (50,),
    (54, 43, 47),
    (51, 55),
    (),
)
BACKWARD = (
    (0, 8),
    (16, 24),
    (1, 9, 2, 10),
    (17, 25, 18, 26),
    (),
    (32, 34),
    (33,),
    (40, 48),
    (41, 49, 3),
    (42, 50, 11),
    (),
    (56, 64, 4),
    (72, 80),
    (57, 65, 58, 66, 19, 73, 12, 81),
    (5,),
    (27,),
    (88, 20),
    (89, 74, 82, 35, 28, 13, 6),
    (96, 104, 43, 21, 36),
    (97, 105, 90, 51, 44, 29, 14, 7),
    (59, 37, 22),
    (),
    (52, 45, 67, 15, 30, 38),
    (60, 53, 75, 23, 46, 68),
    (61, 83, 31, 39, 54, 91),
    (98, 76, 69, 47, 62, 99),
    (106, 84, 77, 55, 70, 107, 92, 85, 63, 78, 100, 93, 86, 101, 94, 102, 71, 108, 79, 109, 87, 95, 103, 110, 111),
)
WIDE = 4


def nn(a, b):
    return lax.dot_general(a, b, (((1,), (0,)), ((), ())), preferred_element_type=F32)


def nt(a, b):
    return lax.dot_general(a, b, (((1,), (1,)), ((), ())), preferred_element_type=F32)


def loop(n, body):
    def step(i, carry):
        body(i)
        return carry

    lax.fori_loop(0, n, step, 0)


def together(n, width, body):
    def step(i):
        running = [body(width * i + j) for j in range(width)]
        for _ in zip(*running, strict=True):
            pass

    loop(n // width, step)


def make_kernel(layers, dims, n_dp, dp_inside, count):
    width = dims[WI][0]
    heads = dims[WI][1] // (3 * HEAD_SIZE + MEMORY_SLOTS)
    nz = n_dp - 1 if dp_inside else 0
    shards = n_dp if dp_inside else 1
    tiles = 2 * dims[F2][0] // 512
    half_tiles = tiles // 2
    items = [(k, l, t) for l in range(layers) for k, t in ITEMS]
    pieces = [(k, l, t) for l in reversed(range(layers)) for k, t in TILES]

    def tile_size(k):
        return min(dims[k][0], 512)


    def kernel(*refs):
        tok, ag, fg, cot, *rest = refs
        hbm, (out, ig, *grad), small = rest[:4], rest[4:10], rest[10]
        r = types.SimpleNamespace(**jax.tree.unflatten(layout, rest[11:]))
        s = lax.axis_index("section")
        z = lax.axis_index("dp")
        y = lax.axis_index("tensor")
        c = lax.rem(s, 2)
        x = s // 2
        oc, ox, oy = 1 - c, 1 - x, 1 - y
        dev_core = (x * 2 + oc, z, y)
        dev_x = (ox * 2 + c, z, y)
        dev_y = (s, z, oy)

        def dev_z(k):
            return (s, lax.rem(z + k, n_dp), y)

        group = [
            (ds, dy, (lax.rem(s + ds, 4), z, lax.rem(y + dy, 2)))
            for ds in range(4)
            for dy in range(2)
            if ds or dy
        ]

        barrier = pltpu.get_barrier_semaphore()
        everyone = [d for _, _, d in group] + [dev_z(k) for k in range(1, nz + 1)]
        for d in everyone:
            pl.semaphore_signal(barrier, inc=1, device_id=d, device_id_type=MESH)

        row0 = pl.multiple_of((2 * x + y) * SPAN + c * HALF, HALF)

        def load(i, src, dst):
            return pltpu.make_async_copy(src, dst, r.ld_sem.at[i])

        tok_ld = load(0, tok.at[pl.ds(row0, HALF), :], r.h.at[0])
        cot_ld = load(1, cot.at[pl.ds(row0, HALF), :], r.g)
        w_ld = {}
        for l in range(layers):
            for k in KINDS:
                at = 2 + l * 4 + k
                w_ld[k, l] = load(at, hbm[k].at[l], r.v[k].at[l, y])

        tok_ld.start()
        w_ld[WI, 0].start()

        def tile_rows(k, t, start, size):
            first = t * 512 if k == F2 else 0
            return pl.ds(pl.multiple_of(first + start, 16), size)

        def tile_cols(k, t):
            return pl.ds(t * 512 if k in (WI, F1) else 0, 512)

        def w_copy(i, stage):
            k, l, t = items[i]
            rows, cols = tile_size(k) // 4, tile_cols(k, t)
            mine = tile_rows(k, t, (2 * x + c) * rows, rows)
            far = tile_rows(k, t, (2 * ox + c) * rows, rows)
            v = r.v[k]
            src, dst, dev = (
                (hbm[k].at[l, mine, cols], v.at[l, y, mine, cols], dev_y),
                (v.at[l, oy, mine, cols], v.at[l, oy, mine, cols], dev_x),
                (v.at[l, oy, mine, cols], v.at[l, oy, mine, cols], dev_core),
                (v.at[l, oy, far, cols], v.at[l, oy, far, cols], dev_core),
            )[stage]
            return pltpu.make_async_remote_copy(
                src_ref=src,
                dst_ref=dst,
                send_sem=r.w_send.at[i * 4 + stage],
                recv_sem=r.w_recv.at[i * 4 + stage],
                device_id=dev,
                device_id_type=MESH,
            )

        def w_event(i, e):
            if e == 0:
                w_copy(i, TO_Y).start()
            elif e == 1:
                w_copy(i, TO_Y).wait_recv()
                w_copy(i, TO_X).start()
                w_copy(i, TO_C0).start()
            elif e == 2:
                w_copy(i, TO_X).wait_recv()
                w_copy(i, TO_C1).start()
            else:
                w_copy(i, TO_C0).wait_recv()
                w_copy(i, TO_C1).wait_recv()

        def w_end():
            for i in range(len(items)):
                for stage in range(4):
                    w_copy(i, stage).wait_send()

        forward_plan = iter(FORWARD)

        def weights_here():
            for code in next(forward_plan):
                w_event(code // 4, code % 4)

        pl.semaphore_wait(barrier, len(everyone))
        weights_here()
        for l in range(layers):
            for k in KINDS:
                if (k, l) != (WI, 0):
                    w_ld[k, l].start()
        cot_ld.start()

        tri_s = lax.broadcasted_iota(jnp.int32, (BLK, BLK), 0)
        tri_t = lax.broadcasted_iota(jnp.int32, (BLK, BLK), 1)
        r.tri[...] = jnp.where(tri_s <= tri_t, 1.0, 0.0).astype(BF16)
        r.state_in[2 * layers] = jnp.zeros(r.state_in.shape[1:], BF16)

        def masked(v, on):
            if not on:
                return v.astype(BF16)
            keep = lax.broadcasted_iota(jnp.int32, (BLK, BLK), 0) <= lax.broadcasted_iota(
                jnp.int32, (BLK, BLK), 1
            )
            return jnp.where(keep, v, 0.0).astype(BF16)

        def blocks(tb):
            return [(b, b == tb) for b in range(tb + 1)]

        def state_copy(slot, buf):
            return pltpu.make_async_remote_copy(
                src_ref=r.state_out.at[buf],
                dst_ref=r.state_in.at[slot],
                send_sem=r.st_send.at[slot],
                recv_sem=r.st_recv.at[slot],
                device_id=dev_core,
                device_id_type=MESH,
            )

        def state_send(slot, buf, from_core):
            @pl.when(c == from_core)
            def _():
                state_copy(slot, buf).start()

        def state_recv(slot, buf, from_core):
            @pl.when(c != from_core)
            def _():
                state_copy(slot, buf).wait_recv()

        def state_sent(slot, buf, from_core):
            @pl.when(c == from_core)
            def _():
                state_copy(slot, buf).wait_send()

        def rms(sub, gain):
            h = r.h[sub].astype(F32)
            scale = lax.rsqrt(jnp.mean(h * h, axis=1, keepdims=True) + NORM_EPS)
            return (h * scale * gain).astype(BF16)

        def rms_back(sub, gain, dn, gain_row):
            h = r.h[sub].astype(F32)
            scale = lax.rsqrt(jnp.mean(h * h, axis=1, keepdims=True) + NORM_EPS)
            a = dn * gain
            hs = h * scale
            r.sm[0, pl.ds(gain_row, 1), :] = jnp.sum(dn * hs, axis=0, keepdims=True)
            dh = scale * (a - hs * jnp.mean(hs * a, axis=1, keepdims=True))
            r.g[...] = (r.g[...].astype(F32) + dh).astype(BF16)

        def project(l, half):
            def head(i):
                hd = half * heads + i
                cols = pl.ds(pl.multiple_of(i * 256, 256), 256)
                p = nn(r.nrm[...], r.v[WI][l, half, :, cols])
                yield
                lane = lax.broadcasted_iota(jnp.int32, (HALF, 128), 1)
                hi = p[:, 128:]
                hi = jnp.where(lane >= 64, jnp.exp(hi), hi)
                pb = jnp.concatenate([p[:, :128], hi], axis=1).astype(BF16)
                r.pj[l, hd] = pb
                pt = pb.T
                r.pjT[l, hd] = pt
                yield
                kv = pt[64:192]
                e = pt[192:256]
                buf = r.state_out.at[0]
                buf[i, 0:64, :] = nt(e, kv).astype(BF16)
                buf[i, 64:192, 0:64] = nt(kv, e).astype(BF16)
                buf[i, 192:256, :] = nn(e, jnp.ones((HALF, 128), BF16)).astype(BF16)
                yield

            together(heads, WIDE, head)

        def attend(l, half, slot):
            def head(i):
                hd = half * heads + i
                q = r.pjT[l, hd, 0:64, :]
                v = r.pjT[l, hd, 128:192, :]
                e = r.pjT[l, hd, 192:256, :]
                sk = r.state_in[slot, i, 0:64, 0:64]
                svt = r.state_in[slot, i, 128:192, 0:64]
                before = r.state_in[slot, i, 192:256, 0:1].astype(F32)
                zero = jnp.zeros((64, BLK), BF16)
                log_sum = jnp.zeros((64, 1), F32)
                for tb in range(2):
                    ts = slice(tb * BLK, (tb + 1) * BLK)
                    qt = q[:, ts]
                    rq = jnp.concatenate([zero, qt], axis=0)
                    num = nn(sk, qt)
                    yield
                    for b, on in blocks(tb):
                        bs = slice(b * BLK, (b + 1) * BLK)
                        at = masked(nn(r.pj[l, hd, bs, 0:128], rq), on)
                        yield
                        num = num + nn(e[:, bs], at)
                        yield
                    zt = nn(e[:, ts], r.tri[...]) + before
                    before = zt[:, BLK - 1 : BLK]
                    rz = 1.0 / zt
                    sc = num * rz * 0.125
                    yield
                    ex = jnp.exp(sc - jnp.max(sc, axis=0, keepdims=True))
                    p = ex * (1.0 / jnp.sum(ex, axis=0, keepdims=True))
                    w = (p * rz).astype(BF16)
                    r.rz[l, hd, :, ts] = rz
                    r.pr[l, hd, :, ts] = p.astype(BF16)
                    r.sc[l, hd, :, ts] = sc.astype(BF16)
                    log_sum = log_sum + jnp.sum(jnp.log(zt), axis=1, keepdims=True)
                    rw = jnp.concatenate([zero, w], axis=0)
                    yield
                    o = nn(svt, w)
                    for b, on in blocks(tb):
                        bs = slice(b * BLK, (b + 1) * BLK)
                        gt = masked(nn(r.pj[l, hd, bs, 128:256], rw), on)
                        yield
                        o = o + nn(v[:, bs], gt)
                        yield
                    r.mixT[l, hd, :, ts] = o.astype(BF16)
                r.lm[l, hd] = jnp.broadcast_to(log_sum, (64, 128))
                yield

            together(heads, WIDE, head)

        def attn_out(l):
            mixed = r.mixT[l].reshape(2 * heads * 64, HALF).T
            wo = r.v[WO][l].reshape(2 * dims[WO][0], width)
            r.h[2 * l + 1] = (r.h[2 * l].astype(F32) + nn(mixed, wo)).astype(BF16)

        def tile_of(i, first):
            j = lax.rem(first * half_tiles + i, tiles)
            return j, j // half_tiles, pl.ds(pl.multiple_of(lax.rem(j, half_tiles) * 512, 512), 512)

        def ffn(l, lo, hi):
            k = 0.7978845608028654

            def tile(i):
                j, half, at = tile_of(i + lo, y)
                w1 = r.v[F1][l, half, :, at]
                w2 = r.v[F2][l, half, at, :]
                for tb in range(2):
                    ts = slice(tb * BLK, (tb + 1) * BLK)
                    b = nn(r.nrm[ts, :], w1)
                    bb = b * b
                    th = jnp.tanh(k * b * (1.0 + 0.044715 * bb))
                    hp = 0.5 * (1.0 + th)
                    act = (b * hp).astype(BF16)
                    slope = hp + (0.5 * k) * b * (1.0 - th * th) * (1.0 + 0.134145 * bb)
                    r.gp[l, j, ts, :] = slope.astype(BF16)
                    r.actT[l, j, :, ts] = act.T
                    r.acc[ts, :] = r.acc[ts, :] + nn(act, w2)

            loop(hi - lo, tile)

        def ffn_back(l, lo, hi):
            def tile(i):
                j, half, at = tile_of(i + lo, oy)
                w1 = r.v[F1][l, half, :, at]
                w2 = r.v[F2][l, half, at, :]
                for tb in range(2):
                    ts = slice(tb * BLK, (tb + 1) * BLK)
                    db = (nt(r.g[ts, :], w2) * r.gp[l, j, ts, :].astype(F32)).astype(BF16)
                    r.nrm[ts, :] = db
                    r.acc[ts, :] = r.acc[ts, :] + nt(db, w1)
                r.v[F2][l, half, at, :] = nn(r.actT[l, j], r.g[...]).astype(BF16)
                r.v[F1][l, half, :, at] = nn(r.nT[...], r.nrm[...]).astype(BF16)

            loop(hi - lo, tile)

        def mixed_back(l):
            wo = r.v[WO][l].reshape(2 * dims[WO][0], width)
            r.nrm[...] = nt(wo, r.g[...]).astype(BF16)

        def attn_out_grad(l):
            mixed = r.mixT[l].reshape(2 * heads * 64, HALF)
            r.v[WO][l] = nn(mixed, r.g[...]).astype(BF16).reshape(r.v[WO].shape[1:])

        def attend_back(l, half, slot):
            def head(i):
                hd = half * heads + i
                q = r.pjT[l, hd, 0:64, :]
                kt = r.pjT[l, hd, 64:128, :]
                e = r.pjT[l, hd, 192:256, :]
                do = r.nrm[pl.ds(pl.multiple_of(hd * 64, 64), 64), :]
                skv = r.state_in[slot, i, 0:64, :]
                skt = r.state_in[slot, i, 64:128, 0:64]
                zero = jnp.zeros((64, BLK), BF16)
                none = jnp.zeros((64, BLK), F32)
                dv, dk, de = [none, none], [none, none], [none, none]
                dzs, dns, ws, dqs = [], [], [], []
                for tb in range(2):
                    ts = slice(tb * BLK, (tb + 1) * BLK)
                    dot, qt = do[:, ts], q[:, ts]
                    rd = jnp.concatenate([dot, zero], axis=0)
                    rz = r.rz[l, hd, :, ts]
                    p = r.pr[l, hd, :, ts].astype(F32)
                    sc = r.sc[l, hd, :, ts].astype(F32)
                    w = p * rz
                    wb = w.astype(BF16)
                    dw = nn(skv, jnp.concatenate([zero, dot], axis=0))
                    dgs = []
                    for b, on in blocks(tb):
                        bs = slice(b * BLK, (b + 1) * BLK)
                        dg = masked(nn(r.pj[l, hd, bs, 128:256], rd), on)
                        yield
                        dw = dw + nn(e[:, bs], dg)
                        dgs.append(dg)
                        yield
                    dp = dw * rz
                    ds = p * (dp - jnp.sum(p * dp, axis=0, keepdims=True))
                    dnb = (ds * rz * 0.125).astype(BF16)
                    dzs.append((-(dw * w + ds * sc) * rz).astype(BF16))
                    dns.append(dnb)
                    ws.append(wb)
                    rw = jnp.concatenate([zero, wb], axis=0)
                    rn = jnp.concatenate([zero, dnb], axis=0)
                    rq = jnp.concatenate([zero, qt], axis=0)
                    yield
                    dq = nn(skt, dnb)
                    for b, on in blocks(tb):
                        bs = slice(b * BLK, (b + 1) * BLK)
                        qk = r.pj[l, hd, bs, 0:128]
                        ve = r.pj[l, hd, bs, 128:256]
                        at = masked(nn(qk, rq), on)
                        yield
                        gt = masked(nn(ve, rw), on)
                        yield
                        da = masked(nn(ve, rn), on)
                        yield
                        dv[b] = dv[b] + nt(dot, gt)
                        de[b] = de[b] + nt(wb, dgs[b]) + nt(dnb, at)
                        dk[b] = dk[b] + nt(qt, da)
                        dq = dq + nn(kt[:, bs], da)
                        yield
                    dqs.append(dq.astype(BF16))
                tri = r.tri[...]
                rev1 = nt(dzs[1], tri)
                rev0 = nt(dzs[0], tri) + rev1[:, 0:1]
                tmp = r.tmp.at[i]
                for b, rev in enumerate((rev0, rev1)):
                    bs = slice(b * BLK, (b + 1) * BLK)
                    tmp[0:64, bs] = dk[b]
                    tmp[64:128, bs] = dv[b]
                    tmp[128:192, bs] = de[b] + rev
                dn_all = jnp.concatenate(dns, axis=1)
                w_all = jnp.concatenate(ws, axis=1)
                buf = r.state_out.at[1]
                buf[i, 0:64, :] = jnp.concatenate([nt(dn_all, q), nt(w_all, do)], axis=1).astype(
                    BF16
                )
                buf[i, 64:128, 0:64] = nt(q, dn_all).astype(BF16)
                buf[i, 128:192, 0:64] = nt(do, w_all).astype(BF16)
                r.pjT[l, hd, 0:64, :] = jnp.concatenate(dqs, axis=1)
                buf[i, 192:256, :] = jnp.broadcast_to(rev0[:, 0:1], (64, 128)).astype(BF16)
                yield

            together(heads, WIDE, head)

        def project_back(l, half, slot):
            def head(i):
                hd = half * heads + i
                kv = r.pjT[l, hd, 64:192, :]
                e = r.pjT[l, hd, 192:256, :]
                sin = r.state_in.at[slot]
                dkv = r.tmp[i, 0:128, :] + nn(sin[i, 64:192, 0:64], e)
                de = r.tmp[i, 128:192, :] + nn(sin[i, 0:64, :], kv)
                de = (de + sin[i, 192:256, 0:1].astype(F32)) * e.astype(F32)
                r.pjT[l, hd, 64:192, :] = dkv.astype(BF16)
                r.pjT[l, hd, 192:256, :] = de.astype(BF16)
                cols = pl.ds(pl.multiple_of(i * 256, 256), 256)
                dp = r.pjT[l, hd]
                r.acc[...] = r.acc[...] + nn(r.v[WI][l, half, :, cols], dp)
                r.v[WI][l, half, :, cols] = nt(r.nT[...], dp).astype(BF16)

            loop(heads, head)

        def out_copies(src, dst, base):
            copies = []
            for ds, dy, dev in group:
                cols = pl.ds(pl.multiple_of(dev[0] * 128, 128), 128)
                copies.append(
                    pltpu.make_async_remote_copy(
                        src_ref=src.at[:, cols],
                        dst_ref=dst.at[pl.ds(row0, HALF), :],
                        send_sem=r.o_send.at[base + 2 * ds + dy],
                        recv_sem=r.o_recv.at[base + 2 * ds + dy],
                        device_id=dev,
                        device_id_type=MESH,
                    )
                )
            own = pltpu.make_async_copy(
                src.at[:, pl.ds(pl.multiple_of(s * 128, 128), 128)],
                dst.at[pl.ds(row0, HALF), :],
                r.o_send.at[base],
            )
            return copies, own

        def out_start(*which):
            copies, own = out_copies(*which)
            for copy in copies:
                copy.start()
            own.start()

        def out_wait(*which):
            copies, own = out_copies(*which)
            for copy in copies:
                copy.wait()
            own.wait()

        n_stage = ZS + 2 * nz

        def g_copy(p, stage):
            k, l, t = pieces[p]
            rows, cols = tile_size(k) // 2, tile_cols(k, t)
            xr = rows // 2
            zr = xr // shards
            part, full = r.v[k].at[l], grad[k].at[l]
            at = p * n_stage + stage
            sems = dict(send_sem=r.g_send.at[at], recv_sem=r.g_recv.at[at])

            def rng(start, size):
                return tile_rows(k, t, start, size)

            shard = rng(c * rows + x * xr + (z * zr if nz else 0), zr)
            head = pl.ds(0, rows)
            if stage == OWN:
                return pltpu.make_async_copy(
                    r.fin.at[p, pl.ds(0, zr)], full.at[shard, cols], r.g_send.at[at]
                )
            if stage == CO:
                src, dev = part.at[oy, rng(oc * rows, rows), cols], dev_core
                dst = r.cr.at[p % len(TILES), 0, head]
            elif stage == CW:
                src, dev = part.at[y, rng(oc * rows, rows), cols], dev_core
                dst = r.cr.at[p % len(TILES), 1, head]
            elif stage == YO:
                src, dst, dev = part.at[oy, rng(c * rows, rows), cols], r.yr.at[p, head], dev_y
            elif stage == XS:
                src = part.at[y, rng(c * rows + ox * xr, xr), cols]
                dst, dev = r.xr.at[p, pl.ds(0, xr)], dev_x
            elif stage == AX:
                span = rng(c * rows + x * xr, xr)
                src, dst, dev = full.at[span, cols], full.at[span, cols], dev_x
            elif stage == AC:
                span = rng(c * rows, rows)
                src, dst, dev = full.at[span, cols], full.at[span, cols], dev_core
            elif stage < ZS + nz:
                step = stage - ZS + 1
                dev = dev_z(step)
                src = part.at[y, rng(c * rows + x * xr + dev[1] * zr, zr), cols]
                dst = r.zr.at[p, step - 1, pl.ds(0, zr)]
            else:
                dev = dev_z(stage - ZS - nz + 1)
                src, dst = r.fin.at[p, pl.ds(0, zr)], full.at[shard, cols]
            return pltpu.make_async_remote_copy(
                src_ref=src, dst_ref=dst, device_id=dev, device_id_type=MESH, **sems
            )

        def add_rows(p, total, half, start, sources, target=None):
            k, l, t = pieces[p]
            cols = tile_cols(k, t)
            cut = min(total, 64)

            def rows_step(i):
                rows = tile_rows(k, t, start + i * cut, cut)
                here = pl.ds(pl.multiple_of(i * cut, 16), cut)
                value = r.v[k][l, half, rows, cols].astype(F32)
                for source in sources:
                    value = value + source[here, :].astype(F32)
                if target is None:
                    r.v[k][l, half, rows, cols] = value.astype(BF16)
                else:
                    target[here, :] = value.astype(BF16)

            loop(total // cut, rows_step)

        def g_event(p, e):
            rows = tile_size(pieces[p][0]) // 2
            xr = rows // 2
            zr = xr // shards
            if e == 0:
                g_copy(p, CO).start()
            elif e == 1:
                g_copy(p, CO).wait_recv()
                add_rows(p, rows, oy, c * rows, [r.cr.at[p % len(TILES), 0]])
                g_copy(p, YO).start()
            elif e == 2:
                g_copy(p, CW).start()
            elif e == 3:
                g_copy(p, CW).wait_recv()
                g_copy(p, YO).wait_recv()
                add_rows(p, rows, y, c * rows, [r.cr.at[p % len(TILES), 1], r.yr.at[p]])
                g_copy(p, XS).start()
            elif e == 4:
                g_copy(p, XS).wait_recv()
                if nz:
                    add_rows(p, xr, y, c * rows + x * xr, [r.xr.at[p]])
                    for step in range(nz):
                        g_copy(p, ZS + step).start()
            elif e == 5:
                sources = [r.zr.at[p, step] for step in range(nz)] if nz else [r.xr.at[p]]
                for step in range(nz):
                    g_copy(p, ZS + step).wait_recv()
                start = c * rows + x * xr + (z * zr if nz else 0)
                add_rows(p, zr, y, start, sources, r.fin.at[p])
                for step in range(nz):
                    g_copy(p, ZS + nz + step).start()
                g_copy(p, OWN).start()
            elif e == 6:
                for step in range(nz):
                    g_copy(p, ZS + nz + step).wait_recv()
                g_copy(p, OWN).wait()
                g_copy(p, AX).start()
            elif e == 7:
                g_copy(p, AX).wait_recv()
                g_copy(p, AC).start()

        backward_plan = iter(BACKWARD)

        def gradients_here():
            for code in next(backward_plan):
                g_event(code // 8, code % 8)

        def g_end():
            for p in range(len(pieces)):
                g_copy(p, AC).wait_recv()
                for stage in range(n_stage):
                    if stage != OWN:
                        g_copy(p, stage).wait_send()

        def small_copy(step):
            dev = [dev_core, dev_y, dev_x][step] if step < 3 else dev_z(step - 2)
            return pltpu.make_async_remote_copy(
                src_ref=r.sm.at[min(step, 3)],
                dst_ref=r.smr.at[step],
                send_sem=r.s_send.at[step],
                recv_sem=r.s_recv.at[step],
                device_id=dev,
                device_id_type=MESH,
            )

        def small_sum(step):
            if step < 3:
                small_copy(step).wait_recv()
                r.sm[step + 1] = r.sm[step] + r.smr[step]
            else:
                total = r.sm[3]
                for k in range(nz):
                    small_copy(3 + k).wait_recv()
                    total = total + r.smr[3 + k]
                own = heads * MEMORY_SLOTS
                mass = jnp.where(y == 0, total[2 * layers : 3 * layers, :own], total[2 * layers : 3 * layers, own:])
                small[...] = total
                small[2 * layers : 3 * layers, :own] = mass * (1.0 / count)

        tok_ld.wait()
        r.sm[0] = jnp.zeros(r.sm.shape[1:], F32)
        for l in range(layers):
            r.nrm[...] = rms(2 * l, ag[pl.ds(l, 1), :])
            weights_here()
            for turn in range(2):
                half = y if turn == 0 else oy
                slot = 2 * l + turn
                use = jnp.where(c == 1, slot, 2 * layers)
                if turn == 0:
                    w_ld[WI, l].wait()
                if slot:
                    state_sent(slot - 1, 0, 0)
                project(l, half)
                state_send(slot, 0, 0)
                weights_here()
                state_recv(slot, 0, 0)
                attend(l, half, use)
                weights_here()
            w_ld[WO, l].wait()
            attn_out(l)
            r.nrm[...] = rms(2 * l + 1, fg[pl.ds(l, 1), :])
            weights_here()
            w_ld[F1, l].wait()
            w_ld[F2, l].wait()
            r.acc[...] = r.h[2 * l + 1].astype(F32)
            ffn(l, 0, half_tiles)
            weights_here()
            for tile in range(half_tiles, tiles):
                ffn(l, tile, tile + 1)
                weights_here()
            r.h[2 * l + 2] = r.acc[...].astype(BF16)
        out_start(r.h.at[2 * layers], out, 0)
        w_end()
        state_sent(2 * layers - 1, 0, 0)
        cot_ld.wait()
        for l in range(layers):
            lm = r.lm[l].reshape(2 * heads * 64, 128).T
            r.sm[0, pl.ds(2 * layers + l, 1), :] = lm[0:1, :]

        for l in reversed(range(layers)):
            r.nT[...] = rms(2 * l + 1, fg[pl.ds(l, 1), :]).T
            r.acc[...] = jnp.zeros(r.acc.shape, F32)
            for tile in range(tiles):
                ffn_back(l, tile, tile + 1)
                gradients_here()
            rms_back(2 * l + 1, fg[pl.ds(l, 1), :], r.acc[...], layers + l)
            gradients_here()
            mixed_back(l)
            attn_out_grad(l)
            gradients_here()
            r.nT[...] = rms(2 * l, ag[pl.ds(l, 1), :]).T
            r.acc[...] = jnp.zeros(r.acc.shape, F32)
            for turn in range(2):
                half = oy if turn == 0 else y
                fwd_slot = jnp.where(c == 1, 2 * l + 1 - turn, 2 * layers)
                slot = 2 * l + turn
                use = jnp.where(c == 0, slot, 2 * layers)
                if not (turn == 0 and l == layers - 1):
                    prev = 2 * l if turn == 1 else 2 * (l + 1) + 1
                    state_sent(prev, 1, 1)
                attend_back(l, half, fwd_slot)
                state_send(slot, 1, 1)
                gradients_here()
                state_recv(slot, 1, 1)
                project_back(l, half, use)
                gradients_here()
            rms_back(2 * l, ag[pl.ds(l, 1), :], r.acc[...].T, l)
            if l == layers - 1:
                out_wait(r.h.at[2 * layers], out, 0)
            if l == 0:
                small_copy(0).start()
            gradients_here()
        state_sent(1, 1, 1)
        for step in range(4):
            small_sum(step)
            if step < 2:
                small_copy(step + 1).start()
            elif step == 2:
                for k in range(nz):
                    small_copy(3 + k).start()
            gradients_here()
        out_start(r.g, ig, 8)
        gradients_here()
        for step in range(3 + nz):
            small_copy(step).wait_send()
        g_end()
        out_wait(r.g, ig, 8)

    L = layers
    nzb = max(nz, 1)
    n_sem = len(pieces) * (ZS + 2 * nz)
    scratch = dict(
        v=[pltpu.VMEM((L, 2, *dims[k]), BF16) for k in KINDS],
        h=pltpu.VMEM((2 * L + 1, HALF, width), BF16),
        nT=pltpu.VMEM((width, HALF), BF16),
        nrm=pltpu.VMEM((HALF, width), BF16),
        g=pltpu.VMEM((HALF, width), BF16),
        pj=pltpu.VMEM((L, 2 * heads, HALF, 256), BF16),
        pjT=pltpu.VMEM((L, 2 * heads, 256, HALF), BF16),
        rz=pltpu.VMEM((L, 2 * heads, 64, HALF), F32),
        pr=pltpu.VMEM((L, 2 * heads, 64, HALF), BF16),
        sc=pltpu.VMEM((L, 2 * heads, 64, HALF), BF16),
        mixT=pltpu.VMEM((L, 2 * heads, 64, HALF), BF16),
        lm=pltpu.VMEM((L, 2 * heads, 64, 128), F32),
        gp=pltpu.VMEM((L, tiles, HALF, 512), BF16),
        actT=pltpu.VMEM((L, tiles, 512, HALF), BF16),
        acc=pltpu.VMEM((HALF, width), F32),
        tmp=pltpu.VMEM((heads, 192, HALF), F32),
        tri=pltpu.VMEM((BLK, BLK), BF16),
        state_out=pltpu.VMEM((2, heads, 256, 128), BF16),
        state_in=pltpu.VMEM((2 * L + 1, heads, 256, 128), BF16),
        sm=pltpu.VMEM((4, 8, width), F32),
        smr=pltpu.VMEM((3 + nzb, 8, width), F32),
        cr=pltpu.VMEM((len(TILES), 2, 256, 512), BF16),
        yr=pltpu.VMEM((len(pieces), 256, 512), BF16),
        xr=pltpu.VMEM((len(pieces), 128, 512), BF16),
        zr=pltpu.VMEM((len(pieces), nzb, 128 // shards, 512), BF16),
        fin=pltpu.VMEM((len(pieces), 128 // shards, 512), BF16),
        ld_sem=pltpu.SemaphoreType.DMA((2 + 4 * L,)),
        w_send=pltpu.SemaphoreType.DMA((4 * len(items),)),
        w_recv=pltpu.SemaphoreType.DMA((4 * len(items),)),
        st_send=pltpu.SemaphoreType.DMA((2 * L,)),
        st_recv=pltpu.SemaphoreType.DMA((2 * L,)),
        o_send=pltpu.SemaphoreType.DMA((16,)),
        o_recv=pltpu.SemaphoreType.DMA((16,)),
        g_send=pltpu.SemaphoreType.DMA((n_sem,)),
        g_recv=pltpu.SemaphoreType.DMA((n_sem,)),
        s_send=pltpu.SemaphoreType.DMA((3 + nzb,)),
        s_recv=pltpu.SemaphoreType.DMA((3 + nzb,)),
    )
    flat, layout = jax.tree.flatten(scratch)
    return kernel, flat


def finish(layers, width, out, ig, small, grads):
    steps = 8 * layers
    own = width // 2

    def kernel(out_in, ig_in, small_in, wi, wo, f1, f2, *results):
        out_to, ig_to, wi_to, wo_to, ag_to, f1_to, f2_to, fg_to, mass_to = results
        out_to[...] = out_in[...]
        ig_to[...] = ig_in[...]
        for source, target in ((wi, wi_to), (wo, wo_to), (f1, f1_to), (f2, f2_to)):
            target[...] = source[...].astype(F32)
        ag_to[...] = small_in[0:layers, :]
        fg_to[...] = small_in[layers : 2 * layers, :]
        mass_to[...] = small_in[2 * layers : 3 * layers, :own]

    edge = pl.BlockSpec((out.shape[0] // steps, out.shape[1]), lambda i: (i, 0))

    def part(v):
        return pl.BlockSpec((1, v.shape[1] // 8, v.shape[2]), lambda i: (i // 8, i % 8, 0))

    def whole(*shape):
        return pl.BlockSpec(shape, lambda i: (0, 0))

    like = [jax.ShapeDtypeStruct(v.shape, F32) for v in grads]
    gain = jax.ShapeDtypeStruct((layers, width), F32)
    mass = jax.ShapeDtypeStruct((layers, own), F32)
    edges = [jax.ShapeDtypeStruct(out.shape, BF16)] * 2
    gain_spec, mass_spec = whole(layers, width), whole(layers, own)
    parts = [part(v) for v in grads]
    return pl.pallas_call(
        kernel,
        grid=(steps,),
        in_specs=[edge, edge, whole(*small.shape), *parts],
        out_specs=[edge, edge, *parts[:2], gain_spec, *parts[2:], gain_spec, mass_spec],
        out_shape=[*edges, *like[:2], gain, *like[2:], gain, mass],
        compiler_params=pltpu.CompilerParams(vmem_limit_bytes=60 * 1024 * 1024),
    )(out, ig, small, *grads)


def solution(mesh):
    n_dp = mesh.shape["dp"]
    dp_inside = n_dp in (2, 4)

    def local(tokens, attn_gain, w_in, w_out, ffn_gain, ffn_in, ffn_out, cotangent):
        layers, width = attn_gain.shape
        arrays = (w_in, w_out, ffn_in, ffn_out)
        dims = [v.shape[1:] for v in arrays]
        kernel, scratch = make_kernel(
            layers, dims, n_dp, dp_inside, tokens.shape[0] * n_dp
        )
        anyspace = pl.BlockSpec(memory_space=pl.ANY)
        vmem = pl.BlockSpec(memory_space=pltpu.VMEM)
        edge = jax.ShapeDtypeStruct((tokens.shape[0], width // 4), BF16)
        results = pl.pallas_call(
            kernel,
            out_shape=[edge, edge]
            + [jax.ShapeDtypeStruct(v.shape, BF16) for v in arrays]
            + [jax.ShapeDtypeStruct((8, width), F32)],
            in_specs=[anyspace, vmem, vmem] + [anyspace] * 5,
            out_specs=[anyspace] * 6 + [vmem],
            scratch_shapes=scratch,
            compiler_params=pltpu.CompilerParams(
                collective_id=0, has_side_effects=True, vmem_limit_bytes=63 * 1024 * 1024
            ),
        )(tokens, attn_gain, ffn_gain, cotangent, *arrays)
        out, ig, *grads, small = results
        if not dp_inside and n_dp > 1:
            grads = [lax.psum(v, "dp") for v in grads]
            small = lax.psum(small, "dp")
        return finish(layers, width, out, ig, small, grads)

    placed = (
        P("dp", None),
        P(),
        P(None, None, "tensor"),
        P(None, "tensor", None),
        P(),
        P(None, None, "tensor"),
        P(None, "tensor", None),
        P("dp", None),
    )
    return jax.shard_map(
        local,
        mesh=mesh,
        in_specs=placed,
        out_specs=(
            P("dp", "section"),
            P("dp", "section"),
            P(None, None, "tensor"),
            P(None, "tensor", None),
            P(),
            P(None, None, "tensor"),
            P(None, "tensor", None),
            P(),
            P(None, "tensor"),
        ),
        check_vma=False,
    )
```

```python
import types

import jax
import jax.numpy as jnp
from jax import lax
from jax.experimental import pallas as pl
from jax.experimental.pallas import tpu as pltpu
from jax.sharding import PartitionSpec as P

HEAD_SIZE = 64
MEMORY_SLOTS = 64
SPAN = 1024
NORM_EPS = 1e-05
MESH = pl.DeviceIdType.MESH
F32 = jnp.float32
BF16 = jnp.bfloat16
HALF = SPAN // 2
BLK = 256
WI, WO, F1, F2 = KINDS = range(4)
TO_Y, TO_X, TO_Z, ON_Z, ON_X, TO_C = range(6)
W_COPIES = 9
CO, YO, XO, CW, XS, AX, AC, OWN, ZS = range(9)
EDGE_COPIES = 9
ITEMS = ((WI, 0), (WI, 1), (WO, 0), (F1, 0), (F2, 0), (F1, 1), (F2, 1))
TILES = ((F2, 0), (F1, 0), (F2, 1), (F1, 1), (WO, 0), (WI, 0), (WI, 1))
FORWARD = (
    (0, 8, 16),
    (),
    (),
    (1, 24, 9, 32, 17, 40, 2, 3, 25, 48, 10, 11, 33, 56, 18, 19, 4, 41, 64, 27, 26, 5, 49, 72, 12, 57, 80, 35, 34, 13),
    (20, 42, 43, 65, 88, 73, 96, 28),
    (50, 51, 58, 59, 36, 81, 104, 89, 21),
    (44, 97, 66, 67),
    (52, 60, 74, 75, 105, 29, 37),
    (82, 83, 45, 53),
    (90, 91),
    (98, 99),
    (68, 76, 106, 107),
    (84, 92, 100, 61, 69),
    (108,),
    (77,),
    (),
    (85, 93),
    (101, 109),
    (),
)
BACKWARD = (
    (224,),
    (0, 16),
    (32, 48),
    (1, 17, 2, 18),
    (33, 49, 34, 50, 225),
    (19,),
    (64, 66, 24, 51),
    (65, 56, 3, 67),
    (80, 96, 35),
    (81, 97, 72, 4),
    (82, 98, 20, 36),
    (),
    (112, 128, 88, 83, 52, 5),
    (113, 129, 144, 160, 21),
    (114, 130, 99, 37, 145, 161, 68),
    (146, 162, 115, 120, 131, 84, 53),
    (6,),
    (176, 178, 136),
    (177, 147, 100, 69, 22, 38),
    (192, 208, 163, 85),
    (193, 209, 116, 132, 148, 101, 54, 70, 7, 23, 179),
    (194, 210, 86, 39),
    (),
    (226, 117, 164, 195, 133, 55),
    (71, 149, 180, 211, 102, 87),
    (118, 165, 227, 134, 196, 150),
    (212, 181, 103, 197, 119, 213, 166, 182, 135, 198, 151, 214, 183, 199, 167, 215),
)
X_FIRST = (0, 1, 0, 1, 1, 1, 0, 1, 1, 0, 0, 0, 0, 0)
X_GATHER = (0, 0, 0, 0, 0, 0, 0, 0, 0, 0, 1, 0, 0, 0)
WIDE = 4


def nn(a, b):
    return lax.dot_general(a, b, (((1,), (0,)), ((), ())), preferred_element_type=F32)


def nt(a, b):
    return lax.dot_general(a, b, (((1,), (1,)), ((), ())), preferred_element_type=F32)


def loop(n, body):
    def step(i, carry):
        body(i)
        return carry

    lax.fori_loop(0, n, step, 0)


def together(n, width, body):
    def step(i):
        running = [body(width * i + j) for j in range(width)]
        for _ in zip(*running, strict=True):
            pass

    loop(n // width, step)


def make_kernel(layers, dims, n_dp, dp_inside, count):
    width = dims[WI][0]
    heads = dims[WI][1] // (3 * HEAD_SIZE + MEMORY_SLOTS)
    nz = n_dp - 1 if dp_inside else 0
    shards = n_dp if dp_inside else 1
    tiles = 2 * dims[F2][0] // 512
    half_tiles = tiles // 2
    items = [(k, l, t) for l in range(layers) for k, t in ITEMS]
    pieces = [(k, l, t) for l in reversed(range(layers)) for k, t in TILES]

    def tile_size(k):
        return min(dims[k][0], 512)


    def kernel(*refs):
        tok, ag, fg, cot, *rest = refs
        hbm, (out, ig, *grad), small = rest[:4], rest[4:10], rest[10]
        r = types.SimpleNamespace(**jax.tree.unflatten(layout, rest[11:]))
        s = lax.axis_index("section")
        z = lax.axis_index("dp")
        y = lax.axis_index("tensor")
        c = lax.rem(s, 2)
        x = s // 2
        oc, ox, oy = 1 - c, 1 - x, 1 - y
        dev_core = (x * 2 + oc, z, y)
        dev_x = (ox * 2 + c, z, y)
        dev_y = (s, z, oy)
        dev_cross = (x * 2 + oc, z, oy)

        z0 = lax.rem(z, 2)
        dev_pair = (s, z + 1 - 2 * z0, y)

        def dev_z(k):
            return (s, lax.rem(z + k, n_dp), y)

        barrier = pltpu.get_barrier_semaphore()
        everyone = [dev_core, dev_x, dev_y, dev_cross]
        everyone += [dev_z(k) for k in range(1, nz + 1)] if nz else [dev_pair]
        for d in everyone:
            pl.semaphore_signal(barrier, inc=1, device_id=d, device_id_type=MESH)

        row0 = pl.multiple_of((2 * x + y) * SPAN + c * HALF, HALF)

        def load(i, src, dst):
            return pltpu.make_async_copy(src, dst, r.ld_sem.at[i])

        tok_ld = load(0, tok.at[pl.ds(row0, HALF), :], r.h.at[0])
        cot_ld = load(1, cot.at[pl.ds(row0, HALF), :], r.g)
        w_ld = {}
        for l in range(layers):
            for k in KINDS:
                at = 2 + l * 4 + k
                w_ld[k, l] = load(at, hbm[k].at[l], r.v[k].at[l, y])

        tok_ld.start()
        w_ld[WI, 0].start()

        def tile_rows(k, t, start, size):
            first = t * 512 if k == F2 else 0
            return pl.ds(pl.multiple_of(first + start, 16), size)

        def tile_cols(k, t):
            return pl.ds(t * 512 if k in (WI, F1) else 0, 512)

        def w_copy(i, stage):
            k, l, t = items[i]
            rows, cols = tile_size(k) // 8, tile_cols(k, t)

            def eighth(cx, cz, start=0, size=rows):
                return tile_rows(k, t, (4 * cx + 2 * cz + c) * rows + start, size)

            mine, half = eighth(x, z0), rows // 2
            v = r.v[k].at[l]
            span, dev = (
                (mine, dev_y),
                (mine, dev_x),
                (mine, dev_pair),
                (eighth(ox, z0, 0, half), dev_pair),
                (eighth(x, 1 - z0, half, half), dev_x),
                (mine, dev_core),
                (eighth(ox, z0), dev_core),
                (eighth(x, 1 - z0), dev_core),
                (eighth(ox, 1 - z0), dev_core),
            )[stage]
            side = y if stage == TO_Y else oy
            return pltpu.make_async_remote_copy(
                src_ref=hbm[k].at[l, span, cols] if stage == TO_Y else v.at[side, span, cols],
                dst_ref=v.at[side, span, cols],
                send_sem=r.w_send.at[i * W_COPIES + stage],
                recv_sem=r.w_recv.at[i * W_COPIES + stage],
                device_id=dev,
                device_id_type=MESH,
            )

        def w_event(i, e):
            waits, starts = (
                ((), (TO_Y,)),
                ((TO_Y,), (TO_X, TO_Z, TO_C)),
                ((TO_X,), (ON_Z, TO_C + 1)),
                ((TO_Z,), (ON_X, TO_C + 2)),
                ((ON_Z, ON_X), (TO_C + 3,)),
                ((TO_C, TO_C + 1, TO_C + 2, TO_C + 3), ()),
            )[e]
            for stage in waits:
                w_copy(i, stage).wait_recv()
            for stage in starts:
                w_copy(i, stage).start()

        def w_end():
            for i in range(len(items)):
                for stage in range(W_COPIES):
                    w_copy(i, stage).wait_send()

        forward_plan = iter(FORWARD)

        def weights_here():
            for code in next(forward_plan):
                w_event(code // 8, code % 8)

        pl.semaphore_wait(barrier, len(everyone))
        weights_here()
        for l in range(layers):
            for k in KINDS:
                if (k, l) != (WI, 0):
                    w_ld[k, l].start()
        cot_ld.start()

        tri_s = lax.broadcasted_iota(jnp.int32, (BLK, BLK), 0)
        tri_t = lax.broadcasted_iota(jnp.int32, (BLK, BLK), 1)
        r.tri[...] = jnp.where(tri_s <= tri_t, 1.0, 0.0).astype(BF16)
        r.state_in[2 * layers] = jnp.zeros(r.state_in.shape[1:], BF16)

        def masked(v, on):
            if not on:
                return v.astype(BF16)
            keep = lax.broadcasted_iota(jnp.int32, (BLK, BLK), 0) <= lax.broadcasted_iota(
                jnp.int32, (BLK, BLK), 1
            )
            return jnp.where(keep, v, 0.0).astype(BF16)

        def blocks(tb):
            return [(b, b == tb) for b in range(tb + 1)]

        def state_copy(slot, buf):
            return pltpu.make_async_remote_copy(
                src_ref=r.state_out.at[buf],
                dst_ref=r.state_in.at[slot],
                send_sem=r.st_send.at[slot],
                recv_sem=r.st_recv.at[slot],
                device_id=dev_core,
                device_id_type=MESH,
            )

        def state_send(slot, buf, from_core):
            @pl.when(c == from_core)
            def _():
                state_copy(slot, buf).start()

        def state_recv(slot, buf, from_core):
            @pl.when(c != from_core)
            def _():
                state_copy(slot, buf).wait_recv()

        def state_sent(slot, buf, from_core):
            @pl.when(c == from_core)
            def _():
                state_copy(slot, buf).wait_send()

        def rms(sub, gain):
            h = r.h[sub].astype(F32)
            scale = lax.rsqrt(jnp.mean(h * h, axis=1, keepdims=True) + NORM_EPS)
            return (h * scale * gain).astype(BF16)

        def rms_back(sub, gain, dn, gain_row):
            h = r.h[sub].astype(F32)
            scale = lax.rsqrt(jnp.mean(h * h, axis=1, keepdims=True) + NORM_EPS)
            a = dn * gain
            hs = h * scale
            r.sm[0, pl.ds(gain_row, 1), :] = jnp.sum(dn * hs, axis=0, keepdims=True)
            dh = scale * (a - hs * jnp.mean(hs * a, axis=1, keepdims=True))
            r.g[...] = (r.g[...].astype(F32) + dh).astype(BF16)

        def project(l, half):
            def head(i):
                hd = half * heads + i
                cols = pl.ds(pl.multiple_of(i * 256, 256), 256)
                p = nn(r.nrm[...], r.v[WI][l, half, :, cols])
                yield
                lane = lax.broadcasted_iota(jnp.int32, (HALF, 128), 1)
                hi = p[:, 128:]
                hi = jnp.where(lane >= 64, jnp.exp(hi), hi)
                pb = jnp.concatenate([p[:, :128], hi], axis=1).astype(BF16)
                r.pj[l, hd] = pb
                pt = pb.T
                r.pjT[l, hd] = pt
                yield
                kv = pt[64:192]
                e = pt[192:256]
                buf = r.state_out.at[0]
                buf[i, 0:64, :] = nt(e, kv).astype(BF16)
                buf[i, 64:192, 0:64] = nt(kv, e).astype(BF16)
                buf[i, 192:256, :] = nn(e, jnp.ones((HALF, 128), BF16)).astype(BF16)
                yield

            together(heads, WIDE, head)

        def attend(l, half, slot):
            def head(i):
                hd = half * heads + i
                q = r.pjT[l, hd, 0:64, :]
                v = r.pjT[l, hd, 128:192, :]
                e = r.pjT[l, hd, 192:256, :]
                sk = r.state_in[slot, i, 0:64, 0:64]
                svt = r.state_in[slot, i, 128:192, 0:64]
                before = r.state_in[slot, i, 192:256, 0:1].astype(F32)
                zero = jnp.zeros((64, BLK), BF16)
                log_sum = jnp.zeros((64, 1), F32)
                for tb in range(2):
                    ts = slice(tb * BLK, (tb + 1) * BLK)
                    qt = q[:, ts]
                    rq = jnp.concatenate([zero, qt], axis=0)
                    num = nn(sk, qt)
                    yield
                    for b, on in blocks(tb):
                        bs = slice(b * BLK, (b + 1) * BLK)
                        at = masked(nn(r.pj[l, hd, bs, 0:128], rq), on)
                        yield
                        num = num + nn(e[:, bs], at)
                        yield
                    zt = nn(e[:, ts], r.tri[...]) + before
                    before = zt[:, BLK - 1 : BLK]
                    rz = 1.0 / zt
                    sc = num * rz * 0.125
                    yield
                    ex = jnp.exp(sc - jnp.max(sc, axis=0, keepdims=True))
                    p = ex * (1.0 / jnp.sum(ex, axis=0, keepdims=True))
                    w = (p * rz).astype(BF16)
                    r.rz[l, hd, :, ts] = rz
                    r.pr[l, hd, :, ts] = p.astype(BF16)
                    r.sc[l, hd, :, ts] = sc.astype(BF16)
                    log_sum = log_sum + jnp.sum(jnp.log(zt), axis=1, keepdims=True)
                    rw = jnp.concatenate([zero, w], axis=0)
                    yield
                    o = nn(svt, w)
                    for b, on in blocks(tb):
                        bs = slice(b * BLK, (b + 1) * BLK)
                        gt = masked(nn(r.pj[l, hd, bs, 128:256], rw), on)
                        yield
                        o = o + nn(v[:, bs], gt)
                        yield
                    r.mixT[l, hd, :, ts] = o.astype(BF16)
                r.lm[l, hd] = jnp.broadcast_to(log_sum, (64, 128))
                yield

            together(heads, WIDE, head)

        def attn_out(l):
            mixed = r.mixT[l].reshape(2 * heads * 64, HALF).T
            wo = r.v[WO][l].reshape(2 * dims[WO][0], width)
            r.h[2 * l + 1] = (r.h[2 * l].astype(F32) + nn(mixed, wo)).astype(BF16)

        def tile_of(i, first):
            j = lax.rem(first * half_tiles + i, tiles)
            return j, j // half_tiles, pl.ds(pl.multiple_of(lax.rem(j, half_tiles) * 512, 512), 512)

        def ffn(l, lo, hi):
            k = 0.7978845608028654

            def tile(i):
                j, half, at = tile_of(i + lo, y)
                w1 = r.v[F1][l, half, :, at]
                w2 = r.v[F2][l, half, at, :]
                for tb in range(2):
                    ts = slice(tb * BLK, (tb + 1) * BLK)
                    b = nn(r.nrm[ts, :], w1)
                    bb = b * b
                    th = jnp.tanh(k * b * (1.0 + 0.044715 * bb))
                    hp = 0.5 * (1.0 + th)
                    act = (b * hp).astype(BF16)
                    slope = hp + (0.5 * k) * b * (1.0 - th * th) * (1.0 + 0.134145 * bb)
                    r.gp[l, j, ts, :] = slope.astype(BF16)
                    r.actT[l, j, :, ts] = act.T
                    r.acc[ts, :] = r.acc[ts, :] + nn(act, w2)

            loop(hi - lo, tile)

        def ffn_back(l, lo, hi):
            def tile(i):
                j, half, at = tile_of(i + lo, oy)
                w1 = r.v[F1][l, half, :, at]
                w2 = r.v[F2][l, half, at, :]
                for tb in range(2):
                    ts = slice(tb * BLK, (tb + 1) * BLK)
                    db = (nt(r.g[ts, :], w2) * r.gp[l, j, ts, :].astype(F32)).astype(BF16)
                    r.nrm[ts, :] = db
                    r.acc[ts, :] = r.acc[ts, :] + nt(db, w1)
                r.v[F2][l, half, at, :] = nn(r.actT[l, j], r.g[...]).astype(BF16)
                r.v[F1][l, half, :, at] = nn(r.nT[...], r.nrm[...]).astype(BF16)

            loop(hi - lo, tile)

        def mixed_back(l):
            wo = r.v[WO][l].reshape(2 * dims[WO][0], width)
            r.nrm[...] = nt(wo, r.g[...]).astype(BF16)

        def attn_out_grad(l):
            mixed = r.mixT[l].reshape(2 * heads * 64, HALF)
            r.v[WO][l] = nn(mixed, r.g[...]).astype(BF16).reshape(r.v[WO].shape[1:])

        def attend_back(l, half, slot):
            def head(i):
                hd = half * heads + i
                q = r.pjT[l, hd, 0:64, :]
                kt = r.pjT[l, hd, 64:128, :]
                e = r.pjT[l, hd, 192:256, :]
                do = r.nrm[pl.ds(pl.multiple_of(hd * 64, 64), 64), :]
                skv = r.state_in[slot, i, 0:64, :]
                skt = r.state_in[slot, i, 64:128, 0:64]
                zero = jnp.zeros((64, BLK), BF16)
                none = jnp.zeros((64, BLK), F32)
                dv, dk, de = [none, none], [none, none], [none, none]
                dzs, dns, ws, dqs = [], [], [], []
                for tb in range(2):
                    ts = slice(tb * BLK, (tb + 1) * BLK)
                    dot, qt = do[:, ts], q[:, ts]
                    rd = jnp.concatenate([dot, zero], axis=0)
                    rz = r.rz[l, hd, :, ts]
                    p = r.pr[l, hd, :, ts].astype(F32)
                    sc = r.sc[l, hd, :, ts].astype(F32)
                    w = p * rz
                    wb = w.astype(BF16)
                    dw = nn(skv, jnp.concatenate([zero, dot], axis=0))
                    dgs = []
                    for b, on in blocks(tb):
                        bs = slice(b * BLK, (b + 1) * BLK)
                        dg = masked(nn(r.pj[l, hd, bs, 128:256], rd), on)
                        yield
                        dw = dw + nn(e[:, bs], dg)
                        dgs.append(dg)
                        yield
                    dp = dw * rz
                    ds = p * (dp - jnp.sum(p * dp, axis=0, keepdims=True))
                    dnb = (ds * rz * 0.125).astype(BF16)
                    dzs.append((-(dw * w + ds * sc) * rz).astype(BF16))
                    dns.append(dnb)
                    ws.append(wb)
                    rw = jnp.concatenate([zero, wb], axis=0)
                    rn = jnp.concatenate([zero, dnb], axis=0)
                    rq = jnp.concatenate([zero, qt], axis=0)
                    yield
                    dq = nn(skt, dnb)
                    for b, on in blocks(tb):
                        bs = slice(b * BLK, (b + 1) * BLK)
                        qk = r.pj[l, hd, bs, 0:128]
                        ve = r.pj[l, hd, bs, 128:256]
                        at = masked(nn(qk, rq), on)
                        yield
                        gt = masked(nn(ve, rw), on)
                        yield
                        da = masked(nn(ve, rn), on)
                        yield
                        dv[b] = dv[b] + nt(dot, gt)
                        de[b] = de[b] + nt(wb, dgs[b]) + nt(dnb, at)
                        dk[b] = dk[b] + nt(qt, da)
                        dq = dq + nn(kt[:, bs], da)
                        yield
                    dqs.append(dq.astype(BF16))
                tri = r.tri[...]
                rev1 = nt(dzs[1], tri)
                rev0 = nt(dzs[0], tri) + rev1[:, 0:1]
                tmp = r.tmp.at[i]
                for b, rev in enumerate((rev0, rev1)):
                    bs = slice(b * BLK, (b + 1) * BLK)
                    tmp[0:64, bs] = dk[b]
                    tmp[64:128, bs] = dv[b]
                    tmp[128:192, bs] = de[b] + rev
                dn_all = jnp.concatenate(dns, axis=1)
                w_all = jnp.concatenate(ws, axis=1)
                buf = r.state_out.at[1]
                buf[i, 0:64, :] = jnp.concatenate([nt(dn_all, q), nt(w_all, do)], axis=1).astype(
                    BF16
                )
                buf[i, 64:128, 0:64] = nt(q, dn_all).astype(BF16)
                buf[i, 128:192, 0:64] = nt(do, w_all).astype(BF16)
                r.pjT[l, hd, 0:64, :] = jnp.concatenate(dqs, axis=1)
                buf[i, 192:256, :] = jnp.broadcast_to(rev0[:, 0:1], (64, 128)).astype(BF16)
                yield

            together(heads, WIDE, head)

        def project_back(l, half, slot):
            def head(i):
                hd = half * heads + i
                kv = r.pjT[l, hd, 64:192, :]
                e = r.pjT[l, hd, 192:256, :]
                sin = r.state_in.at[slot]
                dkv = r.tmp[i, 0:128, :] + nn(sin[i, 64:192, 0:64], e)
                de = r.tmp[i, 128:192, :] + nn(sin[i, 0:64, :], kv)
                de = (de + sin[i, 192:256, 0:1].astype(F32)) * e.astype(F32)
                r.pjT[l, hd, 64:192, :] = dkv.astype(BF16)
                r.pjT[l, hd, 192:256, :] = de.astype(BF16)
                cols = pl.ds(pl.multiple_of(i * 256, 256), 256)
                dp = r.pjT[l, hd]
                r.acc[...] = r.acc[...] + nn(r.v[WI][l, half, :, cols], dp)
                r.v[WI][l, half, :, cols] = nt(r.nT[...], dp).astype(BF16)

            loop(heads, head)

        def edge_copies(n, forward):
            src = r.edge.at[n] if forward else (r.h.at[2 * layers], r.g)[n]
            dst = (out, ig)[n]
            sequence = 2 * (ox if forward else x) + y
            rows = pl.ds(pl.multiple_of(sequence * SPAN + c * HALF, HALF), HALF)
            first = 0 if forward else x * 256

            def part(start, size=128):
                return src.at[:, pl.ds(pl.multiple_of(start, 128), size)]

            at = n * EDGE_COPIES + (5 if forward else 0)
            places = [(dev_core, oc), (dev_y, c), (dev_cross, oc)]
            copies = [(part(first + core * 128), dst.at[rows, :], dev) for dev, core in places]
            if not forward:
                copies.append((part(ox * 256, 256), r.edge.at[n], dev_x))
            remote = [
                pltpu.make_async_remote_copy(
                    src_ref=a,
                    dst_ref=b,
                    send_sem=r.o_send.at[at + 1 + q],
                    recv_sem=r.o_recv.at[at + 1 + q],
                    device_id=dev,
                    device_id_type=MESH,
                )
                for q, (a, b, dev) in enumerate(copies)
            ]
            own = pltpu.make_async_copy(part(first + c * 128), dst.at[rows, :], r.o_send.at[at])
            return remote, own

        def edge_event(n, forward):
            if forward:
                edge_copies(n, False)[0][3].wait_recv()
            remote, own = edge_copies(n, forward)
            for copy in reversed(remote):
                copy.start()
            own.start()

        def edge_end():
            for n in range(2):
                for forward in (False, True):
                    remote, own = edge_copies(n, forward)
                    for q, copy in enumerate(remote):
                        copy.wait_send()
                        if q < 3:
                            copy.wait_recv()
                    own.wait()

        n_stage = ZS + 3 * nz

        def g_copy(p, stage):
            k, l, t = pieces[p]
            rows, cols = tile_size(k) // 2, tile_cols(k, t)
            xr = rows // 2
            zr = xr // shards
            part, full = r.v[k].at[l], grad[k].at[l]
            at = p * n_stage + stage
            sems = dict(send_sem=r.g_send.at[at], recv_sem=r.g_recv.at[at])

            def rng(start, size):
                return tile_rows(k, t, start, size)

            shard = rng(c * rows + x * xr + (z * zr if nz else 0), zr)
            head = pl.ds(0, rows)
            if stage == OWN:
                return pltpu.make_async_copy(
                    r.fin.at[p, pl.ds(0, zr)], full.at[shard, cols], r.g_send.at[at]
                )
            x_first, x_gather = X_FIRST[p] == 1, X_GATHER[p] == 1
            cut, low = pl.ds(0, xr), pl.ds(xr, xr)
            if stage == CO:
                src, dev = part.at[oy, rng(oc * rows, rows), cols], dev_core
                dst = r.co.at[p % len(TILES), head]
            elif stage == CW:
                src, dev = part.at[y, rng(oc * rows, rows), cols], dev_core
                dst = r.cw.at[p, head]
            elif stage == XO:
                src, dev = part.at[oy, rng(c * rows + ox * xr, xr), cols], dev_x
                dst = r.yr.at[p, cut]
            elif stage == YO and x_first:
                src, dev = part.at[oy, rng(c * rows + x * xr, xr), cols], dev_y
                dst = r.yr.at[p, low]
            elif stage == YO:
                src, dst, dev = part.at[oy, rng(c * rows, rows), cols], r.yr.at[p, head], dev_y
            elif stage == XS:
                src = part.at[y, rng(c * rows + ox * xr, xr), cols]
                dst, dev = r.xr.at[p, cut], dev_x
            elif stage == AX and x_gather:
                src, dst, dev = r.fin.at[p, pl.ds(0, zr)], full.at[shard, cols], dev_x
            elif stage == AX:
                span = rng(c * rows + x * xr, xr)
                src, dst, dev = full.at[span, cols], full.at[span, cols], dev_x
            elif stage == AC:
                span = rng(c * rows, rows)
                src, dst, dev = full.at[span, cols], full.at[span, cols], dev_core
            elif stage < ZS + nz:
                step = stage - ZS + 1
                dev = dev_z(step)
                src = part.at[y, rng(c * rows + x * xr + dev[1] * zr, zr), cols]
                dst = r.zr.at[p, step - 1, pl.ds(0, zr)]
            elif stage < ZS + 2 * nz:
                dev = dev_z(stage - ZS - nz + 1)
                src, dst = r.fin.at[p, pl.ds(0, zr)], full.at[shard, cols]
            else:
                dev = dev_z(stage - ZS - 2 * nz + 1)
                span = rng(c * rows + ox * xr + z * zr, zr)
                src, dst = full.at[span, cols], full.at[span, cols]
            return pltpu.make_async_remote_copy(
                src_ref=src, dst_ref=dst, device_id=dev, device_id_type=MESH, **sems
            )

        def used(p, stage):
            if stage == XO:
                return X_FIRST[p] == 1
            return stage < ZS + 2 * nz or X_GATHER[p] == 1

        def add_rows(p, total, half, start, sources, target=None):
            k, l, t = pieces[p]
            cols = tile_cols(k, t)
            cut = min(total, 64)

            def rows_step(i):
                rows = tile_rows(k, t, start + i * cut, cut)
                here = pl.ds(pl.multiple_of(i * cut, 16), cut)
                value = r.v[k][l, half, rows, cols].astype(F32)
                for source in sources:
                    value = value + source[here, :].astype(F32)
                if target is None:
                    r.v[k][l, half, rows, cols] = value.astype(BF16)
                else:
                    target[here, :] = value.astype(BF16)

            loop(total // cut, rows_step)

        def g_event(p, e):
            rows = tile_size(pieces[p][0]) // 2
            xr = rows // 2
            zr = xr // shards
            x_first, x_gather = X_FIRST[p] == 1, X_GATHER[p] == 1
            here = c * rows + x * xr
            to_z = [ZS + step for step in range(nz)]
            gather = [ZS + nz + step for step in range(nz)]
            on_z = [ZS + 2 * nz + step for step in range(nz)]

            def wait(*stages):
                for stage in stages:
                    g_copy(p, stage).wait_recv()

            def start(*stages):
                for stage in stages:
                    g_copy(p, stage).start()

            if e == 0:
                start(CO)
            elif e == 1:
                wait(CO)
                add_rows(p, rows, oy, c * rows, [r.co.at[p % len(TILES)]])
                start(XO if x_first else YO)
            elif e == 2:
                start(CW)
            elif e == 3 and x_first:
                wait(CW)
                add_rows(p, rows, y, c * rows, [r.cw.at[p]])
                start(XS)
            elif e == 3:
                wait(CW, YO)
                add_rows(p, rows, y, c * rows, [r.cw.at[p], r.yr.at[p]])
                start(XS)
            elif e == 8:
                wait(XO)
                add_rows(p, xr, oy, here, [r.yr.at[p]])
                start(YO)
            elif e == 4:
                wait(XS)
                sources = [r.xr.at[p]]
                if x_first:
                    wait(YO)
                    sources.append(r.yr.at[p, pl.ds(xr, xr)])
                add_rows(p, xr, y, here, sources)
                start(*to_z)
            elif e == 5:
                wait(*to_z)
                sources = [r.zr.at[p, step] for step in range(nz)]
                add_rows(p, zr, y, here + (z * zr if nz else 0), sources, r.fin.at[p])
                start(*([AX] if x_gather else gather))
                start(OWN)
            elif e == 6:
                g_copy(p, OWN).wait()
                if x_gather:
                    wait(AX)
                    start(*gather, *on_z)
                else:
                    wait(*gather)
                    start(AX)
            elif e == 7:
                if x_gather:
                    wait(*gather, *on_z)
                else:
                    wait(AX)
                start(AC)

        backward_plan = iter(BACKWARD)

        def gradients_here():
            for code in next(backward_plan):
                p, e = divmod(code, 16)
                if p < len(pieces):
                    g_event(p, e)
                else:
                    edge_event(e // 2, e % 2 == 1)

        def g_end():
            for p in range(len(pieces)):
                g_copy(p, AC).wait_recv()
                for stage in range(n_stage):
                    if stage != OWN and used(p, stage):
                        g_copy(p, stage).wait_send()

        def small_copy(step):
            dev = [dev_core, dev_y, dev_x][step] if step < 3 else dev_z(step - 2)
            return pltpu.make_async_remote_copy(
                src_ref=r.sm.at[min(step, 3)],
                dst_ref=r.smr.at[step],
                send_sem=r.s_send.at[step],
                recv_sem=r.s_recv.at[step],
                device_id=dev,
                device_id_type=MESH,
            )

        def small_sum(step):
            if step < 3:
                small_copy(step).wait_recv()
                r.sm[step + 1] = r.sm[step] + r.smr[step]
            else:
                total = r.sm[3]
                for k in range(nz):
                    small_copy(3 + k).wait_recv()
                    total = total + r.smr[3 + k]
                own = heads * MEMORY_SLOTS
                mass = jnp.where(y == 0, total[2 * layers : 3 * layers, :own], total[2 * layers : 3 * layers, own:])
                small[...] = total
                small[2 * layers : 3 * layers, :own] = mass * (1.0 / count)

        tok_ld.wait()
        r.sm[0] = jnp.zeros(r.sm.shape[1:], F32)
        for l in range(layers):
            r.nrm[...] = rms(2 * l, ag[pl.ds(l, 1), :])
            weights_here()
            for turn in range(2):
                half = y if turn == 0 else oy
                slot = 2 * l + turn
                use = jnp.where(c == 1, slot, 2 * layers)
                if turn == 0:
                    w_ld[WI, l].wait()
                if slot:
                    state_sent(slot - 1, 0, 0)
                project(l, half)
                state_send(slot, 0, 0)
                weights_here()
                state_recv(slot, 0, 0)
                attend(l, half, use)
                weights_here()
            w_ld[WO, l].wait()
            attn_out(l)
            r.nrm[...] = rms(2 * l + 1, fg[pl.ds(l, 1), :])
            weights_here()
            w_ld[F1, l].wait()
            w_ld[F2, l].wait()
            r.acc[...] = r.h[2 * l + 1].astype(F32)
            ffn(l, 0, half_tiles)
            weights_here()
            for tile in range(half_tiles, tiles):
                ffn(l, tile, tile + 1)
                weights_here()
            r.h[2 * l + 2] = r.acc[...].astype(BF16)
        gradients_here()
        w_end()
        state_sent(2 * layers - 1, 0, 0)
        cot_ld.wait()
        for l in range(layers):
            lm = r.lm[l].reshape(2 * heads * 64, 128).T
            r.sm[0, pl.ds(2 * layers + l, 1), :] = lm[0:1, :]

        for l in reversed(range(layers)):
            r.nT[...] = rms(2 * l + 1, fg[pl.ds(l, 1), :]).T
            r.acc[...] = jnp.zeros(r.acc.shape, F32)
            for tile in range(tiles):
                ffn_back(l, tile, tile + 1)
                gradients_here()
            rms_back(2 * l + 1, fg[pl.ds(l, 1), :], r.acc[...], layers + l)
            gradients_here()
            mixed_back(l)
            attn_out_grad(l)
            gradients_here()
            r.nT[...] = rms(2 * l, ag[pl.ds(l, 1), :]).T
            r.acc[...] = jnp.zeros(r.acc.shape, F32)
            for turn in range(2):
                half = oy if turn == 0 else y
                fwd_slot = jnp.where(c == 1, 2 * l + 1 - turn, 2 * layers)
                slot = 2 * l + turn
                use = jnp.where(c == 0, slot, 2 * layers)
                if not (turn == 0 and l == layers - 1):
                    prev = 2 * l if turn == 1 else 2 * (l + 1) + 1
                    state_sent(prev, 1, 1)
                attend_back(l, half, fwd_slot)
                state_send(slot, 1, 1)
                gradients_here()
                state_recv(slot, 1, 1)
                project_back(l, half, use)
                gradients_here()
            rms_back(2 * l, ag[pl.ds(l, 1), :], r.acc[...].T, l)
            if l == 0:
                small_copy(0).start()
            gradients_here()
        state_sent(1, 1, 1)
        for step in range(4):
            small_sum(step)
            if step < 2:
                small_copy(step + 1).start()
            elif step == 2:
                for k in range(nz):
                    small_copy(3 + k).start()
            gradients_here()
        for step in range(3 + nz):
            small_copy(step).wait_send()
        g_end()
        edge_end()

    L = layers
    nzb = max(nz, 1)
    n_sem = len(pieces) * (ZS + 3 * nz)
    scratch = dict(
        v=[pltpu.VMEM((L, 2, *dims[k]), BF16) for k in KINDS],
        h=pltpu.VMEM((2 * L + 1, HALF, width), BF16),
        nT=pltpu.VMEM((width, HALF), BF16),
        nrm=pltpu.VMEM((HALF, width), BF16),
        g=pltpu.VMEM((HALF, width), BF16),
        pj=pltpu.VMEM((L, 2 * heads, HALF, 256), BF16),
        pjT=pltpu.VMEM((L, 2 * heads, 256, HALF), BF16),
        rz=pltpu.VMEM((L, 2 * heads, 64, HALF), F32),
        pr=pltpu.VMEM((L, 2 * heads, 64, HALF), BF16),
        sc=pltpu.VMEM((L, 2 * heads, 64, HALF), BF16),
        mixT=pltpu.VMEM((L, 2 * heads, 64, HALF), BF16),
        lm=pltpu.VMEM((L, 2 * heads, 64, 128), F32),
        gp=pltpu.VMEM((L, tiles, HALF, 512), BF16),
        actT=pltpu.VMEM((L, tiles, 512, HALF), BF16),
        acc=pltpu.VMEM((HALF, width), F32),
        tmp=pltpu.VMEM((heads, 192, HALF), F32),
        tri=pltpu.VMEM((BLK, BLK), BF16),
        state_out=pltpu.VMEM((2, heads, 256, 128), BF16),
        state_in=pltpu.VMEM((2 * L + 1, heads, 256, 128), BF16),
        sm=pltpu.VMEM((4, 8, width), F32),
        smr=pltpu.VMEM((3 + nzb, 8, width), F32),
        co=pltpu.VMEM((len(TILES), 256, 512), BF16),
        cw=pltpu.VMEM((len(pieces), 256, 512), BF16),
        edge=pltpu.VMEM((2, HALF, 256), BF16),
        yr=pltpu.VMEM((len(pieces), 256, 512), BF16),
        xr=pltpu.VMEM((len(pieces), 128, 512), BF16),
        zr=pltpu.VMEM((len(pieces), nzb, 128 // shards, 512), BF16),
        fin=pltpu.VMEM((len(pieces), 128 // shards, 512), BF16),
        ld_sem=pltpu.SemaphoreType.DMA((2 + 4 * L,)),
        w_send=pltpu.SemaphoreType.DMA((W_COPIES * len(items),)),
        w_recv=pltpu.SemaphoreType.DMA((W_COPIES * len(items),)),
        st_send=pltpu.SemaphoreType.DMA((2 * L,)),
        st_recv=pltpu.SemaphoreType.DMA((2 * L,)),
        o_send=pltpu.SemaphoreType.DMA((2 * EDGE_COPIES,)),
        o_recv=pltpu.SemaphoreType.DMA((2 * EDGE_COPIES,)),
        g_send=pltpu.SemaphoreType.DMA((n_sem,)),
        g_recv=pltpu.SemaphoreType.DMA((n_sem,)),
        s_send=pltpu.SemaphoreType.DMA((3 + nzb,)),
        s_recv=pltpu.SemaphoreType.DMA((3 + nzb,)),
    )
    flat, layout = jax.tree.flatten(scratch)
    return kernel, flat


def finish(layers, width, out, ig, small, grads):
    steps = 2 * layers
    own = width // 2

    def kernel(out_in, ig_in, small_in, wi, wo, f1, f2, *results):
        out_to, ig_to, wi_to, wo_to, ag_to, f1_to, f2_to, fg_to, mass_to = results
        out_to[...] = out_in[...]
        ig_to[...] = ig_in[...]
        for source, target in ((wi, wi_to), (wo, wo_to), (f1, f1_to), (f2, f2_to)):
            target[...] = source[...].astype(F32)
        ag_to[...] = small_in[0:layers, :]
        fg_to[...] = small_in[layers : 2 * layers, :]
        mass_to[...] = small_in[2 * layers : 3 * layers, :own]

    edge = pl.BlockSpec((out.shape[0] // steps, out.shape[1]), lambda i: (i, 0))

    def part(v):
        return pl.BlockSpec((1, v.shape[1] // 2, v.shape[2]), lambda i: (i // 2, i % 2, 0))

    def whole(*shape):
        return pl.BlockSpec(shape, lambda i: (0, 0))

    like = [jax.ShapeDtypeStruct(v.shape, F32) for v in grads]
    gain = jax.ShapeDtypeStruct((layers, width), F32)
    mass = jax.ShapeDtypeStruct((layers, own), F32)
    edges = [jax.ShapeDtypeStruct(out.shape, BF16)] * 2
    gain_spec, mass_spec = whole(layers, width), whole(layers, own)
    parts = [part(v) for v in grads]
    return pl.pallas_call(
        kernel,
        grid=(steps,),
        in_specs=[edge, edge, whole(*small.shape), *parts],
        out_specs=[edge, edge, *parts[:2], gain_spec, *parts[2:], gain_spec, mass_spec],
        out_shape=[*edges, *like[:2], gain, *like[2:], gain, mass],
        compiler_params=pltpu.CompilerParams(vmem_limit_bytes=60 * 1024 * 1024),
    )(out, ig, small, *grads)


def solution(mesh):
    n_dp = mesh.shape["dp"]
    dp_inside = n_dp in (2, 4)

    def local(tokens, attn_gain, w_in, w_out, ffn_gain, ffn_in, ffn_out, cotangent):
        layers, width = attn_gain.shape
        arrays = (w_in, w_out, ffn_in, ffn_out)
        dims = [v.shape[1:] for v in arrays]
        kernel, scratch = make_kernel(
            layers, dims, n_dp, dp_inside, tokens.shape[0] * n_dp
        )
        anyspace = pl.BlockSpec(memory_space=pl.ANY)
        vmem = pl.BlockSpec(memory_space=pltpu.VMEM)
        edge = jax.ShapeDtypeStruct((tokens.shape[0], width // 4), BF16)
        results = pl.pallas_call(
            kernel,
            out_shape=[edge, edge]
            + [jax.ShapeDtypeStruct(v.shape, BF16) for v in arrays]
            + [jax.ShapeDtypeStruct((8, width), F32)],
            in_specs=[anyspace, vmem, vmem] + [anyspace] * 5,
            out_specs=[anyspace] * 6 + [vmem],
            scratch_shapes=scratch,
            compiler_params=pltpu.CompilerParams(
                collective_id=0, has_side_effects=True, vmem_limit_bytes=63 * 1024 * 1024
            ),
        )(tokens, attn_gain, ffn_gain, cotangent, *arrays)
        out, ig, *grads, small = results
        if not dp_inside and n_dp > 1:
            grads = [lax.psum(v, "dp") for v in grads]
            small = lax.psum(small, "dp")
        return finish(layers, width, out, ig, small, grads)

    placed = (
        P("dp", None),
        P(),
        P(None, None, "tensor"),
        P(None, "tensor", None),
        P(),
        P(None, None, "tensor"),
        P(None, "tensor", None),
        P("dp", None),
    )
    return jax.shard_map(
        local,
        mesh=mesh,
        in_specs=placed,
        out_specs=(
            P("dp", "section"),
            P("dp", "section"),
            P(None, None, "tensor"),
            P(None, "tensor", None),
            P(),
            P(None, None, "tensor"),
            P(None, "tensor", None),
            P(),
            P(None, "tensor"),
        ),
        check_vma=False,
    )
```

```python
import types

import jax
import jax.numpy as jnp
from jax import lax
from jax.experimental import pallas as pl
from jax.experimental.pallas import tpu as pltpu
from jax.sharding import PartitionSpec as P

HEAD_SIZE = 64
MEMORY_SLOTS = 64
SPAN = 1024
NORM_EPS = 1e-05
GELU = 0.7978845608028654
MESH = pl.DeviceIdType.MESH
F32 = jnp.float32
BF16 = jnp.bfloat16
HALF = SPAN // 2
BLK = 256
WI, WO, F1, F2 = KINDS = range(4)
TO_Y, TO_X, TO_Z, ON_Z, ON_X, TO_C = range(6)
W_RECV = 5
CO, YO, XO, CW, XS, AX, OWN, ZS, AC = range(9)
G_RECV = 8
ITEMS = ((WI, 0), (WI, 1), (WO, 0), (F1, 0), (F2, 0), (F1, 1), (F2, 1))
TILES = ((F2, 0), (F1, 0), (F2, 1), (F1, 1), (WO, 0), (WI, 0), (WI, 1))
FORWARD = (
    (0, 8),
    (),
    (),
    (),
    (1, 16),
    (),
    (9, 24, 17, 32, 2, 3, 10, 11, 25, 40, 18, 19, 4, 33, 48, 12, 5, 41, 56, 13),
    (20, 26, 27, 49, 64),
    (28, 34, 35, 42, 43, 57, 72, 65, 80, 21),
    (50, 51, 36),
    (44, 58, 59, 73, 88, 81, 96, 29, 37),
    (66, 67, 45, 52, 60, 89, 104, 75, 53),
    (74, 97, 82, 83),
    (68,),
    (105, 91, 90),
    (76, 84, 98, 99, 61, 69),
    (106, 107),
    (92, 100, 108, 77),
    (),
    (85, 93),
    (101, 109),
    (),
)
BACKWARD = (
    (224,),
    (0, 16),
    (32, 48),
    (2, 18, 1, 17, 33),
    (34, 50, 3, 19, 49, 225),
    (),
    (64, 66, 8, 35, 51),
    (24, 40, 65),
    (80, 96, 4),
    (5, 56, 20, 81, 97),
    (82, 98, 67, 36, 6),
    (),
    (112, 128, 99, 21, 104, 52),
    (144, 160, 37, 68, 113, 83, 7, 129),
    (114, 130, 22, 145, 161, 100),
    (53, 146, 162, 131),
    (84,),
    (176, 178, 38),
    (69, 101, 136, 115, 147, 23, 54, 177),
    (85, 192, 208, 39, 70),
    (163, 116, 132, 148, 86, 102, 193, 209, 179),
    (194, 210, 55, 71),
    (117, 164),
    (226, 133, 87, 195, 149),
    (103, 180, 118, 211, 165),
    (227, 134, 196, 150, 181),
    (119, 166, 212, 197, 135, 213, 151, 182, 198, 167, 214, 199, 183, 215),
)
X_FIRST = (1, 1, 1, 1, 0, 0, 1, 0, 1, 0, 0, 0, 0, 0)
X_GATHER = (0, 0, 0, 0, 1, 0, 0, 0, 0, 0, 0, 1, 0, 0)


def nn(a, b):
    return lax.dot_general(a, b, (((1,), (0,)), ((), ())), preferred_element_type=F32)


def nt(a, b):
    return lax.dot_general(a, b, (((1,), (1,)), ((), ())), preferred_element_type=F32)


def loop(n, body):
    def step(i, carry):
        body(i)
        return carry

    lax.fori_loop(0, n, step, 0)


def together(n, body, between=None):
    running = [body(i) for i in range(n)]
    for turn, _ in enumerate(zip(*running, strict=True)):
        if between is not None and turn % 5 == 4:
            between()


def make_kernel(layers, dims, n_dp, dp_inside, count):
    width = dims[WI][0]
    heads = dims[WI][1] // (3 * HEAD_SIZE + MEMORY_SLOTS)
    nz = n_dp - 1 if dp_inside else 0
    shards = n_dp if dp_inside else 1
    tiles = 2 * dims[F2][0] // 512
    half_tiles = tiles // 2
    items = [(k, l, t) for l in range(layers) for k, t in ITEMS]
    pieces = [(k, l, t) for l in reversed(range(layers)) for k, t in TILES]

    def tile_size(k):
        return min(dims[k][0], 512)


    def kernel(*refs):
        tok, ag_in, fg_in, cot, *rest = refs
        hbm, (out, ig, *grad), small = rest[:4], rest[4:10], rest[10]
        r = types.SimpleNamespace(**jax.tree.unflatten(layout, rest[11:]))
        s = lax.axis_index("section")
        z = lax.axis_index("dp")
        y = lax.axis_index("tensor")
        c = lax.rem(s, 2)
        x = s // 2
        oc, ox, oy = 1 - c, 1 - x, 1 - y
        dev_core = (x * 2 + oc, z, y)
        dev_x = (ox * 2 + c, z, y)
        dev_y = (s, z, oy)
        dev_cross = (x * 2 + oc, z, oy)

        z0 = lax.rem(z, 2)
        dev_pair = (s, z + 1 - 2 * z0, y)

        def dev_z(k):
            return (s, lax.rem(z + k, n_dp), y)

        barrier = pltpu.get_barrier_semaphore()
        everyone = [dev_core, dev_x, dev_y, dev_cross]
        everyone += [dev_z(k) for k in range(1, nz + 1)] if nz else [dev_pair]
        for d in everyone:
            pl.semaphore_signal(barrier, inc=1, device_id=d, device_id_type=MESH)

        row0 = pl.multiple_of((2 * x + y) * SPAN + c * HALF, HALF)

        def load(i, src, dst):
            return pltpu.make_async_copy(src, dst, r.ld_sem.at[i])

        tok_ld = load(0, tok.at[pl.ds(row0, HALF), :], r.h.at[0])
        cot_ld = load(1, cot.at[pl.ds(row0, HALF), :], r.g)
        ag_ld, fg_ld = load(2, ag_in, r.ag), load(3, fg_in, r.fg)
        ag, fg = r.ag, r.fg
        w_ld = {}
        for l in range(layers):
            for k in KINDS:
                at = 4 + l * 4 + k
                w_ld[k, l] = load(at, hbm[k].at[l], r.v[k].at[l, y])

        tok_ld.start()
        ag_ld.start()
        w_ld[WI, 0].start()
        fg_ld.start()

        def drain(sem, rows):
            some = tok.at[pl.ds(0, rows), :]
            pltpu.make_async_copy(some, some, sem).wait()

        def tile_rows(k, t, start, size):
            first = t * 512 if k == F2 else 0
            return pl.ds(pl.multiple_of(first + start, 16), size)

        def tile_cols(k, t):
            return pl.ds(t * 512 if k in (WI, F1) else 0, 512)

        def w_copy(i, stage):
            k, l, t = items[i]
            rows, cols = tile_size(k) // 8, tile_cols(k, t)

            def eighth(cx, cz, start=0, size=rows):
                return tile_rows(k, t, (4 * cx + 2 * cz + c) * rows + start, size)

            mine, half = eighth(x, z0), rows // 2
            v = r.v[k].at[l]
            span, dev = (
                (mine, dev_y),
                (mine, dev_x),
                (mine, dev_pair),
                (eighth(ox, z0, 0, half), dev_pair),
                (eighth(x, 1 - z0, half, half), dev_x),
                (mine, dev_core),
                (eighth(ox, z0), dev_core),
                (eighth(x, 1 - z0), dev_core),
                (eighth(ox, 1 - z0), dev_core),
            )[stage]
            side = y if stage == TO_Y else oy
            return pltpu.make_async_remote_copy(
                src_ref=hbm[k].at[l, span, cols] if stage == TO_Y else v.at[side, span, cols],
                dst_ref=v.at[side, span, cols],
                send_sem=r.w_send.at[l],
                recv_sem=r.w_recv.at[i * W_RECV + (TO_Y, TO_X, TO_Z, ON_Z, ON_Z, *[ON_X] * 4)[stage]],
                device_id=dev,
                device_id_type=MESH,
            )

        def w_event(i, e):
            rows = tile_size(items[i][0]) // 8
            if e in (1, 2, 3):
                w_copy(i, (TO_Y, TO_X, TO_Z)[e - 1]).wait_recv()
            elif e == 4:
                drain(r.w_recv.at[i * W_RECV + ON_Z], rows)
            elif e == 5:
                drain(r.w_recv.at[i * W_RECV + ON_X], 4 * rows)
            for stage in (
                (TO_Y,),
                (TO_X, TO_Z, TO_C),
                (ON_Z, TO_C + 1),
                (ON_X, TO_C + 2),
                (TO_C + 3,),
                (),
            )[e]:
                w_copy(i, stage).start()

        def w_end():
            for layer in range(layers):
                drain(r.w_send.at[layer], sum(tile_size(k) for k, l, t in items if l == layer))

        forward_plan = iter(FORWARD)

        def weights_here():
            for code in next(forward_plan):
                w_event(code // 8, code % 8)

        pl.semaphore_wait(barrier, len(everyone))
        weights_here()
        for l in range(layers):
            for k in KINDS:
                if (k, l) != (WI, 0):
                    w_ld[k, l].start()
        cot_ld.start()

        tri_s = lax.broadcasted_iota(jnp.int32, (BLK, BLK), 0)
        tri_t = lax.broadcasted_iota(jnp.int32, (BLK, BLK), 1)
        r.tri[...] = jnp.where(tri_s <= tri_t, 1.0, 0.0).astype(BF16)
        r.state_in[2 * layers] = jnp.zeros(r.state_in.shape[1:], BF16)

        def masked(v, on):
            if not on:
                return v.astype(BF16)
            keep = lax.broadcasted_iota(jnp.int32, (BLK, BLK), 0) <= lax.broadcasted_iota(
                jnp.int32, (BLK, BLK), 1
            )
            return jnp.where(keep, v, 0.0).astype(BF16)

        def blocks(tb):
            return [(b, b == tb) for b in range(tb + 1)]

        def state_copy(slot, buf):
            return pltpu.make_async_remote_copy(
                src_ref=r.state_out.at[buf],
                dst_ref=r.state_in.at[slot],
                send_sem=r.st_send.at[slot],
                recv_sem=r.st_recv.at[slot],
                device_id=dev_core,
                device_id_type=MESH,
            )

        def state_send(slot, buf, from_core):
            @pl.when(c == from_core)
            def _():
                state_copy(slot, buf).start()

        def state_recv(slot, buf, from_core):
            @pl.when(c != from_core)
            def _():
                state_copy(slot, buf).wait_recv()

        def state_sent(slot, buf, from_core):
            @pl.when(c == from_core)
            def _():
                state_copy(slot, buf).wait_send()

        def rms(sub, gain):
            h = r.h[sub].astype(F32)
            scale = lax.rsqrt(jnp.mean(h * h, axis=1, keepdims=True) + NORM_EPS)
            return (h * scale * gain).astype(BF16)

        def rms_back(sub, gain, dn, gain_row):
            h = r.h[sub].astype(F32)
            scale = lax.rsqrt(jnp.mean(h * h, axis=1, keepdims=True) + NORM_EPS)
            a = dn * gain
            hs = h * scale
            r.sm[0, pl.ds(gain_row, 1), :] = jnp.sum(dn * hs, axis=0, keepdims=True)
            dh = scale * (a - hs * jnp.mean(hs * a, axis=1, keepdims=True))
            r.g[...] = (r.g[...].astype(F32) + dh).astype(BF16)

        def project(l, half):
            def head(i):
                hd = half * heads + i
                cols = pl.ds(pl.multiple_of(i * 256, 256), 256)
                p = nn(r.nrm[...], r.v[WI][l, half, :, cols])
                yield
                lane = lax.broadcasted_iota(jnp.int32, (HALF, 128), 1)
                hi = p[:, 128:]
                hi = jnp.where(lane >= 64, jnp.exp(hi), hi)
                pb = jnp.concatenate([p[:, :128], hi], axis=1).astype(BF16)
                r.pj[l, hd] = pb
                pt = pb.T
                r.pjT[l, hd] = pt
                yield
                kv = pt[64:192]
                e = pt[192:256]
                buf = r.state_out.at[0]
                buf[i, 0:64, :] = nt(e, kv).astype(BF16)
                buf[i, 64:192, 0:64] = nt(kv, e).astype(BF16)
                buf[i, 192:256, :] = nn(e, jnp.ones((HALF, 128), BF16)).astype(BF16)
                yield

            together(heads, head)

        def attend(l, half, slot, between):
            def head(i):
                hd = half * heads + i
                q = r.pjT[l, hd, 0:64, :]
                v = r.pjT[l, hd, 128:192, :]
                e = r.pjT[l, hd, 192:256, :]
                sk = r.state_in[slot, i, 0:64, 0:64]
                svt = r.state_in[slot, i, 128:192, 0:64]
                before = r.state_in[slot, i, 192:256, 0:1].astype(F32)
                zero = jnp.zeros((64, BLK), BF16)
                log_sum = jnp.zeros((64, 1), F32)
                for tb in range(2):
                    ts = slice(tb * BLK, (tb + 1) * BLK)
                    qt = q[:, ts]
                    rq = jnp.concatenate([zero, qt], axis=0)
                    num = nn(sk, qt)
                    yield
                    for b, on in blocks(tb):
                        bs = slice(b * BLK, (b + 1) * BLK)
                        at = masked(nn(r.pj[l, hd, bs, 0:128], rq), on)
                        yield
                        num = num + nn(e[:, bs], at)
                        yield
                    zt = nn(e[:, ts], r.tri[...]) + before
                    before = zt[:, BLK - 1 : BLK]
                    rz = 1.0 / zt
                    sc = num * rz * 0.125
                    yield
                    ex = jnp.exp(sc - jnp.max(sc, axis=0, keepdims=True))
                    p = ex * (1.0 / jnp.sum(ex, axis=0, keepdims=True))
                    w = (p * rz).astype(BF16)
                    r.rz[l, hd, :, ts] = rz
                    r.pr[l, hd, :, ts] = p.astype(BF16)
                    r.sc[l, hd, :, ts] = sc.astype(BF16)
                    log_sum = log_sum + jnp.sum(jnp.log(zt), axis=1, keepdims=True)
                    rw = jnp.concatenate([zero, w], axis=0)
                    yield
                    o = nn(svt, w)
                    for b, on in blocks(tb):
                        bs = slice(b * BLK, (b + 1) * BLK)
                        gt = masked(nn(r.pj[l, hd, bs, 128:256], rw), on)
                        yield
                        o = o + nn(v[:, bs], gt)
                        yield
                    r.mixT[l, hd, :, ts] = o.astype(BF16)
                r.lm[l, hd] = jnp.broadcast_to(log_sum, (64, 128))
                yield

            together(heads, head, between)

        def attn_out(l):
            mixed = r.mixT[l].reshape(2 * heads * 64, HALF).T
            wo = r.v[WO][l].reshape(2 * dims[WO][0], width)
            r.h[2 * l + 1] = (r.h[2 * l].astype(F32) + nn(mixed, wo)).astype(BF16)

        def tile_of(i, first):
            j = lax.rem(first * half_tiles + i, tiles)
            return j, j // half_tiles, pl.ds(pl.multiple_of(lax.rem(j, half_tiles) * 512, 512), 512)

        def ffn(l, lo, hi):
            def tile(i):
                j, half, at = tile_of(i + lo, y)
                w1 = r.v[F1][l, half, :, at]
                w2 = r.v[F2][l, half, at, :]
                for tb in range(2):
                    ts = slice(tb * BLK, (tb + 1) * BLK)
                    b = nn(r.nrm[ts, :], w1)
                    r.before[l, j, ts, :] = b.astype(BF16)
                    th = jnp.tanh(b * (GELU + (GELU * 0.044715) * (b * b)))
                    act = (0.5 * b * th + 0.5 * b).astype(BF16)
                    r.acc[ts, :] = r.acc[ts, :] + nn(act, w2)

            loop(hi - lo, tile)

        def ffn_back(l, lo, hi):
            def tile(i):
                j, half, at = tile_of(i + lo, oy)
                w1 = r.v[F1][l, half, :, at]
                w2 = r.v[F2][l, half, at, :]
                for tb in range(2):
                    ts = slice(tb * BLK, (tb + 1) * BLK)
                    b = r.before[l, j, ts, :].astype(F32)
                    bb = b * b
                    th = jnp.tanh(b * (GELU + (GELU * 0.044715) * bb))
                    slope = 0.5 + 0.5 * th
                    r.actT[:, ts] = (b * slope).astype(BF16).T
                    slope = slope + (0.5 * b) * (1.0 - th * th) * (GELU + (GELU * 0.134145) * bb)
                    db = (nt(r.g[ts, :], w2) * slope).astype(BF16)
                    r.nrm[ts, :] = db
                    r.acc[ts, :] = r.acc[ts, :] + nt(db, w1)
                r.v[F2][l, half, at, :] = nn(r.actT[...], r.g[...]).astype(BF16)
                r.v[F1][l, half, :, at] = nn(r.nT[...], r.nrm[...]).astype(BF16)

            loop(hi - lo, tile)

        def mixed_back(l):
            wo = r.v[WO][l].reshape(2 * dims[WO][0], width)
            r.nrm[...] = nt(wo, r.g[...]).astype(BF16)

        def attn_out_grad(l):
            mixed = r.mixT[l].reshape(2 * heads * 64, HALF)
            r.v[WO][l] = nn(mixed, r.g[...]).astype(BF16).reshape(r.v[WO].shape[1:])

        def attend_back(l, half, slot):
            def head(i):
                hd = half * heads + i
                q = r.pjT[l, hd, 0:64, :]
                kt = r.pjT[l, hd, 64:128, :]
                e = r.pjT[l, hd, 192:256, :]
                do = r.nrm[pl.ds(pl.multiple_of(hd * 64, 64), 64), :]
                skv = r.state_in[slot, i, 0:64, :]
                skt = r.state_in[slot, i, 64:128, 0:64]
                zero = jnp.zeros((64, BLK), BF16)
                none = jnp.zeros((64, BLK), F32)
                dv, dk, de = [none, none], [none, none], [none, none]
                dzs, dns, ws, dqs = [], [], [], []
                for tb in range(2):
                    ts = slice(tb * BLK, (tb + 1) * BLK)
                    dot, qt = do[:, ts], q[:, ts]
                    rd = jnp.concatenate([dot, zero], axis=0)
                    rz = r.rz[l, hd, :, ts]
                    p = r.pr[l, hd, :, ts].astype(F32)
                    sc = r.sc[l, hd, :, ts].astype(F32)
                    w = p * rz
                    wb = w.astype(BF16)
                    dw = nn(skv, jnp.concatenate([zero, dot], axis=0))
                    dgs = []
                    for b, on in blocks(tb):
                        bs = slice(b * BLK, (b + 1) * BLK)
                        dg = masked(nn(r.pj[l, hd, bs, 128:256], rd), on)
                        yield
                        dw = dw + nn(e[:, bs], dg)
                        dgs.append(dg)
                        yield
                    dp = dw * rz
                    ds = p * (dp - jnp.sum(p * dp, axis=0, keepdims=True))
                    dnb = (ds * rz * 0.125).astype(BF16)
                    dzs.append((-(dw * w + ds * sc) * rz).astype(BF16))
                    dns.append(dnb)
                    ws.append(wb)
                    rw = jnp.concatenate([zero, wb], axis=0)
                    rn = jnp.concatenate([zero, dnb], axis=0)
                    rq = jnp.concatenate([zero, qt], axis=0)
                    yield
                    dq = nn(skt, dnb)
                    for b, on in blocks(tb):
                        bs = slice(b * BLK, (b + 1) * BLK)
                        qk = r.pj[l, hd, bs, 0:128]
                        ve = r.pj[l, hd, bs, 128:256]
                        at = masked(nn(qk, rq), on)
                        yield
                        gt = masked(nn(ve, rw), on)
                        yield
                        da = masked(nn(ve, rn), on)
                        yield
                        dv[b] = dv[b] + nt(dot, gt)
                        de[b] = de[b] + nt(wb, dgs[b]) + nt(dnb, at)
                        dk[b] = dk[b] + nt(qt, da)
                        dq = dq + nn(kt[:, bs], da)
                        yield
                    dqs.append(dq.astype(BF16))
                tri = r.tri[...]
                rev1 = nt(dzs[1], tri)
                rev0 = nt(dzs[0], tri) + rev1[:, 0:1]
                tmp = r.tmp.at[i]
                for b, rev in enumerate((rev0, rev1)):
                    bs = slice(b * BLK, (b + 1) * BLK)
                    tmp[0:64, bs] = dk[b]
                    tmp[64:128, bs] = dv[b]
                    tmp[128:192, bs] = de[b] + rev
                dn_all = jnp.concatenate(dns, axis=1)
                w_all = jnp.concatenate(ws, axis=1)
                buf = r.state_out.at[1]
                buf[i, 0:64, :] = jnp.concatenate([nt(dn_all, q), nt(w_all, do)], axis=1).astype(
                    BF16
                )
                buf[i, 64:128, 0:64] = nt(q, dn_all).astype(BF16)
                buf[i, 128:192, 0:64] = nt(do, w_all).astype(BF16)
                r.pjT[l, hd, 0:64, :] = jnp.concatenate(dqs, axis=1)
                buf[i, 192:256, :] = jnp.broadcast_to(rev0[:, 0:1], (64, 128)).astype(BF16)
                yield

            together(heads, head)

        def project_back(l, half, slot):
            def head(i):
                hd = half * heads + i
                kv = r.pjT[l, hd, 64:192, :]
                e = r.pjT[l, hd, 192:256, :]
                sin = r.state_in.at[slot]
                dkv = r.tmp[i, 0:128, :] + nn(sin[i, 64:192, 0:64], e)
                de = r.tmp[i, 128:192, :] + nn(sin[i, 0:64, :], kv)
                de = (de + sin[i, 192:256, 0:1].astype(F32)) * e.astype(F32)
                r.pjT[l, hd, 64:192, :] = dkv.astype(BF16)
                r.pjT[l, hd, 192:256, :] = de.astype(BF16)
                cols = pl.ds(pl.multiple_of(i * 256, 256), 256)
                dp = r.pjT[l, hd]
                r.acc[...] = r.acc[...] + nn(r.v[WI][l, half, :, cols], dp)
                r.v[WI][l, half, :, cols] = nt(r.nT[...], dp).astype(BF16)

            loop(heads, head)

        def edge_copies(n, forward):
            src = r.edge.at[n] if forward else (r.h.at[2 * layers], r.g)[n]
            dst = (out, ig)[n]
            sequence = 2 * (ox if forward else x) + y
            rows = pl.ds(pl.multiple_of(sequence * SPAN + c * HALF, HALF), HALF)
            first = 0 if forward else x * 256

            def part(start, size=128):
                return src.at[:, pl.ds(pl.multiple_of(start, 128), size)]

            places = [(dev_core, oc), (dev_y, c), (dev_cross, oc)]
            copies = [(part(first + core * 128), dst.at[rows, :], dev) for dev, core in places]
            if not forward:
                copies.append((part(ox * 256, 256), r.edge.at[n], dev_x))
            remote = [
                pltpu.make_async_remote_copy(
                    src_ref=a,
                    dst_ref=b,
                    send_sem=r.o_send.at[0],
                    recv_sem=r.o_recv.at[n if q == 3 else 2],
                    device_id=dev,
                    device_id_type=MESH,
                )
                for q, (a, b, dev) in enumerate(copies)
            ]
            own = pltpu.make_async_copy(part(first + c * 128), dst.at[rows, :], r.o_recv.at[2])
            return remote, own

        def edge_event(n, forward):
            if forward:
                edge_copies(n, False)[0][3].wait_recv()
            remote, own = edge_copies(n, forward)
            for copy in reversed(remote):
                copy.start()
            own.start()

        def edge_end():
            drain(r.o_recv.at[2], 4 * HALF)
            drain(r.o_send.at[0], 4 * HALF)

        to_z = [(ZS, step) for step in range(1, nz + 1)]
        gather = [(OWN, step) for step in range(1, nz + 1)]
        on_z = [(OWN, nz + step) for step in range(1, nz + 1)]

        def g_copy(p, stage, step=0):
            k, l, t = pieces[p]
            rows, cols = tile_size(k) // 2, tile_cols(k, t)
            xr = rows // 2
            zr = xr // shards
            part, full = r.v[k].at[l], grad[k].at[l]
            at = len(pieces) * G_RECV if stage == AC else p * G_RECV + stage
            sems = dict(send_sem=r.g_send.at[p], recv_sem=r.g_recv.at[at])

            def rng(start, size):
                return tile_rows(k, t, start, size)

            shard = rng(c * rows + x * xr + (z * zr if nz else 0), zr)
            head = pl.ds(0, rows)
            if stage == OWN and step == 0:
                return pltpu.make_async_copy(
                    r.fin.at[p, pl.ds(0, zr)], full.at[shard, cols], r.g_recv.at[at]
                )
            x_first, x_gather = X_FIRST[p] == 1, X_GATHER[p] == 1
            cut, low = pl.ds(0, xr), pl.ds(xr, xr)
            if stage == CO:
                src, dev = part.at[oy, rng(oc * rows, rows), cols], dev_core
                dst = r.co.at[p % len(TILES), head]
            elif stage == CW:
                src, dev = part.at[y, rng(oc * rows, rows), cols], dev_core
                dst = r.cw.at[p, head]
            elif stage == XO:
                src, dev = part.at[oy, rng(c * rows + ox * xr, xr), cols], dev_x
                dst = r.yr.at[p, cut]
            elif stage == YO and x_first:
                src, dev = part.at[oy, rng(c * rows + x * xr, xr), cols], dev_y
                dst = r.yr.at[p, low]
            elif stage == YO:
                src, dst, dev = part.at[oy, rng(c * rows, rows), cols], r.yr.at[p, head], dev_y
            elif stage == XS:
                src = part.at[y, rng(c * rows + ox * xr, xr), cols]
                dst, dev = r.xr.at[p, cut], dev_x
            elif stage == AX and x_gather:
                src, dst, dev = r.fin.at[p, pl.ds(0, zr)], full.at[shard, cols], dev_x
            elif stage == AX:
                span = rng(c * rows + x * xr, xr)
                src, dst, dev = full.at[span, cols], full.at[span, cols], dev_x
            elif stage == AC:
                span = rng(c * rows, rows)
                src, dst, dev = full.at[span, cols], full.at[span, cols], dev_core
            elif stage == ZS:
                dev = dev_z(step)
                src = part.at[y, rng(c * rows + x * xr + dev[1] * zr, zr), cols]
                dst = r.zr.at[p, step - 1, pl.ds(0, zr)]
            elif step <= nz:
                dev = dev_z(step)
                src, dst = r.fin.at[p, pl.ds(0, zr)], full.at[shard, cols]
            else:
                dev = dev_z(step - nz)
                span = rng(c * rows + ox * xr + z * zr, zr)
                src, dst = full.at[span, cols], full.at[span, cols]
            return pltpu.make_async_remote_copy(
                src_ref=src, dst_ref=dst, device_id=dev, device_id_type=MESH, **sems
            )

        def add_rows(p, total, half, start, sources, target=None):
            k, l, t = pieces[p]
            cols = tile_cols(k, t)
            cut = min(total, 64)

            def rows_step(i):
                rows = tile_rows(k, t, start + i * cut, cut)
                here = pl.ds(pl.multiple_of(i * cut, 16), cut)
                value = r.v[k][l, half, rows, cols].astype(F32)
                for source in sources:
                    value = value + source[here, :].astype(F32)
                if target is None:
                    r.v[k][l, half, rows, cols] = value.astype(BF16)
                else:
                    target[here, :] = value.astype(BF16)

            loop(total // cut, rows_step)

        def g_event(p, e):
            rows = tile_size(pieces[p][0]) // 2
            xr = rows // 2
            zr = xr // shards
            x_first, x_gather = X_FIRST[p] == 1, X_GATHER[p] == 1
            here = c * rows + x * xr

            def wait(*stages):
                for stage in stages:
                    g_copy(p, stage).wait_recv()

            def start(*stages):
                for stage in stages:
                    g_copy(p, *stage).start() if isinstance(stage, tuple) else g_copy(p, stage).start()

            def wait_rows(stage, count):
                if count:
                    drain(r.g_recv.at[p * G_RECV + stage], count)

            if e == 0:
                start(CO)
            elif e == 1:
                wait(CO)
                add_rows(p, rows, oy, c * rows, [r.co.at[p % len(TILES)]])
                start(XO if x_first else YO)
            elif e == 2:
                start(CW)
            elif e == 3 and x_first:
                wait(CW)
                add_rows(p, rows, y, c * rows, [r.cw.at[p]])
                start(XS)
            elif e == 3:
                wait(CW, YO)
                add_rows(p, rows, y, c * rows, [r.cw.at[p], r.yr.at[p]])
                start(XS)
            elif e == 8:
                wait(XO)
                add_rows(p, xr, oy, here, [r.yr.at[p]])
                start(YO)
            elif e == 4:
                wait(XS)
                sources = [r.xr.at[p]]
                if x_first:
                    wait(YO)
                    sources.append(r.yr.at[p, pl.ds(xr, xr)])
                add_rows(p, xr, y, here, sources)
                start(*to_z)
            elif e == 5:
                wait_rows(ZS, nz * zr)
                sources = [r.zr.at[p, step] for step in range(nz)]
                add_rows(p, zr, y, here + (z * zr if nz else 0), sources, r.fin.at[p])
                start(*([AX] if x_gather else gather))
                start(OWN)
            elif e == 6 and x_gather:
                wait(AX)
                start(*gather, *on_z)
            elif e == 6:
                wait_rows(OWN, zr * (1 + nz))
                start(AX)
            elif e == 7:
                if x_gather:
                    wait_rows(OWN, zr * (1 + 2 * nz))
                else:
                    wait(AX)
                start(AC)

        backward_plan = iter(BACKWARD)

        def gradients_here():
            for code in next(backward_plan):
                p, e = divmod(code, 16)
                if p < len(pieces):
                    g_event(p, e)
                else:
                    edge_event(e // 2, e % 2 == 1)

        def g_end():
            sizes = [tile_size(k) // 2 for k, _, _ in pieces]
            drain(r.g_recv.at[len(pieces) * G_RECV], sum(sizes))
            for p, rows in enumerate(sizes):
                xr = rows // 2
                sent = 3 * rows + xr + (2 * xr if X_FIRST[p] else rows)
                sent += xr // shards * (nz + (2 * nz + 1 if X_GATHER[p] else nz))
                sent += 0 if X_GATHER[p] else xr
                drain(r.g_send.at[p], sent)

        def small_copy(step):
            dev = [dev_core, dev_y, dev_x][step] if step < 3 else dev_z(step - 2)
            return pltpu.make_async_remote_copy(
                src_ref=r.sm.at[min(step, 3)],
                dst_ref=r.smr.at[step],
                send_sem=r.s_send.at[step],
                recv_sem=r.s_recv.at[step],
                device_id=dev,
                device_id_type=MESH,
            )

        def small_sum(step):
            if step < 3:
                small_copy(step).wait_recv()
                r.sm[step + 1] = r.sm[step] + r.smr[step]
            else:
                total = r.sm[3]
                for k in range(nz):
                    small_copy(3 + k).wait_recv()
                    total = total + r.smr[3 + k]
                own = heads * MEMORY_SLOTS
                mass = jnp.where(y == 0, total[2 * layers : 3 * layers, :own], total[2 * layers : 3 * layers, own:])
                r.total[...] = total
                r.total[2 * layers : 3 * layers, :own] = mass * (1.0 / count)
                small_out().start()

        def small_out():
            return load(4 + 4 * layers, r.total, small)

        tok_ld.wait()
        ag_ld.wait()
        fg_ld.wait()
        r.sm[0] = jnp.zeros(r.sm.shape[1:], F32)
        for l in range(layers):
            r.nrm[...] = rms(2 * l, ag[pl.ds(l, 1), :])
            weights_here()
            for turn in range(2):
                half = y if turn == 0 else oy
                slot = 2 * l + turn
                use = jnp.where(c == 1, slot, 2 * layers)
                if turn == 0:
                    w_ld[WI, l].wait()
                if slot:
                    state_sent(slot - 1, 0, 0)
                project(l, half)
                state_send(slot, 0, 0)
                weights_here()
                state_recv(slot, 0, 0)
                attend(l, half, use, weights_here if slot == 0 else None)
                weights_here()
            w_ld[WO, l].wait()
            attn_out(l)
            r.nrm[...] = rms(2 * l + 1, fg[pl.ds(l, 1), :])
            weights_here()
            w_ld[F1, l].wait()
            w_ld[F2, l].wait()
            r.acc[...] = r.h[2 * l + 1].astype(F32)
            ffn(l, 0, half_tiles)
            weights_here()
            for tile in range(half_tiles, tiles):
                ffn(l, tile, tile + 1)
                weights_here()
            r.h[2 * l + 2] = r.acc[...].astype(BF16)
        gradients_here()
        w_end()
        state_sent(2 * layers - 1, 0, 0)
        cot_ld.wait()
        for l in range(layers):
            lm = r.lm[l].reshape(2 * heads * 64, 128).T
            r.sm[0, pl.ds(2 * layers + l, 1), :] = lm[0:1, :]

        for l in reversed(range(layers)):
            r.nT[...] = rms(2 * l + 1, fg[pl.ds(l, 1), :]).T
            r.acc[...] = jnp.zeros(r.acc.shape, F32)
            for tile in range(tiles):
                ffn_back(l, tile, tile + 1)
                gradients_here()
            rms_back(2 * l + 1, fg[pl.ds(l, 1), :], r.acc[...], layers + l)
            gradients_here()
            mixed_back(l)
            attn_out_grad(l)
            gradients_here()
            r.nT[...] = rms(2 * l, ag[pl.ds(l, 1), :]).T
            r.acc[...] = jnp.zeros(r.acc.shape, F32)
            for turn in range(2):
                half = oy if turn == 0 else y
                fwd_slot = jnp.where(c == 1, 2 * l + 1 - turn, 2 * layers)
                slot = 2 * l + turn
                use = jnp.where(c == 0, slot, 2 * layers)
                if not (turn == 0 and l == layers - 1):
                    prev = 2 * l if turn == 1 else 2 * (l + 1) + 1
                    state_sent(prev, 1, 1)
                attend_back(l, half, fwd_slot)
                state_send(slot, 1, 1)
                gradients_here()
                state_recv(slot, 1, 1)
                project_back(l, half, use)
                gradients_here()
            rms_back(2 * l, ag[pl.ds(l, 1), :], r.acc[...].T, l)
            if l == 0:
                small_copy(0).start()
            gradients_here()
        state_sent(1, 1, 1)
        for step in range(4):
            small_sum(step)
            if step < 2:
                small_copy(step + 1).start()
            elif step == 2:
                for k in range(nz):
                    small_copy(3 + k).start()
            gradients_here()
        for step in range(3 + nz):
            small_copy(step).wait_send()
        small_out().wait()
        g_end()
        edge_end()

    L = layers
    nzb = max(nz, 1)
    scratch = dict(
        v=[pltpu.VMEM((L, 2, *dims[k]), BF16) for k in KINDS],
        h=pltpu.VMEM((2 * L + 1, HALF, width), BF16),
        nT=pltpu.VMEM((width, HALF), BF16),
        nrm=pltpu.VMEM((HALF, width), BF16),
        ag=pltpu.VMEM((L, width), F32),
        fg=pltpu.VMEM((L, width), F32),
        total=pltpu.VMEM((8, width), F32),
        g=pltpu.VMEM((HALF, width), BF16),
        pj=pltpu.VMEM((L, 2 * heads, HALF, 256), BF16),
        pjT=pltpu.VMEM((L, 2 * heads, 256, HALF), BF16),
        rz=pltpu.VMEM((L, 2 * heads, 64, HALF), F32),
        pr=pltpu.VMEM((L, 2 * heads, 64, HALF), BF16),
        sc=pltpu.VMEM((L, 2 * heads, 64, HALF), BF16),
        mixT=pltpu.VMEM((L, 2 * heads, 64, HALF), BF16),
        lm=pltpu.VMEM((L, 2 * heads, 64, 128), F32),
        before=pltpu.VMEM((L, tiles, HALF, 512), BF16),
        actT=pltpu.VMEM((512, HALF), BF16),
        acc=pltpu.VMEM((HALF, width), F32),
        tmp=pltpu.VMEM((heads, 192, HALF), F32),
        tri=pltpu.VMEM((BLK, BLK), BF16),
        state_out=pltpu.VMEM((2, heads, 256, 128), BF16),
        state_in=pltpu.VMEM((2 * L + 1, heads, 256, 128), BF16),
        sm=pltpu.VMEM((4, 8, width), F32),
        smr=pltpu.VMEM((3 + nzb, 8, width), F32),
        co=pltpu.VMEM((len(TILES), 256, 512), BF16),
        cw=pltpu.VMEM((len(pieces), 256, 512), BF16),
        edge=pltpu.VMEM((2, HALF, 256), BF16),
        yr=pltpu.VMEM((len(pieces), 256, 512), BF16),
        xr=pltpu.VMEM((len(pieces), 128, 512), BF16),
        zr=pltpu.VMEM((len(pieces), nzb, 128 // shards, 512), BF16),
        fin=pltpu.VMEM((len(pieces), 128 // shards, 512), BF16),
        ld_sem=pltpu.SemaphoreType.DMA((5 + 4 * L,)),
        w_send=pltpu.SemaphoreType.DMA((L,)),
        w_recv=pltpu.SemaphoreType.DMA((W_RECV * len(items),)),
        st_send=pltpu.SemaphoreType.DMA((2 * L,)),
        st_recv=pltpu.SemaphoreType.DMA((2 * L,)),
        o_send=pltpu.SemaphoreType.DMA((1,)),
        o_recv=pltpu.SemaphoreType.DMA((3,)),
        g_send=pltpu.SemaphoreType.DMA((len(pieces),)),
        g_recv=pltpu.SemaphoreType.DMA((len(pieces) * G_RECV + 1,)),
        s_send=pltpu.SemaphoreType.DMA((3 + nzb,)),
        s_recv=pltpu.SemaphoreType.DMA((3 + nzb,)),
    )
    flat, layout = jax.tree.flatten(scratch)
    return kernel, flat


def finish(layers, width, out, ig, small, grads):
    steps = 2 * layers
    own = width // 2

    def kernel(out_in, ig_in, small_in, wi, wo, f1, f2, *results):
        out_to, ig_to, wi_to, wo_to, ag_to, f1_to, f2_to, fg_to, mass_to = results
        out_to[...] = out_in[...]
        ig_to[...] = ig_in[...]
        for source, target in ((wi, wi_to), (wo, wo_to), (f1, f1_to), (f2, f2_to)):
            target[...] = source[...].astype(F32)
        ag_to[...] = small_in[0:layers, :]
        fg_to[...] = small_in[layers : 2 * layers, :]
        mass_to[...] = small_in[2 * layers : 3 * layers, :own]

    edge = pl.BlockSpec((out.shape[0] // steps, out.shape[1]), lambda i: (i, 0))

    def part(v):
        return pl.BlockSpec((1, v.shape[1] // 2, v.shape[2]), lambda i: (i // 2, i % 2, 0))

    def whole(*shape):
        return pl.BlockSpec(shape, lambda i: (0, 0))

    like = [jax.ShapeDtypeStruct(v.shape, F32) for v in grads]
    gain = jax.ShapeDtypeStruct((layers, width), F32)
    mass = jax.ShapeDtypeStruct((layers, own), F32)
    edges = [jax.ShapeDtypeStruct(out.shape, BF16)] * 2
    gain_spec, mass_spec = whole(layers, width), whole(layers, own)
    parts = [part(v) for v in grads]
    return pl.pallas_call(
        kernel,
        grid=(steps,),
        in_specs=[edge, edge, whole(*small.shape), *parts],
        out_specs=[edge, edge, *parts[:2], gain_spec, *parts[2:], gain_spec, mass_spec],
        out_shape=[*edges, *like[:2], gain, *like[2:], gain, mass],
        compiler_params=pltpu.CompilerParams(vmem_limit_bytes=60 * 1024 * 1024),
    )(out, ig, small, *grads)


def solution(mesh):
    n_dp = mesh.shape["dp"]
    dp_inside = n_dp in (2, 4)

    def local(tokens, attn_gain, w_in, w_out, ffn_gain, ffn_in, ffn_out, cotangent):
        layers, width = attn_gain.shape
        arrays = (w_in, w_out, ffn_in, ffn_out)
        dims = [v.shape[1:] for v in arrays]
        kernel, scratch = make_kernel(
            layers, dims, n_dp, dp_inside, tokens.shape[0] * n_dp
        )
        anyspace = pl.BlockSpec(memory_space=pl.ANY)
        vmem = pl.BlockSpec(memory_space=pltpu.VMEM)
        edge = jax.ShapeDtypeStruct((tokens.shape[0], width // 4), BF16)
        results = pl.pallas_call(
            kernel,
            out_shape=[edge, edge]
            + [jax.ShapeDtypeStruct(v.shape, BF16) for v in arrays]
            + [jax.ShapeDtypeStruct((8, width), F32)],
            in_specs=[anyspace] * 8,
            out_specs=[anyspace] * 7,
            scratch_shapes=scratch,
            compiler_params=pltpu.CompilerParams(
                collective_id=0, has_side_effects=True, vmem_limit_bytes=63 * 1024 * 1024
            ),
        )(tokens, attn_gain, ffn_gain, cotangent, *arrays)
        out, ig, *grads, small = results
        if not dp_inside and n_dp > 1:
            grads = [lax.psum(v, "dp") for v in grads]
            small = lax.psum(small, "dp")
        return finish(layers, width, out, ig, small, grads)

    placed = (
        P("dp", None),
        P(),
        P(None, None, "tensor"),
        P(None, "tensor", None),
        P(),
        P(None, None, "tensor"),
        P(None, "tensor", None),
        P("dp", None),
    )
    return jax.shard_map(
        local,
        mesh=mesh,
        in_specs=placed,
        out_specs=(
            P("dp", "section"),
            P("dp", "section"),
            P(None, None, "tensor"),
            P(None, "tensor", None),
            P(),
            P(None, None, "tensor"),
            P(None, "tensor", None),
            P(),
            P(None, "tensor"),
        ),
        check_vma=False,
    )
```

```python
import types

import jax
import jax.numpy as jnp
from jax import lax
from jax.experimental import pallas as pl
from jax.experimental.pallas import tpu as pltpu
from jax.sharding import PartitionSpec as P

HEAD_SIZE = 64
MEMORY_SLOTS = 64
SPAN = 1024
NORM_EPS = 1e-05
GELU = 0.7978845608028654
MESH = pl.DeviceIdType.MESH
F32 = jnp.float32
BF16 = jnp.bfloat16
HALF = SPAN // 2
BLK = 256
WI, WO, F1, F2 = KINDS = range(4)
TO_Y, TO_X, TO_Z, ON_Z, ON_X, TO_C = range(6)
W_RECV = 5
CO, YO, XO, CW, XS, AX, OWN, ZS, AC = range(9)
G_RECV = 8
ITEMS = (
    (WI, 0, 0, 1, 0),
    (WI, 0, 1, 1, 0),
    (WO, 0, 0, 1, 0),
    (F1, 0, 0, 1, 0),
    (F2, 0, 0, 1, 0),
    (F1, 0, 1, 1, 0),
    (F2, 0, 1, 1, 0),
    (WI, 1, 0, 1, 0),
    (WI, 1, 1, 1, 0),
    (WO, 1, 0, 1, 1),
    (F1, 1, 0, 2, 0),
    (F2, 1, 0, 2, 1),
)
TILES = ((F2, 0), (F1, 0), (F2, 1), (F1, 1), (WO, 0), (WI, 0), (WI, 1))
FORWARD = (
    (0, 8, 16, 24, 32, 40, 48, 56, 64, 72, 80, 88),
    (),
    (),
    (1,),
    (),
    (9,),
    (17, 2, 3, 25, 10, 11, 33, 18, 19, 4, 41, 5, 26, 27, 49, 12, 57, 13),
    (20, 34, 35, 65),
    (28, 42, 43, 50, 51, 73, 21),
    (58, 59),
    (36, 66, 44, 67, 81, 29, 52, 37),
    (60, 68, 45, 53),
    (),
    (),
    (83, 82),
    (61, 69),
    (84,),
    (89, 77),
    (),
    (85, 93),
    (),
    (),
)
BACKWARD = (
    (224,),
    (0, 16),
    (32, 48),
    (2, 1, 18, 17, 33),
    (3, 34, 19, 50, 49, 225),
    (),
    (8, 64, 35, 66),
    (40, 24, 51, 65),
    (80, 96, 4),
    (5, 56, 81, 20, 97),
    (36, 82, 98, 67, 6),
    (),
    (83, 88, 128, 21, 112, 52),
    (144, 160, 37, 68, 129, 99, 7, 113),
    (145, 22, 130, 114, 161, 84),
    (146, 162, 53),
    (100, 115),
    (38, 176, 178),
    (23, 85, 131, 147, 69, 120, 54, 177),
    (39, 192, 101, 208),
    (193, 148, 86, 163, 70, 132, 102, 209, 116, 179),
    (194, 149, 55, 210, 87),
    (),
    (195, 226, 133, 164, 71, 117),
    (103, 211, 150, 180, 134, 196),
    (165, 118, 227, 181, 212, 197),
    (182, 151, 213, 135, 166, 198, 119, 183, 214, 199, 215, 167),
)
X_FIRST = (1, 1, 1, 1, 0, 1, 0, 1, 0, 0, 0, 0, 0, 0)
X_GATHER = (0, 0, 0, 0, 0, 0, 0, 0, 0, 0, 1, 0, 0, 0)


def nn(a, b):
    return lax.dot_general(a, b, (((1,), (0,)), ((), ())), preferred_element_type=F32)


def nt(a, b):
    return lax.dot_general(a, b, (((1,), (1,)), ((), ())), preferred_element_type=F32)


def loop(n, body):
    def step(i, carry):
        body(i)
        return carry

    lax.fori_loop(0, n, step, 0)


def together(n, body, between=None):
    running = [body(i) for i in range(n)]
    for turn, _ in enumerate(zip(*running, strict=True)):
        if between is not None and turn % 5 == 4:
            between()


def make_kernel(layers, dims, n_dp, dp_inside, count):
    width = dims[WI][0]
    heads = dims[WI][1] // (3 * HEAD_SIZE + MEMORY_SLOTS)
    nz = n_dp - 1 if dp_inside else 0
    shards = n_dp if dp_inside else 1
    tiles = 2 * dims[F2][0] // 512
    half_tiles = tiles // 2
    pieces = [(k, l, t) for l in reversed(range(layers)) for k, t in TILES]

    def tile_size(k):
        return min(dims[k][0], 512)


    def kernel(*refs):
        tok, ag_in, fg_in, cot, *rest = refs
        hbm, (out, ig, *grad), small = rest[:4], rest[4:10], rest[10]
        r = types.SimpleNamespace(**jax.tree.unflatten(layout, rest[11:]))
        s = lax.axis_index("section")
        z = lax.axis_index("dp")
        y = lax.axis_index("tensor")
        c = lax.rem(s, 2)
        x = s // 2
        oc, ox, oy = 1 - c, 1 - x, 1 - y
        dev_core = (x * 2 + oc, z, y)
        dev_x = (ox * 2 + c, z, y)
        dev_y = (s, z, oy)
        dev_cross = (x * 2 + oc, z, oy)

        z0 = lax.rem(z, 2)
        dev_pair = (s, z + 1 - 2 * z0, y)

        def dev_z(k):
            return (s, lax.rem(z + k, n_dp), y)

        barrier = pltpu.get_barrier_semaphore()
        everyone = [dev_core, dev_x, dev_y, dev_cross]
        everyone += [dev_z(k) for k in range(1, nz + 1)] if nz else [dev_pair]
        for d in everyone:
            pl.semaphore_signal(barrier, inc=1, device_id=d, device_id_type=MESH)

        row0 = pl.multiple_of((2 * x + y) * SPAN + c * HALF, HALF)

        def load(i, src, dst):
            return pltpu.make_async_copy(src, dst, r.ld_sem.at[i])

        tok_ld = load(0, tok.at[pl.ds(row0, HALF), :], r.h.at[0])
        cot_ld = load(1, cot.at[pl.ds(row0, HALF), :], r.g)
        ag_ld, fg_ld = load(2, ag_in, r.ag), load(3, fg_in, r.fg)
        ag, fg = r.ag, r.fg
        w_ld = {}
        for l in range(layers):
            for k in KINDS:
                at = 4 + l * 4 + k
                w_ld[k, l] = load(at, hbm[k].at[l], r.v[k].at[l, y])

        tok_ld.start()
        ag_ld.start()
        w_ld[WI, 0].start()
        fg_ld.start()

        def drain(sem, rows):
            some = tok.at[pl.ds(0, rows), :]
            pltpu.make_async_copy(some, some, sem).wait()

        def tile_rows(k, t, start, size):
            first = t * 512 if k == F2 else 0
            return pl.ds(pl.multiple_of(first + start, 16), size)

        def tile_cols(k, t, n=1):
            return pl.ds(t * 512, n * 512) if k in (WI, F1) else pl.ds(0, 512)

        def w_copy(i, stage):
            k, l, t, n, straight = ITEMS[i]
            total = tile_size(k) * (n if k == F2 else 1)
            rows, cols = total // 8, tile_cols(k, t, n)

            def eighth(cx, cz, start=0, size=rows):
                return tile_rows(k, t, (4 * cx + 2 * cz + c) * rows + start, size)

            mine, half = eighth(x, z0), rows // 2
            if straight:
                mine = tile_rows(k, t, c * (total // 2), total // 2)
            v = r.v[k].at[l]
            span, dev = (
                (mine, dev_y),
                (mine, dev_x),
                (mine, dev_pair),
                (eighth(ox, z0, 0, half), dev_pair),
                (eighth(x, 1 - z0, half, half), dev_x),
                (mine, dev_core),
                (eighth(ox, z0), dev_core),
                (eighth(x, 1 - z0), dev_core),
                (eighth(ox, 1 - z0), dev_core),
            )[stage]
            side = y if stage == TO_Y else oy
            return pltpu.make_async_remote_copy(
                src_ref=hbm[k].at[l, span, cols] if stage == TO_Y else v.at[side, span, cols],
                dst_ref=v.at[side, span, cols],
                send_sem=r.w_send.at[l],
                recv_sem=r.w_recv.at[i * W_RECV + (TO_Y, TO_X, TO_Z, ON_Z, ON_Z, *[ON_X] * 4)[stage]],
                device_id=dev,
                device_id_type=MESH,
            )

        def w_event(i, e):
            k, _, _, n, straight = ITEMS[i]
            rows = tile_size(k) * n // 8
            if e in (1, 2, 3):
                w_copy(i, (TO_Y, TO_X, TO_Z)[e - 1]).wait_recv()
            elif e == 4:
                drain(r.w_recv.at[i * W_RECV + ON_Z], rows)
            elif e == 5:
                drain(r.w_recv.at[i * W_RECV + ON_X], 4 * rows)
            starts = (
                (TO_Y,),
                (TO_C,) if straight else (TO_X, TO_Z, TO_C),
                (ON_Z, TO_C + 1),
                (ON_X, TO_C + 2),
                (TO_C + 3,),
                (),
            )[e]
            for stage in starts:
                w_copy(i, stage).start()

        def w_end():
            for layer in range(layers):
                sent = [tile_size(k) * n for k, l, _, n, _ in ITEMS if l == layer]
                drain(r.w_send.at[layer], sum(sent))

        forward_plan = iter(FORWARD)

        def weights_here():
            for code in next(forward_plan):
                w_event(code // 8, code % 8)

        pl.semaphore_wait(barrier, len(everyone))
        weights_here()
        for l in range(layers):
            for k in KINDS:
                if (k, l) != (WI, 0):
                    w_ld[k, l].start()
        cot_ld.start()

        tri_s = lax.broadcasted_iota(jnp.int32, (BLK, BLK), 0)
        tri_t = lax.broadcasted_iota(jnp.int32, (BLK, BLK), 1)
        r.tri[...] = jnp.where(tri_s <= tri_t, 1.0, 0.0).astype(BF16)
        r.state_in[2 * layers] = jnp.zeros(r.state_in.shape[1:], BF16)

        def masked(v, on):
            if not on:
                return v.astype(BF16)
            keep = lax.broadcasted_iota(jnp.int32, (BLK, BLK), 0) <= lax.broadcasted_iota(
                jnp.int32, (BLK, BLK), 1
            )
            return jnp.where(keep, v, 0.0).astype(BF16)

        def blocks(tb):
            return [(b, b == tb) for b in range(tb + 1)]

        def state_copy(slot, buf):
            return pltpu.make_async_remote_copy(
                src_ref=r.state_out.at[buf],
                dst_ref=r.state_in.at[slot],
                send_sem=r.st_send.at[slot],
                recv_sem=r.st_recv.at[slot],
                device_id=dev_core,
                device_id_type=MESH,
            )

        def state_send(slot, buf, from_core):
            @pl.when(c == from_core)
            def _():
                state_copy(slot, buf).start()

        def state_recv(slot, buf, from_core):
            @pl.when(c != from_core)
            def _():
                state_copy(slot, buf).wait_recv()

        def state_sent(slot, buf, from_core):
            @pl.when(c == from_core)
            def _():
                state_copy(slot, buf).wait_send()

        def rms(sub, gain):
            h = r.h[sub].astype(F32)
            scale = lax.rsqrt(jnp.mean(h * h, axis=1, keepdims=True) + NORM_EPS)
            return (h * scale * gain).astype(BF16)

        def rms_back(sub, gain, dn, gain_row):
            h = r.h[sub].astype(F32)
            scale = lax.rsqrt(jnp.mean(h * h, axis=1, keepdims=True) + NORM_EPS)
            a = dn * gain
            hs = h * scale
            r.sm[0, pl.ds(gain_row, 1), :] = jnp.sum(dn * hs, axis=0, keepdims=True)
            dh = scale * (a - hs * jnp.mean(hs * a, axis=1, keepdims=True))
            r.g[...] = (r.g[...].astype(F32) + dh).astype(BF16)

        def project(l, half):
            def head(i):
                hd = half * heads + i
                cols = pl.ds(pl.multiple_of(i * 256, 256), 256)
                p = nn(r.nrm[...], r.v[WI][l, half, :, cols])
                yield
                lane = lax.broadcasted_iota(jnp.int32, (HALF, 128), 1)
                hi = p[:, 128:]
                hi = jnp.where(lane >= 64, jnp.exp(hi), hi)
                pb = jnp.concatenate([p[:, :128], hi], axis=1).astype(BF16)
                r.pj[l, hd] = pb
                pt = pb.T
                r.pjT[l, hd] = pt
                yield
                kv = pt[64:192]
                e = pt[192:256]
                buf = r.state_out.at[0]
                buf[i, 0:64, :] = nt(e, kv).astype(BF16)
                buf[i, 64:192, 0:64] = nt(kv, e).astype(BF16)
                buf[i, 192:256, :] = nn(e, jnp.ones((HALF, 128), BF16)).astype(BF16)
                yield

            together(heads, head)

        def attend(l, half, slot, between):
            def head(i):
                hd = half * heads + i
                q = r.pjT[l, hd, 0:64, :]
                v = r.pjT[l, hd, 128:192, :]
                e = r.pjT[l, hd, 192:256, :]
                sk = r.state_in[slot, i, 0:64, 0:64]
                svt = r.state_in[slot, i, 128:192, 0:64]
                before = r.state_in[slot, i, 192:256, 0:1].astype(F32)
                zero = jnp.zeros((64, BLK), BF16)
                log_sum = jnp.zeros((64, 1), F32)
                for tb in range(2):
                    ts = slice(tb * BLK, (tb + 1) * BLK)
                    qt = q[:, ts]
                    rq = jnp.concatenate([zero, qt], axis=0)
                    num = nn(sk, qt)
                    yield
                    for b, on in blocks(tb):
                        bs = slice(b * BLK, (b + 1) * BLK)
                        at = masked(nn(r.pj[l, hd, bs, 0:128], rq), on)
                        yield
                        num = num + nn(e[:, bs], at)
                        yield
                    zt = nn(e[:, ts], r.tri[...]) + before
                    before = zt[:, BLK - 1 : BLK]
                    rz = 1.0 / zt
                    sc = num * rz * 0.125
                    yield
                    ex = jnp.exp(sc - jnp.max(sc, axis=0, keepdims=True))
                    p = ex * (1.0 / jnp.sum(ex, axis=0, keepdims=True))
                    w = (p * rz).astype(BF16)
                    r.rz[l, hd, :, ts] = rz
                    r.pr[l, hd, :, ts] = p.astype(BF16)
                    r.sc[l, hd, :, ts] = sc.astype(BF16)
                    log_sum = log_sum + jnp.sum(jnp.log(zt), axis=1, keepdims=True)
                    rw = jnp.concatenate([zero, w], axis=0)
                    yield
                    o = nn(svt, w)
                    for b, on in blocks(tb):
                        bs = slice(b * BLK, (b + 1) * BLK)
                        gt = masked(nn(r.pj[l, hd, bs, 128:256], rw), on)
                        yield
                        o = o + nn(v[:, bs], gt)
                        yield
                    r.mixT[l, hd, :, ts] = o.astype(BF16)
                r.lm[l, hd] = jnp.broadcast_to(log_sum, (64, 128))
                yield

            together(heads, head, between)

        def attn_out(l):
            mixed = r.mixT[l].reshape(2 * heads * 64, HALF).T
            wo = r.v[WO][l].reshape(2 * dims[WO][0], width)
            r.h[2 * l + 1] = (r.h[2 * l].astype(F32) + nn(mixed, wo)).astype(BF16)

        def tile_of(i, first):
            j = lax.rem(first * half_tiles + i, tiles)
            return j, j // half_tiles, pl.ds(pl.multiple_of(lax.rem(j, half_tiles) * 512, 512), 512)

        def ffn(l, lo, hi):
            def part(i):
                j, half, at = tile_of(i // 2 + lo, y)
                ts = slice(i % 2 * BLK, (i % 2 + 1) * BLK)
                b = nn(r.nrm[ts, :], r.v[F1][l, half, :, at])
                yield
                r.before[l, j, ts, :] = b.astype(BF16)
                th = jnp.tanh(b * (GELU + (GELU * 0.044715) * (b * b)))
                act = (0.5 * b * th + 0.5 * b).astype(BF16)
                yield
                r.acc[ts, :] = r.acc[ts, :] + nn(act, r.v[F2][l, half, at, :])
                yield

            together(2 * (hi - lo), part)

        def ffn_back(l, lo, hi):
            def tile(i):
                j, half, at = tile_of(i + lo, oy)
                w1 = r.v[F1][l, half, :, at]
                w2 = r.v[F2][l, half, at, :]
                for tb in range(2):
                    ts = slice(tb * BLK, (tb + 1) * BLK)
                    b = r.before[l, j, ts, :].astype(F32)
                    bb = b * b
                    th = jnp.tanh(b * (GELU + (GELU * 0.044715) * bb))
                    slope = 0.5 + 0.5 * th
                    r.actT[:, ts] = (b * slope).astype(BF16).T
                    slope = slope + (0.5 * b) * (1.0 - th * th) * (GELU + (GELU * 0.134145) * bb)
                    db = (nt(r.g[ts, :], w2) * slope).astype(BF16)
                    r.nrm[ts, :] = db
                    r.acc[ts, :] = r.acc[ts, :] + nt(db, w1)
                r.v[F2][l, half, at, :] = nn(r.actT[...], r.g[...]).astype(BF16)
                r.v[F1][l, half, :, at] = nn(r.nT[...], r.nrm[...]).astype(BF16)

            loop(hi - lo, tile)

        def mixed_back(l):
            wo = r.v[WO][l].reshape(2 * dims[WO][0], width)
            r.nrm[...] = nt(wo, r.g[...]).astype(BF16)

        def attn_out_grad(l):
            mixed = r.mixT[l].reshape(2 * heads * 64, HALF)
            r.v[WO][l] = nn(mixed, r.g[...]).astype(BF16).reshape(r.v[WO].shape[1:])

        def attend_back(l, half, slot):
            def head(i):
                hd = half * heads + i
                q = r.pjT[l, hd, 0:64, :]
                kt = r.pjT[l, hd, 64:128, :]
                e = r.pjT[l, hd, 192:256, :]
                do = r.nrm[pl.ds(pl.multiple_of(hd * 64, 64), 64), :]
                skv = r.state_in[slot, i, 0:64, :]
                skt = r.state_in[slot, i, 64:128, 0:64]
                zero = jnp.zeros((64, BLK), BF16)
                none = jnp.zeros((64, BLK), F32)
                dv, dk, de = [none, none], [none, none], [none, none]
                dzs, dns, ws, dqs = [], [], [], []
                for tb in range(2):
                    ts = slice(tb * BLK, (tb + 1) * BLK)
                    dot, qt = do[:, ts], q[:, ts]
                    rd = jnp.concatenate([dot, zero], axis=0)
                    rz = r.rz[l, hd, :, ts]
                    p = r.pr[l, hd, :, ts].astype(F32)
                    sc = r.sc[l, hd, :, ts].astype(F32)
                    w = p * rz
                    wb = w.astype(BF16)
                    dw = nn(skv, jnp.concatenate([zero, dot], axis=0))
                    dgs = []
                    for b, on in blocks(tb):
                        bs = slice(b * BLK, (b + 1) * BLK)
                        dg = masked(nn(r.pj[l, hd, bs, 128:256], rd), on)
                        yield
                        dw = dw + nn(e[:, bs], dg)
                        dgs.append(dg)
                        yield
                    dp = dw * rz
                    ds = p * (dp - jnp.sum(p * dp, axis=0, keepdims=True))
                    dnb = (ds * rz * 0.125).astype(BF16)
                    dzs.append((-(dw * w + ds * sc) * rz).astype(BF16))
                    dns.append(dnb)
                    ws.append(wb)
                    rw = jnp.concatenate([zero, wb], axis=0)
                    rn = jnp.concatenate([zero, dnb], axis=0)
                    rq = jnp.concatenate([zero, qt], axis=0)
                    yield
                    dq = nn(skt, dnb)
                    for b, on in blocks(tb):
                        bs = slice(b * BLK, (b + 1) * BLK)
                        qk = r.pj[l, hd, bs, 0:128]
                        ve = r.pj[l, hd, bs, 128:256]
                        at = masked(nn(qk, rq), on)
                        yield
                        gt = masked(nn(ve, rw), on)
                        yield
                        da = masked(nn(ve, rn), on)
                        yield
                        dv[b] = dv[b] + nt(dot, gt)
                        de[b] = de[b] + nt(wb, dgs[b]) + nt(dnb, at)
                        dk[b] = dk[b] + nt(qt, da)
                        dq = dq + nn(kt[:, bs], da)
                        yield
                    dqs.append(dq.astype(BF16))
                tri = r.tri[...]
                rev1 = nt(dzs[1], tri)
                rev0 = nt(dzs[0], tri) + rev1[:, 0:1]
                tmp = r.tmp.at[i]
                for b, rev in enumerate((rev0, rev1)):
                    bs = slice(b * BLK, (b + 1) * BLK)
                    tmp[0:64, bs] = dk[b]
                    tmp[64:128, bs] = dv[b]
                    tmp[128:192, bs] = de[b] + rev
                dn_all = jnp.concatenate(dns, axis=1)
                w_all = jnp.concatenate(ws, axis=1)
                buf = r.state_out.at[1]
                buf[i, 0:64, :] = jnp.concatenate([nt(dn_all, q), nt(w_all, do)], axis=1).astype(
                    BF16
                )
                buf[i, 64:128, 0:64] = nt(q, dn_all).astype(BF16)
                buf[i, 128:192, 0:64] = nt(do, w_all).astype(BF16)
                r.pjT[l, hd, 0:64, :] = jnp.concatenate(dqs, axis=1)
                buf[i, 192:256, :] = jnp.broadcast_to(rev0[:, 0:1], (64, 128)).astype(BF16)
                yield

            together(heads, head)

        def project_back(l, half, slot):
            def head(i):
                hd = half * heads + i
                kv = r.pjT[l, hd, 64:192, :]
                e = r.pjT[l, hd, 192:256, :]
                sin = r.state_in.at[slot]
                dkv = r.tmp[i, 0:128, :] + nn(sin[i, 64:192, 0:64], e)
                de = r.tmp[i, 128:192, :] + nn(sin[i, 0:64, :], kv)
                de = (de + sin[i, 192:256, 0:1].astype(F32)) * e.astype(F32)
                r.pjT[l, hd, 64:192, :] = dkv.astype(BF16)
                r.pjT[l, hd, 192:256, :] = de.astype(BF16)
                cols = pl.ds(pl.multiple_of(i * 256, 256), 256)
                dp = r.pjT[l, hd]
                r.acc[...] = r.acc[...] + nn(r.v[WI][l, half, :, cols], dp)
                r.v[WI][l, half, :, cols] = nt(r.nT[...], dp).astype(BF16)

            loop(heads, head)

        def edge_copies(n, forward):
            src = r.edge.at[n] if forward else (r.h.at[2 * layers], r.g)[n]
            dst = (out, ig)[n]
            sequence = 2 * (ox if forward else x) + y
            rows = pl.ds(pl.multiple_of(sequence * SPAN + c * HALF, HALF), HALF)
            first = 0 if forward else x * 256

            def part(start, size=128):
                return src.at[:, pl.ds(pl.multiple_of(start, 128), size)]

            places = [(dev_core, oc), (dev_y, c), (dev_cross, oc)]
            copies = [(part(first + core * 128), dst.at[rows, :], dev) for dev, core in places]
            if not forward:
                copies.append((part(ox * 256, 256), r.edge.at[n], dev_x))
            remote = [
                pltpu.make_async_remote_copy(
                    src_ref=a,
                    dst_ref=b,
                    send_sem=r.o_send.at[0],
                    recv_sem=r.o_recv.at[n if q == 3 else 2],
                    device_id=dev,
                    device_id_type=MESH,
                )
                for q, (a, b, dev) in enumerate(copies)
            ]
            own = pltpu.make_async_copy(part(first + c * 128), dst.at[rows, :], r.o_recv.at[2])
            return remote, own

        def edge_event(n, forward):
            if forward:
                edge_copies(n, False)[0][3].wait_recv()
            remote, own = edge_copies(n, forward)
            for copy in reversed(remote):
                copy.start()
            own.start()

        def edge_end():
            drain(r.o_recv.at[2], 4 * HALF)
            drain(r.o_send.at[0], 4 * HALF)

        to_z = [(ZS, step) for step in range(1, nz + 1)]
        gather = [(OWN, step) for step in range(1, nz + 1)]
        on_z = [(OWN, nz + step) for step in range(1, nz + 1)]

        def g_copy(p, stage, step=0):
            k, l, t = pieces[p]
            rows, cols = tile_size(k) // 2, tile_cols(k, t)
            xr = rows // 2
            zr = xr // shards
            part, full = r.v[k].at[l], grad[k].at[l]
            at = len(pieces) * G_RECV if stage == AC else p * G_RECV + stage
            sems = dict(send_sem=r.g_send.at[p], recv_sem=r.g_recv.at[at])

            def rng(start, size):
                return tile_rows(k, t, start, size)

            shard = rng(c * rows + x * xr + (z * zr if nz else 0), zr)
            head = pl.ds(0, rows)
            if stage == OWN and step == 0:
                return pltpu.make_async_copy(
                    r.fin.at[p, pl.ds(0, zr)], full.at[shard, cols], r.g_recv.at[at]
                )
            x_first, x_gather = X_FIRST[p] == 1, X_GATHER[p] == 1
            cut, low = pl.ds(0, xr), pl.ds(xr, xr)
            if stage == CO:
                src, dev = part.at[oy, rng(oc * rows, rows), cols], dev_core
                dst = r.co.at[p % len(TILES), head]
            elif stage == CW:
                src, dev = part.at[y, rng(oc * rows, rows), cols], dev_core
                dst = r.cw.at[p, head]
            elif stage == XO:
                src, dev = part.at[oy, rng(c * rows + ox * xr, xr), cols], dev_x
                dst = r.yr.at[p, cut]
            elif stage == YO and x_first:
                src, dev = part.at[oy, rng(c * rows + x * xr, xr), cols], dev_y
                dst = r.yr.at[p, low]
            elif stage == YO:
                src, dst, dev = part.at[oy, rng(c * rows, rows), cols], r.yr.at[p, head], dev_y
            elif stage == XS:
                src = part.at[y, rng(c * rows + ox * xr, xr), cols]
                dst, dev = r.xr.at[p, cut], dev_x
            elif stage == AX and x_gather:
                src, dst, dev = r.fin.at[p, pl.ds(0, zr)], full.at[shard, cols], dev_x
            elif stage == AX:
                span = rng(c * rows + x * xr, xr)
                src, dst, dev = full.at[span, cols], full.at[span, cols], dev_x
            elif stage == AC:
                span = rng(c * rows, rows)
                src, dst, dev = full.at[span, cols], full.at[span, cols], dev_core
            elif stage == ZS:
                dev = dev_z(step)
                src = part.at[y, rng(c * rows + x * xr + dev[1] * zr, zr), cols]
                dst = r.zr.at[p, step - 1, pl.ds(0, zr)]
            elif step <= nz:
                dev = dev_z(step)
                src, dst = r.fin.at[p, pl.ds(0, zr)], full.at[shard, cols]
            else:
                dev = dev_z(step - nz)
                span = rng(c * rows + ox * xr + z * zr, zr)
                src, dst = full.at[span, cols], full.at[span, cols]
            return pltpu.make_async_remote_copy(
                src_ref=src, dst_ref=dst, device_id=dev, device_id_type=MESH, **sems
            )

        def add_rows(p, total, half, start, sources, target=None):
            k, l, t = pieces[p]
            cols = tile_cols(k, t)
            cut = min(total, 64)

            def rows_step(i):
                rows = tile_rows(k, t, start + i * cut, cut)
                here = pl.ds(pl.multiple_of(i * cut, 16), cut)
                value = r.v[k][l, half, rows, cols].astype(F32)
                for source in sources:
                    value = value + source[here, :].astype(F32)
                if target is None:
                    r.v[k][l, half, rows, cols] = value.astype(BF16)
                else:
                    target[here, :] = value.astype(BF16)

            loop(total // cut, rows_step)

        def g_event(p, e):
            rows = tile_size(pieces[p][0]) // 2
            xr = rows // 2
            zr = xr // shards
            x_first, x_gather = X_FIRST[p] == 1, X_GATHER[p] == 1
            here = c * rows + x * xr

            def wait(*stages):
                for stage in stages:
                    g_copy(p, stage).wait_recv()

            def start(*stages):
                for stage in stages:
                    g_copy(p, *stage).start() if isinstance(stage, tuple) else g_copy(p, stage).start()

            def wait_rows(stage, count):
                if count:
                    drain(r.g_recv.at[p * G_RECV + stage], count)

            if e == 0:
                start(CO)
            elif e == 1:
                wait(CO)
                add_rows(p, rows, oy, c * rows, [r.co.at[p % len(TILES)]])
                start(XO if x_first else YO)
            elif e == 2:
                start(CW)
            elif e == 3 and x_first:
                wait(CW)
                add_rows(p, rows, y, c * rows, [r.cw.at[p]])
                start(XS)
            elif e == 3:
                wait(CW, YO)
                add_rows(p, rows, y, c * rows, [r.cw.at[p], r.yr.at[p]])
                start(XS)
            elif e == 8:
                wait(XO)
                add_rows(p, xr, oy, here, [r.yr.at[p]])
                start(YO)
            elif e == 4:
                wait(XS)
                sources = [r.xr.at[p]]
                if x_first:
                    wait(YO)
                    sources.append(r.yr.at[p, pl.ds(xr, xr)])
                add_rows(p, xr, y, here, sources)
                start(*to_z)
            elif e == 5:
                wait_rows(ZS, nz * zr)
                sources = [r.zr.at[p, step] for step in range(nz)]
                add_rows(p, zr, y, here + (z * zr if nz else 0), sources, r.fin.at[p])
                start(*([AX] if x_gather else gather))
                start(OWN)
            elif e == 6 and x_gather:
                wait(AX)
                start(*gather, *on_z)
            elif e == 6:
                wait_rows(OWN, zr * (1 + nz))
                start(AX)
            elif e == 7:
                if x_gather:
                    wait_rows(OWN, zr * (1 + 2 * nz))
                else:
                    wait(AX)
                start(AC)

        backward_plan = iter(BACKWARD)

        def gradients_here():
            for code in next(backward_plan):
                p, e = divmod(code, 16)
                if p < len(pieces):
                    g_event(p, e)
                else:
                    edge_event(e // 2, e % 2 == 1)

        def g_end():
            sizes = [tile_size(k) // 2 for k, _, _ in pieces]
            drain(r.g_recv.at[len(pieces) * G_RECV], sum(sizes))
            for p, rows in enumerate(sizes):
                xr = rows // 2
                sent = 3 * rows + xr + (2 * xr if X_FIRST[p] else rows)
                sent += xr // shards * (nz + (2 * nz + 1 if X_GATHER[p] else nz))
                sent += 0 if X_GATHER[p] else xr
                drain(r.g_send.at[p], sent)

        def small_copy(step):
            dev = [dev_core, dev_y, dev_x][step] if step < 3 else dev_z(step - 2)
            return pltpu.make_async_remote_copy(
                src_ref=r.sm.at[min(step, 3)],
                dst_ref=r.smr.at[step],
                send_sem=r.s_send.at[step],
                recv_sem=r.s_recv.at[step],
                device_id=dev,
                device_id_type=MESH,
            )

        def small_sum(step):
            if step < 3:
                small_copy(step).wait_recv()
                r.sm[step + 1] = r.sm[step] + r.smr[step]
            else:
                total = r.sm[3]
                for k in range(nz):
                    small_copy(3 + k).wait_recv()
                    total = total + r.smr[3 + k]
                own = heads * MEMORY_SLOTS
                mass = jnp.where(y == 0, total[2 * layers : 3 * layers, :own], total[2 * layers : 3 * layers, own:])
                r.total[...] = total
                r.total[2 * layers : 3 * layers, :own] = mass * (1.0 / count)
                small_out().start()

        def small_out():
            return load(4 + 4 * layers, r.total, small)

        tok_ld.wait()
        ag_ld.wait()
        fg_ld.wait()
        r.sm[0] = jnp.zeros(r.sm.shape[1:], F32)
        for l in range(layers):
            r.nrm[...] = rms(2 * l, ag[pl.ds(l, 1), :])
            weights_here()
            for turn in range(2):
                half = y if turn == 0 else oy
                slot = 2 * l + turn
                use = jnp.where(c == 1, slot, 2 * layers)
                if turn == 0:
                    w_ld[WI, l].wait()
                if slot:
                    state_sent(slot - 1, 0, 0)
                project(l, half)
                state_send(slot, 0, 0)
                weights_here()
                state_recv(slot, 0, 0)
                attend(l, half, use, weights_here if slot == 0 else None)
                weights_here()
            w_ld[WO, l].wait()
            attn_out(l)
            r.nrm[...] = rms(2 * l + 1, fg[pl.ds(l, 1), :])
            weights_here()
            w_ld[F1, l].wait()
            w_ld[F2, l].wait()
            r.acc[...] = r.h[2 * l + 1].astype(F32)
            ffn(l, 0, half_tiles)
            weights_here()
            for tile in range(half_tiles, tiles):
                ffn(l, tile, tile + 1)
                weights_here()
            r.h[2 * l + 2] = r.acc[...].astype(BF16)
        gradients_here()
        w_end()
        state_sent(2 * layers - 1, 0, 0)
        cot_ld.wait()
        for l in range(layers):
            lm = r.lm[l].reshape(2 * heads * 64, 128).T
            r.sm[0, pl.ds(2 * layers + l, 1), :] = lm[0:1, :]

        for l in reversed(range(layers)):
            r.nT[...] = rms(2 * l + 1, fg[pl.ds(l, 1), :]).T
            r.acc[...] = jnp.zeros(r.acc.shape, F32)
            for tile in range(tiles):
                ffn_back(l, tile, tile + 1)
                gradients_here()
            rms_back(2 * l + 1, fg[pl.ds(l, 1), :], r.acc[...], layers + l)
            gradients_here()
            mixed_back(l)
            attn_out_grad(l)
            gradients_here()
            r.nT[...] = rms(2 * l, ag[pl.ds(l, 1), :]).T
            r.acc[...] = jnp.zeros(r.acc.shape, F32)
            for turn in range(2):
                half = oy if turn == 0 else y
                fwd_slot = jnp.where(c == 1, 2 * l + 1 - turn, 2 * layers)
                slot = 2 * l + turn
                use = jnp.where(c == 0, slot, 2 * layers)
                if not (turn == 0 and l == layers - 1):
                    prev = 2 * l if turn == 1 else 2 * (l + 1) + 1
                    state_sent(prev, 1, 1)
                attend_back(l, half, fwd_slot)
                state_send(slot, 1, 1)
                gradients_here()
                state_recv(slot, 1, 1)
                project_back(l, half, use)
                gradients_here()
            rms_back(2 * l, ag[pl.ds(l, 1), :], r.acc[...].T, l)
            if l == 0:
                small_copy(0).start()
            gradients_here()
        state_sent(1, 1, 1)
        for step in range(4):
            small_sum(step)
            if step < 2:
                small_copy(step + 1).start()
            elif step == 2:
                for k in range(nz):
                    small_copy(3 + k).start()
            gradients_here()
        for step in range(3 + nz):
            small_copy(step).wait_send()
        small_out().wait()
        g_end()
        edge_end()

    L = layers
    nzb = max(nz, 1)
    scratch = dict(
        v=[pltpu.VMEM((L, 2, *dims[k]), BF16) for k in KINDS],
        h=pltpu.VMEM((2 * L + 1, HALF, width), BF16),
        nT=pltpu.VMEM((width, HALF), BF16),
        nrm=pltpu.VMEM((HALF, width), BF16),
        ag=pltpu.VMEM((L, width), F32),
        fg=pltpu.VMEM((L, width), F32),
        total=pltpu.VMEM((8, width), F32),
        g=pltpu.VMEM((HALF, width), BF16),
        pj=pltpu.VMEM((L, 2 * heads, HALF, 256), BF16),
        pjT=pltpu.VMEM((L, 2 * heads, 256, HALF), BF16),
        rz=pltpu.VMEM((L, 2 * heads, 64, HALF), F32),
        pr=pltpu.VMEM((L, 2 * heads, 64, HALF), BF16),
        sc=pltpu.VMEM((L, 2 * heads, 64, HALF), BF16),
        mixT=pltpu.VMEM((L, 2 * heads, 64, HALF), BF16),
        lm=pltpu.VMEM((L, 2 * heads, 64, 128), F32),
        before=pltpu.VMEM((L, tiles, HALF, 512), BF16),
        actT=pltpu.VMEM((512, HALF), BF16),
        acc=pltpu.VMEM((HALF, width), F32),
        tmp=pltpu.VMEM((heads, 192, HALF), F32),
        tri=pltpu.VMEM((BLK, BLK), BF16),
        state_out=pltpu.VMEM((2, heads, 256, 128), BF16),
        state_in=pltpu.VMEM((2 * L + 1, heads, 256, 128), BF16),
        sm=pltpu.VMEM((4, 8, width), F32),
        smr=pltpu.VMEM((3 + nzb, 8, width), F32),
        co=pltpu.VMEM((len(TILES), 256, 512), BF16),
        cw=pltpu.VMEM((len(pieces), 256, 512), BF16),
        edge=pltpu.VMEM((2, HALF, 256), BF16),
        yr=pltpu.VMEM((len(pieces), 256, 512), BF16),
        xr=pltpu.VMEM((len(pieces), 128, 512), BF16),
        zr=pltpu.VMEM((len(pieces), nzb, 128 // shards, 512), BF16),
        fin=pltpu.VMEM((len(pieces), 128 // shards, 512), BF16),
        ld_sem=pltpu.SemaphoreType.DMA((5 + 4 * L,)),
        w_send=pltpu.SemaphoreType.DMA((L,)),
        w_recv=pltpu.SemaphoreType.DMA((W_RECV * len(ITEMS),)),
        st_send=pltpu.SemaphoreType.DMA((2 * L,)),
        st_recv=pltpu.SemaphoreType.DMA((2 * L,)),
        o_send=pltpu.SemaphoreType.DMA((1,)),
        o_recv=pltpu.SemaphoreType.DMA((3,)),
        g_send=pltpu.SemaphoreType.DMA((len(pieces),)),
        g_recv=pltpu.SemaphoreType.DMA((len(pieces) * G_RECV + 1,)),
        s_send=pltpu.SemaphoreType.DMA((3 + nzb,)),
        s_recv=pltpu.SemaphoreType.DMA((3 + nzb,)),
    )
    flat, layout = jax.tree.flatten(scratch)
    return kernel, flat


def finish(layers, width, out, ig, small, grads):
    steps = 2 * layers
    own = width // 2

    def kernel(out_in, ig_in, small_in, wi, wo, f1, f2, *results):
        out_to, ig_to, wi_to, wo_to, ag_to, f1_to, f2_to, fg_to, mass_to = results
        out_to[...] = out_in[...]
        ig_to[...] = ig_in[...]
        for source, target in ((wi, wi_to), (wo, wo_to), (f1, f1_to), (f2, f2_to)):
            target[...] = source[...].astype(F32)
        ag_to[...] = small_in[0:layers, :]
        fg_to[...] = small_in[layers : 2 * layers, :]
        mass_to[...] = small_in[2 * layers : 3 * layers, :own]

    edge = pl.BlockSpec((out.shape[0] // steps, out.shape[1]), lambda i: (i, 0))

    def part(v):
        return pl.BlockSpec((1, v.shape[1] // 2, v.shape[2]), lambda i: (i // 2, i % 2, 0))

    def whole(*shape):
        return pl.BlockSpec(shape, lambda i: (0, 0))

    like = [jax.ShapeDtypeStruct(v.shape, F32) for v in grads]
    gain = jax.ShapeDtypeStruct((layers, width), F32)
    mass = jax.ShapeDtypeStruct((layers, own), F32)
    edges = [jax.ShapeDtypeStruct(out.shape, BF16)] * 2
    gain_spec, mass_spec = whole(layers, width), whole(layers, own)
    parts = [part(v) for v in grads]
    return pl.pallas_call(
        kernel,
        grid=(steps,),
        in_specs=[edge, edge, whole(*small.shape), *parts],
        out_specs=[edge, edge, *parts[:2], gain_spec, *parts[2:], gain_spec, mass_spec],
        out_shape=[*edges, *like[:2], gain, *like[2:], gain, mass],
        compiler_params=pltpu.CompilerParams(vmem_limit_bytes=60 * 1024 * 1024),
    )(out, ig, small, *grads)


def solution(mesh):
    n_dp = mesh.shape["dp"]
    dp_inside = n_dp in (2, 4)

    def local(tokens, attn_gain, w_in, w_out, ffn_gain, ffn_in, ffn_out, cotangent):
        layers, width = attn_gain.shape
        arrays = (w_in, w_out, ffn_in, ffn_out)
        dims = [v.shape[1:] for v in arrays]
        kernel, scratch = make_kernel(
            layers, dims, n_dp, dp_inside, tokens.shape[0] * n_dp
        )
        anyspace = pl.BlockSpec(memory_space=pl.ANY)
        vmem = pl.BlockSpec(memory_space=pltpu.VMEM)
        edge = jax.ShapeDtypeStruct((tokens.shape[0], width // 4), BF16)
        results = pl.pallas_call(
            kernel,
            out_shape=[edge, edge]
            + [jax.ShapeDtypeStruct(v.shape, BF16) for v in arrays]
            + [jax.ShapeDtypeStruct((8, width), F32)],
            in_specs=[anyspace] * 8,
            out_specs=[anyspace] * 7,
            scratch_shapes=scratch,
            compiler_params=pltpu.CompilerParams(
                collective_id=0, has_side_effects=True, vmem_limit_bytes=63 * 1024 * 1024
            ),
        )(tokens, attn_gain, ffn_gain, cotangent, *arrays)
        out, ig, *grads, small = results
        if not dp_inside and n_dp > 1:
            grads = [lax.psum(v, "dp") for v in grads]
            small = lax.psum(small, "dp")
        return finish(layers, width, out, ig, small, grads)

    placed = (
        P("dp", None),
        P(),
        P(None, None, "tensor"),
        P(None, "tensor", None),
        P(),
        P(None, None, "tensor"),
        P(None, "tensor", None),
        P("dp", None),
    )
    return jax.shard_map(
        local,
        mesh=mesh,
        in_specs=placed,
        out_specs=(
            P("dp", "section"),
            P("dp", "section"),
            P(None, None, "tensor"),
            P(None, "tensor", None),
            P(),
            P(None, None, "tensor"),
            P(None, "tensor", None),
            P(),
            P(None, "tensor"),
        ),
        check_vma=False,
    )
```

```python
import types

import jax
import jax.numpy as jnp
from jax import lax
from jax.experimental import pallas as pl
from jax.experimental.pallas import tpu as pltpu
from jax.sharding import PartitionSpec as P

HEAD_SIZE = 64
MEMORY_SLOTS = 64
SPAN = 1024
NORM_EPS = 1e-05
GELU = 0.7978845608028654
MESH = pl.DeviceIdType.MESH
F32 = jnp.float32
BF16 = jnp.bfloat16
HALF = SPAN // 2
BLK = 256
WI, WO, F1, F2 = KINDS = range(4)
TO_Y, TO_X, TO_Z, ON_Z, ON_X, TO_C = range(6)
W_RECV = 5
CO, YO, XO, CW, XS, AX, OWN, ZS, AC = range(9)
G_RECV = 8
ITEMS = (
    (WI, 0, 0, 1, 0),
    (WI, 0, 1, 1, 0),
    (WO, 0, 0, 1, 0),
    (F1, 0, 0, 1, 0),
    (F2, 0, 0, 1, 0),
    (F1, 0, 1, 1, 0),
    (F2, 0, 1, 1, 0),
    (WI, 1, 0, 1, 0),
    (WI, 1, 1, 1, 0),
    (WO, 1, 0, 1, 1),
    (F1, 1, 0, 2, 0),
    (F2, 1, 0, 2, 1),
)
TILES = ((F2, 0), (F1, 0), (F2, 1), (F1, 1), (WO, 0), (WI, 0), (WI, 1))
FORWARD = (
    (0, 8, 16, 24, 32, 40, 48, 56, 64, 72, 80, 88),
    (),
    (),
    (1,),
    (),
    (9,),
    (17, 2, 3, 25, 10, 11, 33, 18, 19, 4, 41, 5, 26, 27, 49, 12, 57, 13),
    (20, 34, 35, 65),
    (28, 42, 43, 50, 51, 73, 21),
    (58, 59),
    (36, 66, 44, 67, 81, 29, 52, 37),
    (60, 68, 45, 53),
    (),
    (),
    (83, 82),
    (61, 69),
    (84,),
    (89, 77),
    (),
    (85, 93),
    (),
    (),
)
BACKWARD = (
    (224,),
    (0, 16),
    (48, 32),
    (2, 18, 1, 17, 49),
    (50, 3, 19, 34, 33, 225),
    (),
    (8, 51, 66, 64, 35),
    (67, 24, 65),
    (),
    (),
    (56,),
    (),
    (80, 4, 96),
    (),
    (81, 20, 97),
    (40,),
    (5,),
    (52,),
    (82, 21, 98),
    (6,),
    (83, 128, 53, 112, 72),
    (160, 7, 144, 129, 99, 22, 113),
    (130, 84, 161, 54, 114, 36, 145),
    (136, 162, 131, 68, 146),
    (),
    (178, 176, 85, 100),
    (177, 115, 23, 37),
    (69,),
    (),
    (55, 86),
    (163,),
    (192, 208, 101),
    (116, 38),
    (193, 70, 209, 87, 147),
    (),
    (132, 164, 102),
    (),
    (179, 194, 39, 71, 117, 210),
    (133,),
    (226, 148, 195, 165, 103),
    (118, 180, 211, 134, 149),
    (227, 166, 196, 181, 119),
    (150, 212, 197, 135, 213, 167, 182, 198, 151, 214, 199, 183, 215),
)
X_FIRST = (1, 1, 1, 1, 1, 0, 0, 0, 1, 0, 0, 0, 0, 0)
X_GATHER = (0, 0, 0, 0, 0, 0, 0, 0, 0, 0, 0, 1, 0, 0)


def nn(a, b):
    return lax.dot_general(a, b, (((1,), (0,)), ((), ())), preferred_element_type=F32)


def nt(a, b):
    return lax.dot_general(a, b, (((1,), (1,)), ((), ())), preferred_element_type=F32)


def loop(n, body):
    def step(i, carry):
        body(i)
        return carry

    lax.fori_loop(0, n, step, 0)


def together(n, body, between=None):
    running = [body(i) for i in range(n)]
    for turn, _ in enumerate(zip(*running, strict=True)):
        if between is not None and turn % 5 == 4:
            between()


def make_kernel(layers, dims, n_dp, dp_inside, count):
    width = dims[WI][0]
    heads = dims[WI][1] // (3 * HEAD_SIZE + MEMORY_SLOTS)
    nz = n_dp - 1 if dp_inside else 0
    shards = n_dp if dp_inside else 1
    tiles = 2 * dims[F2][0] // 512
    half_tiles = tiles // 2
    pieces = [(k, l, t) for l in reversed(range(layers)) for k, t in TILES]

    def tile_size(k):
        return min(dims[k][0], 512)


    def kernel(*refs):
        tok, ag_in, fg_in, cot, *rest = refs
        hbm, (out, ig, *grad), small = rest[:4], rest[4:10], rest[10]
        r = types.SimpleNamespace(**jax.tree.unflatten(layout, rest[11:]))
        s = lax.axis_index("section")
        z = lax.axis_index("dp")
        y = lax.axis_index("tensor")
        c = lax.rem(s, 2)
        x = s // 2
        oc, ox, oy = 1 - c, 1 - x, 1 - y
        dev_core = (x * 2 + oc, z, y)
        dev_x = (ox * 2 + c, z, y)
        dev_y = (s, z, oy)
        dev_cross = (x * 2 + oc, z, oy)

        z0 = lax.rem(z, 2)
        dev_pair = (s, z + 1 - 2 * z0, y)

        def dev_z(k):
            return (s, lax.rem(z + k, n_dp), y)

        barrier = pltpu.get_barrier_semaphore()
        everyone = [dev_core, dev_x, dev_y, dev_cross]
        everyone += [dev_z(k) for k in range(1, nz + 1)] if nz else [dev_pair]
        for d in everyone:
            pl.semaphore_signal(barrier, inc=1, device_id=d, device_id_type=MESH)

        row0 = pl.multiple_of((2 * x + y) * SPAN + c * HALF, HALF)

        def load(i, src, dst):
            return pltpu.make_async_copy(src, dst, r.ld_sem.at[i])

        tok_ld = load(0, tok.at[pl.ds(row0, HALF), :], r.h.at[0])
        cot_ld = load(1, cot.at[pl.ds(row0, HALF), :], r.g)
        ag_ld, fg_ld = load(2, ag_in, r.ag), load(3, fg_in, r.fg)
        ag, fg = r.ag, r.fg
        w_ld = {}
        for l in range(layers):
            for k in KINDS:
                at = 4 + l * 4 + k
                w_ld[k, l] = load(at, hbm[k].at[l], r.v[k].at[l, y])

        tok_ld.start()
        ag_ld.start()
        w_ld[WI, 0].start()
        fg_ld.start()

        def drain(sem, rows):
            some = tok.at[pl.ds(0, rows), :]
            pltpu.make_async_copy(some, some, sem).wait()

        def tile_rows(k, t, start, size):
            first = t * 512 if k == F2 else 0
            return pl.ds(pl.multiple_of(first + start, 16), size)

        def tile_cols(k, t, n=1):
            return pl.ds(t * 512, n * 512) if k in (WI, F1) else pl.ds(0, 512)

        def w_copy(i, stage):
            k, l, t, n, straight = ITEMS[i]
            total = tile_size(k) * (n if k == F2 else 1)
            rows, cols = total // 8, tile_cols(k, t, n)

            def eighth(cx, cz, start=0, size=rows):
                return tile_rows(k, t, (4 * cx + 2 * cz + c) * rows + start, size)

            mine, half = eighth(x, z0), rows // 2
            if straight:
                mine = tile_rows(k, t, c * (total // 2), total // 2)
            v = r.v[k].at[l]
            span, dev = (
                (mine, dev_y),
                (mine, dev_x),
                (mine, dev_pair),
                (eighth(ox, z0, 0, half), dev_pair),
                (eighth(x, 1 - z0, half, half), dev_x),
                (mine, dev_core),
                (eighth(ox, z0), dev_core),
                (eighth(x, 1 - z0), dev_core),
                (eighth(ox, 1 - z0), dev_core),
            )[stage]
            side = y if stage == TO_Y else oy
            return pltpu.make_async_remote_copy(
                src_ref=hbm[k].at[l, span, cols] if stage == TO_Y else v.at[side, span, cols],
                dst_ref=v.at[side, span, cols],
                send_sem=r.w_send.at[l],
                recv_sem=r.w_recv.at[i * W_RECV + (TO_Y, TO_X, TO_Z, ON_Z, ON_Z, *[ON_X] * 4)[stage]],
                device_id=dev,
                device_id_type=MESH,
            )

        def w_event(i, e):
            k, _, _, n, straight = ITEMS[i]
            rows = tile_size(k) * n // 8
            if e in (1, 2, 3):
                w_copy(i, (TO_Y, TO_X, TO_Z)[e - 1]).wait_recv()
            elif e == 4:
                drain(r.w_recv.at[i * W_RECV + ON_Z], rows)
            elif e == 5:
                drain(r.w_recv.at[i * W_RECV + ON_X], 4 * rows)
            starts = (
                (TO_Y,),
                (TO_C,) if straight else (TO_X, TO_Z, TO_C),
                (ON_Z, TO_C + 1),
                (ON_X, TO_C + 2),
                (TO_C + 3,),
                (),
            )[e]
            for stage in starts:
                w_copy(i, stage).start()

        def w_end():
            for layer in range(layers):
                sent = [tile_size(k) * n for k, l, _, n, _ in ITEMS if l == layer]
                drain(r.w_send.at[layer], sum(sent))

        forward_plan = iter(FORWARD)

        def weights_here():
            for code in next(forward_plan):
                w_event(code // 8, code % 8)

        pl.semaphore_wait(barrier, len(everyone))
        weights_here()
        for l in range(layers):
            for k in KINDS:
                if (k, l) != (WI, 0):
                    w_ld[k, l].start()
        cot_ld.start()

        tri_s = lax.broadcasted_iota(jnp.int32, (BLK, BLK), 0)
        tri_t = lax.broadcasted_iota(jnp.int32, (BLK, BLK), 1)
        r.tri[...] = jnp.where(tri_s <= tri_t, 1.0, 0.0).astype(BF16)
        r.state_in[2 * layers] = jnp.zeros(r.state_in.shape[1:], BF16)

        def masked(v, on):
            if not on:
                return v.astype(BF16)
            keep = lax.broadcasted_iota(jnp.int32, (BLK, BLK), 0) <= lax.broadcasted_iota(
                jnp.int32, (BLK, BLK), 1
            )
            return jnp.where(keep, v, 0.0).astype(BF16)

        def blocks(tb):
            return [(b, b == tb) for b in range(tb + 1)]

        def state_copy(slot, buf):
            return pltpu.make_async_remote_copy(
                src_ref=r.state_out.at[buf],
                dst_ref=r.state_in.at[slot],
                send_sem=r.st_send.at[slot],
                recv_sem=r.st_recv.at[slot],
                device_id=dev_core,
                device_id_type=MESH,
            )

        def state_send(slot, buf, from_core):
            @pl.when(c == from_core)
            def _():
                state_copy(slot, buf).start()

        def state_recv(slot, buf, from_core):
            @pl.when(c != from_core)
            def _():
                state_copy(slot, buf).wait_recv()

        def state_sent(slot, buf, from_core):
            @pl.when(c == from_core)
            def _():
                state_copy(slot, buf).wait_send()

        def rms(sub, gain):
            h = r.h[sub].astype(F32)
            scale = lax.rsqrt(jnp.mean(h * h, axis=1, keepdims=True) + NORM_EPS)
            return (h * scale * gain).astype(BF16)

        def rms_back(sub, gain, dn, gain_row):
            h = r.h[sub].astype(F32)
            scale = lax.rsqrt(jnp.mean(h * h, axis=1, keepdims=True) + NORM_EPS)
            a = dn * gain
            hs = h * scale
            r.sm[0, pl.ds(gain_row, 1), :] = jnp.sum(dn * hs, axis=0, keepdims=True)
            dh = scale * (a - hs * jnp.mean(hs * a, axis=1, keepdims=True))
            r.g[...] = (r.g[...].astype(F32) + dh).astype(BF16)

        def project(l, half):
            def head(i):
                hd = half * heads + i
                cols = pl.ds(pl.multiple_of(i * 256, 256), 256)
                p = nn(r.nrm[...], r.v[WI][l, half, :, cols])
                yield
                lane = lax.broadcasted_iota(jnp.int32, (HALF, 128), 1)
                hi = p[:, 128:]
                hi = jnp.where(lane >= 64, jnp.exp(hi), hi)
                pb = jnp.concatenate([p[:, :128], hi], axis=1).astype(BF16)
                r.pj[l, hd] = pb
                pt = pb.T
                r.pjT[l, hd] = pt
                yield
                kv = pt[64:192]
                e = pt[192:256]
                buf = r.state_out.at[0]
                buf[i, 0:64, :] = nt(e, kv).astype(BF16)
                buf[i, 64:192, 0:64] = nt(kv, e).astype(BF16)
                buf[i, 192:256, :] = nn(e, jnp.ones((HALF, 128), BF16)).astype(BF16)
                yield

            together(heads, head)

        def attend(l, half, slot, between):
            def head(i):
                hd = half * heads + i
                q = r.pjT[l, hd, 0:64, :]
                v = r.pjT[l, hd, 128:192, :]
                e = r.pjT[l, hd, 192:256, :]
                sk = r.state_in[slot, i, 0:64, 0:64]
                svt = r.state_in[slot, i, 128:192, 0:64]
                before = r.state_in[slot, i, 192:256, 0:1].astype(F32)
                zero = jnp.zeros((64, BLK), BF16)
                log_sum = jnp.zeros((64, 1), F32)
                for tb in range(2):
                    ts = slice(tb * BLK, (tb + 1) * BLK)
                    qt = q[:, ts]
                    rq = jnp.concatenate([zero, qt], axis=0)
                    num = nn(sk, qt)
                    yield
                    for b, on in blocks(tb):
                        bs = slice(b * BLK, (b + 1) * BLK)
                        at = masked(nn(r.pj[l, hd, bs, 0:128], rq), on)
                        yield
                        num = num + nn(e[:, bs], at)
                        yield
                    zt = nn(e[:, ts], r.tri[...]) + before
                    before = zt[:, BLK - 1 : BLK]
                    rz = 1.0 / zt
                    sc = num * rz * 0.125
                    yield
                    ex = jnp.exp(sc - jnp.max(sc, axis=0, keepdims=True))
                    p = ex * (1.0 / jnp.sum(ex, axis=0, keepdims=True))
                    w = (p * rz).astype(BF16)
                    r.rz[l, hd, :, ts] = rz
                    r.pr[l, hd, :, ts] = p.astype(BF16)
                    r.sc[l, hd, :, ts] = sc.astype(BF16)
                    log_sum = log_sum + jnp.sum(jnp.log(zt), axis=1, keepdims=True)
                    rw = jnp.concatenate([zero, w], axis=0)
                    yield
                    o = nn(svt, w)
                    for b, on in blocks(tb):
                        bs = slice(b * BLK, (b + 1) * BLK)
                        gt = masked(nn(r.pj[l, hd, bs, 128:256], rw), on)
                        yield
                        o = o + nn(v[:, bs], gt)
                        yield
                    r.mixT[l, hd, :, ts] = o.astype(BF16)
                r.lm[l, hd] = jnp.broadcast_to(log_sum, (64, 128))
                yield

            together(heads, head, between)

        def attn_out(l):
            mixed = r.mixT[l].reshape(2 * heads * 64, HALF).T
            wo = r.v[WO][l].reshape(2 * dims[WO][0], width)
            r.h[2 * l + 1] = (r.h[2 * l].astype(F32) + nn(mixed, wo)).astype(BF16)

        def tile_of(i, first):
            j = lax.rem(first * half_tiles + i, tiles)
            return j, j // half_tiles, pl.ds(pl.multiple_of(lax.rem(j, half_tiles) * 512, 512), 512)

        def ffn(l, lo, hi):
            def part(i):
                j, half, at = tile_of(i // 2 + lo, y)
                ts = slice(i % 2 * BLK, (i % 2 + 1) * BLK)
                b = nn(r.nrm[ts, :], r.v[F1][l, half, :, at])
                yield
                r.before[l, j, ts, :] = b.astype(BF16)
                th = jnp.tanh(b * (GELU + (GELU * 0.044715) * (b * b)))
                act = (0.5 * b * th + 0.5 * b).astype(BF16)
                yield
                r.acc[ts, :] = r.acc[ts, :] + nn(act, r.v[F2][l, half, at, :])
                yield

            together(2 * (hi - lo), part)

        def ffn_back(l, lo, hi):
            def tile(i):
                j, half, at = tile_of(i + lo, oy)
                w1 = r.v[F1][l, half, :, at]
                w2 = r.v[F2][l, half, at, :]
                for tb in range(2):
                    ts = slice(tb * BLK, (tb + 1) * BLK)
                    b = r.before[l, j, ts, :].astype(F32)
                    bb = b * b
                    th = jnp.tanh(b * (GELU + (GELU * 0.044715) * bb))
                    slope = 0.5 + 0.5 * th
                    r.actT[:, ts] = (b * slope).astype(BF16).T
                    slope = slope + (0.5 * b) * (1.0 - th * th) * (GELU + (GELU * 0.134145) * bb)
                    db = (nt(r.g[ts, :], w2) * slope).astype(BF16)
                    r.nrm[ts, :] = db
                    r.acc[ts, :] = r.acc[ts, :] + nt(db, w1)
                r.v[F2][l, half, at, :] = nn(r.actT[...], r.g[...]).astype(BF16)
                r.v[F1][l, half, :, at] = nn(r.nT[...], r.nrm[...]).astype(BF16)

            loop(hi - lo, tile)

        def mixed_back(l):
            wo = r.v[WO][l].reshape(2 * dims[WO][0], width)
            r.nrm[...] = nt(wo, r.g[...]).astype(BF16)

        def attn_out_grad(l):
            mixed = r.mixT[l].reshape(2 * heads * 64, HALF)
            r.v[WO][l] = nn(mixed, r.g[...]).astype(BF16).reshape(r.v[WO].shape[1:])

        def attend_back(l, half, slot):
            def head(i):
                hd = half * heads + i
                q = r.pjT[l, hd, 0:64, :]
                kt = r.pjT[l, hd, 64:128, :]
                e = r.pjT[l, hd, 192:256, :]
                do = r.nrm[pl.ds(pl.multiple_of(hd * 64, 64), 64), :]
                skv = r.state_in[slot, i, 0:64, :]
                skt = r.state_in[slot, i, 64:128, 0:64]
                zero = jnp.zeros((64, BLK), BF16)
                none = jnp.zeros((64, BLK), F32)
                dv, dk, de = [none, none], [none, none], [none, none]
                dzs, dns, ws, dqs = [], [], [], []
                for tb in range(2):
                    ts = slice(tb * BLK, (tb + 1) * BLK)
                    dot, qt = do[:, ts], q[:, ts]
                    rd = jnp.concatenate([dot, zero], axis=0)
                    rz = r.rz[l, hd, :, ts]
                    p = r.pr[l, hd, :, ts].astype(F32)
                    sc = r.sc[l, hd, :, ts].astype(F32)
                    w = p * rz
                    wb = w.astype(BF16)
                    dw = nn(skv, jnp.concatenate([zero, dot], axis=0))
                    dgs = []
                    for b, on in blocks(tb):
                        bs = slice(b * BLK, (b + 1) * BLK)
                        dg = masked(nn(r.pj[l, hd, bs, 128:256], rd), on)
                        yield
                        dw = dw + nn(e[:, bs], dg)
                        dgs.append(dg)
                        yield
                    dp = dw * rz
                    ds = p * (dp - jnp.sum(p * dp, axis=0, keepdims=True))
                    dnb = (ds * rz * 0.125).astype(BF16)
                    dzs.append((-(dw * w + ds * sc) * rz).astype(BF16))
                    dns.append(dnb)
                    ws.append(wb)
                    rw = jnp.concatenate([zero, wb], axis=0)
                    rn = jnp.concatenate([zero, dnb], axis=0)
                    rq = jnp.concatenate([zero, qt], axis=0)
                    yield
                    dq = nn(skt, dnb)
                    for b, on in blocks(tb):
                        bs = slice(b * BLK, (b + 1) * BLK)
                        qk = r.pj[l, hd, bs, 0:128]
                        ve = r.pj[l, hd, bs, 128:256]
                        at = masked(nn(qk, rq), on)
                        yield
                        gt = masked(nn(ve, rw), on)
                        yield
                        da = masked(nn(ve, rn), on)
                        yield
                        dv[b] = dv[b] + nt(dot, gt)
                        de[b] = de[b] + nt(wb, dgs[b]) + nt(dnb, at)
                        dk[b] = dk[b] + nt(qt, da)
                        dq = dq + nn(kt[:, bs], da)
                        yield
                    dqs.append(dq.astype(BF16))
                tri = r.tri[...]
                rev1 = nt(dzs[1], tri)
                rev0 = nt(dzs[0], tri) + rev1[:, 0:1]
                tmp = r.tmp.at[i]
                for b, rev in enumerate((rev0, rev1)):
                    bs = slice(b * BLK, (b + 1) * BLK)
                    tmp[0:64, bs] = dk[b]
                    tmp[64:128, bs] = dv[b]
                    tmp[128:192, bs] = de[b] + rev
                dn_all = jnp.concatenate(dns, axis=1)
                w_all = jnp.concatenate(ws, axis=1)
                buf = r.state_out.at[1]
                buf[i, 0:64, :] = jnp.concatenate([nt(dn_all, q), nt(w_all, do)], axis=1).astype(
                    BF16
                )
                buf[i, 64:128, 0:64] = nt(q, dn_all).astype(BF16)
                buf[i, 128:192, 0:64] = nt(do, w_all).astype(BF16)
                r.pjT[l, hd, 0:64, :] = jnp.concatenate(dqs, axis=1)
                buf[i, 192:256, :] = jnp.broadcast_to(rev0[:, 0:1], (64, 128)).astype(BF16)
                yield

            together(heads, head, gradients_here)

        def project_back(l, half, slot):
            def head(i):
                hd = half * heads + i
                kv = r.pjT[l, hd, 64:192, :]
                e = r.pjT[l, hd, 192:256, :]
                sin = r.state_in.at[slot]
                dkv = r.tmp[i, 0:128, :] + nn(sin[i, 64:192, 0:64], e)
                de = r.tmp[i, 128:192, :] + nn(sin[i, 0:64, :], kv)
                de = (de + sin[i, 192:256, 0:1].astype(F32)) * e.astype(F32)
                r.pjT[l, hd, 64:192, :] = dkv.astype(BF16)
                r.pjT[l, hd, 192:256, :] = de.astype(BF16)
                cols = pl.ds(pl.multiple_of(i * 256, 256), 256)
                dp = r.pjT[l, hd]
                r.acc[...] = r.acc[...] + nn(r.v[WI][l, half, :, cols], dp)
                r.v[WI][l, half, :, cols] = nt(r.nT[...], dp).astype(BF16)

            loop(heads, head)

        def edge_copies(n, forward):
            src = r.edge.at[n] if forward else (r.h.at[2 * layers], r.g)[n]
            dst = (out, ig)[n]
            sequence = 2 * (ox if forward else x) + y
            rows = pl.ds(pl.multiple_of(sequence * SPAN + c * HALF, HALF), HALF)
            first = 0 if forward else x * 256

            def part(start, size=128):
                return src.at[:, pl.ds(pl.multiple_of(start, 128), size)]

            places = [(dev_core, oc), (dev_y, c), (dev_cross, oc)]
            copies = [(part(first + core * 128), dst.at[rows, :], dev) for dev, core in places]
            if not forward:
                copies.append((part(ox * 256, 256), r.edge.at[n], dev_x))
            remote = [
                pltpu.make_async_remote_copy(
                    src_ref=a,
                    dst_ref=b,
                    send_sem=r.o_send.at[0],
                    recv_sem=r.o_recv.at[n if q == 3 else 2],
                    device_id=dev,
                    device_id_type=MESH,
                )
                for q, (a, b, dev) in enumerate(copies)
            ]
            own = pltpu.make_async_copy(part(first + c * 128), dst.at[rows, :], r.o_recv.at[2])
            return remote, own

        def edge_event(n, forward):
            if forward:
                edge_copies(n, False)[0][3].wait_recv()
            remote, own = edge_copies(n, forward)
            for copy in reversed(remote):
                copy.start()
            own.start()

        def edge_end():
            drain(r.o_recv.at[2], 4 * HALF)
            drain(r.o_send.at[0], 4 * HALF)

        to_z = [(ZS, step) for step in range(1, nz + 1)]
        gather = [(OWN, step) for step in range(1, nz + 1)]
        on_z = [(OWN, nz + step) for step in range(1, nz + 1)]

        def g_copy(p, stage, step=0):
            k, l, t = pieces[p]
            rows, cols = tile_size(k) // 2, tile_cols(k, t)
            xr = rows // 2
            zr = xr // shards
            part, full = r.v[k].at[l], grad[k].at[l]
            at = len(pieces) * G_RECV if stage == AC else p * G_RECV + stage
            sems = dict(send_sem=r.g_send.at[p], recv_sem=r.g_recv.at[at])

            def rng(start, size):
                return tile_rows(k, t, start, size)

            shard = rng(c * rows + x * xr + (z * zr if nz else 0), zr)
            head = pl.ds(0, rows)
            if stage == OWN and step == 0:
                return pltpu.make_async_copy(
                    r.fin.at[p, pl.ds(0, zr)], full.at[shard, cols], r.g_recv.at[at]
                )
            x_first, x_gather = X_FIRST[p] == 1, X_GATHER[p] == 1
            cut, low = pl.ds(0, xr), pl.ds(xr, xr)
            if stage == CO:
                src, dev = part.at[oy, rng(oc * rows, rows), cols], dev_core
                dst = r.co.at[p % len(TILES), head]
            elif stage == CW:
                src, dev = part.at[y, rng(oc * rows, rows), cols], dev_core
                dst = r.cw.at[p, head]
            elif stage == XO:
                src, dev = part.at[oy, rng(c * rows + ox * xr, xr), cols], dev_x
                dst = r.yr.at[p, cut]
            elif stage == YO and x_first:
                src, dev = part.at[oy, rng(c * rows + x * xr, xr), cols], dev_y
                dst = r.yr.at[p, low]
            elif stage == YO:
                src, dst, dev = part.at[oy, rng(c * rows, rows), cols], r.yr.at[p, head], dev_y
            elif stage == XS:
                src = part.at[y, rng(c * rows + ox * xr, xr), cols]
                dst, dev = r.xr.at[p, cut], dev_x
            elif stage == AX and x_gather:
                src, dst, dev = r.fin.at[p, pl.ds(0, zr)], full.at[shard, cols], dev_x
            elif stage == AX:
                span = rng(c * rows + x * xr, xr)
                src, dst, dev = full.at[span, cols], full.at[span, cols], dev_x
            elif stage == AC:
                span = rng(c * rows, rows)
                src, dst, dev = full.at[span, cols], full.at[span, cols], dev_core
            elif stage == ZS:
                dev = dev_z(step)
                src = part.at[y, rng(c * rows + x * xr + dev[1] * zr, zr), cols]
                dst = r.zr.at[p, step - 1, pl.ds(0, zr)]
            elif step <= nz:
                dev = dev_z(step)
                src, dst = r.fin.at[p, pl.ds(0, zr)], full.at[shard, cols]
            else:
                dev = dev_z(step - nz)
                span = rng(c * rows + ox * xr + z * zr, zr)
                src, dst = full.at[span, cols], full.at[span, cols]
            return pltpu.make_async_remote_copy(
                src_ref=src, dst_ref=dst, device_id=dev, device_id_type=MESH, **sems
            )

        def add_rows(p, total, half, start, sources, target=None):
            k, l, t = pieces[p]
            cols = tile_cols(k, t)
            cut = min(total, 64)

            def rows_step(i):
                rows = tile_rows(k, t, start + i * cut, cut)
                here = pl.ds(pl.multiple_of(i * cut, 16), cut)
                value = r.v[k][l, half, rows, cols].astype(F32)
                for source in sources:
                    value = value + source[here, :].astype(F32)
                if target is None:
                    r.v[k][l, half, rows, cols] = value.astype(BF16)
                else:
                    target[here, :] = value.astype(BF16)

            loop(total // cut, rows_step)

        def g_event(p, e):
            rows = tile_size(pieces[p][0]) // 2
            xr = rows // 2
            zr = xr // shards
            x_first, x_gather = X_FIRST[p] == 1, X_GATHER[p] == 1
            here = c * rows + x * xr

            def wait(*stages):
                for stage in stages:
                    g_copy(p, stage).wait_recv()

            def start(*stages):
                for stage in stages:
                    g_copy(p, *stage).start() if isinstance(stage, tuple) else g_copy(p, stage).start()

            def wait_rows(stage, count):
                if count:
                    drain(r.g_recv.at[p * G_RECV + stage], count)

            if e == 0:
                start(CO)
            elif e == 1:
                wait(CO)
                add_rows(p, rows, oy, c * rows, [r.co.at[p % len(TILES)]])
                start(XO if x_first else YO)
            elif e == 2:
                start(CW)
            elif e == 3 and x_first:
                wait(CW)
                add_rows(p, rows, y, c * rows, [r.cw.at[p]])
                start(XS)
            elif e == 3:
                wait(CW, YO)
                add_rows(p, rows, y, c * rows, [r.cw.at[p], r.yr.at[p]])
                start(XS)
            elif e == 8:
                wait(XO)
                add_rows(p, xr, oy, here, [r.yr.at[p]])
                start(YO)
            elif e == 4:
                wait(XS)
                sources = [r.xr.at[p]]
                if x_first:
                    wait(YO)
                    sources.append(r.yr.at[p, pl.ds(xr, xr)])
                add_rows(p, xr, y, here, sources)
                start(*to_z)
            elif e == 5:
                wait_rows(ZS, nz * zr)
                sources = [r.zr.at[p, step] for step in range(nz)]
                add_rows(p, zr, y, here + (z * zr if nz else 0), sources, r.fin.at[p])
                start(*([AX] if x_gather else gather))
                start(OWN)
            elif e == 6 and x_gather:
                wait(AX)
                start(*gather, *on_z)
            elif e == 6:
                wait_rows(OWN, zr * (1 + nz))
                start(AX)
            elif e == 7:
                if x_gather:
                    wait_rows(OWN, zr * (1 + 2 * nz))
                else:
                    wait(AX)
                start(AC)

        backward_plan = iter(BACKWARD)

        def gradients_here():
            for code in next(backward_plan):
                p, e = divmod(code, 16)
                if p < len(pieces):
                    g_event(p, e)
                else:
                    edge_event(e // 2, e % 2 == 1)

        def g_end():
            sizes = [tile_size(k) // 2 for k, _, _ in pieces]
            drain(r.g_recv.at[len(pieces) * G_RECV], sum(sizes))
            for p, rows in enumerate(sizes):
                xr = rows // 2
                sent = 3 * rows + xr + (2 * xr if X_FIRST[p] else rows)
                sent += xr // shards * (nz + (2 * nz + 1 if X_GATHER[p] else nz))
                sent += 0 if X_GATHER[p] else xr
                drain(r.g_send.at[p], sent)

        def small_copy(step):
            dev = [dev_core, dev_y, dev_x][step] if step < 3 else dev_z(step - 2)
            return pltpu.make_async_remote_copy(
                src_ref=r.sm.at[min(step, 3)],
                dst_ref=r.smr.at[step],
                send_sem=r.s_send.at[step],
                recv_sem=r.s_recv.at[step],
                device_id=dev,
                device_id_type=MESH,
            )

        def small_sum(step):
            if step < 3:
                small_copy(step).wait_recv()
                r.sm[step + 1] = r.sm[step] + r.smr[step]
            else:
                total = r.sm[3]
                for k in range(nz):
                    small_copy(3 + k).wait_recv()
                    total = total + r.smr[3 + k]
                own = heads * MEMORY_SLOTS
                mass = jnp.where(y == 0, total[2 * layers : 3 * layers, :own], total[2 * layers : 3 * layers, own:])
                r.total[...] = total
                r.total[2 * layers : 3 * layers, :own] = mass * (1.0 / count)
                small_out().start()

        def small_out():
            return load(4 + 4 * layers, r.total, small)

        tok_ld.wait()
        ag_ld.wait()
        fg_ld.wait()
        r.sm[0] = jnp.zeros(r.sm.shape[1:], F32)
        for l in range(layers):
            r.nrm[...] = rms(2 * l, ag[pl.ds(l, 1), :])
            weights_here()
            for turn in range(2):
                half = y if turn == 0 else oy
                slot = 2 * l + turn
                use = jnp.where(c == 1, slot, 2 * layers)
                if turn == 0:
                    w_ld[WI, l].wait()
                if slot:
                    state_sent(slot - 1, 0, 0)
                project(l, half)
                state_send(slot, 0, 0)
                weights_here()
                state_recv(slot, 0, 0)
                attend(l, half, use, weights_here if slot == 0 else None)
                weights_here()
            w_ld[WO, l].wait()
            attn_out(l)
            r.nrm[...] = rms(2 * l + 1, fg[pl.ds(l, 1), :])
            weights_here()
            w_ld[F1, l].wait()
            w_ld[F2, l].wait()
            r.acc[...] = r.h[2 * l + 1].astype(F32)
            ffn(l, 0, half_tiles)
            weights_here()
            for tile in range(half_tiles, tiles):
                ffn(l, tile, tile + 1)
                weights_here()
            r.h[2 * l + 2] = r.acc[...].astype(BF16)
        gradients_here()
        w_end()
        state_sent(2 * layers - 1, 0, 0)
        cot_ld.wait()
        for l in range(layers):
            lm = r.lm[l].reshape(2 * heads * 64, 128).T
            r.sm[0, pl.ds(2 * layers + l, 1), :] = lm[0:1, :]

        for l in reversed(range(layers)):
            r.nT[...] = rms(2 * l + 1, fg[pl.ds(l, 1), :]).T
            r.acc[...] = jnp.zeros(r.acc.shape, F32)
            for tile in range(tiles):
                ffn_back(l, tile, tile + 1)
                gradients_here()
            rms_back(2 * l + 1, fg[pl.ds(l, 1), :], r.acc[...], layers + l)
            gradients_here()
            mixed_back(l)
            attn_out_grad(l)
            gradients_here()
            r.nT[...] = rms(2 * l, ag[pl.ds(l, 1), :]).T
            r.acc[...] = jnp.zeros(r.acc.shape, F32)
            for turn in range(2):
                half = oy if turn == 0 else y
                fwd_slot = jnp.where(c == 1, 2 * l + 1 - turn, 2 * layers)
                slot = 2 * l + turn
                use = jnp.where(c == 0, slot, 2 * layers)
                if not (turn == 0 and l == layers - 1):
                    prev = 2 * l if turn == 1 else 2 * (l + 1) + 1
                    state_sent(prev, 1, 1)
                attend_back(l, half, fwd_slot)
                state_send(slot, 1, 1)
                gradients_here()
                state_recv(slot, 1, 1)
                project_back(l, half, use)
                gradients_here()
            rms_back(2 * l, ag[pl.ds(l, 1), :], r.acc[...].T, l)
            if l == 0:
                small_copy(0).start()
            gradients_here()
        state_sent(1, 1, 1)
        for step in range(4):
            small_sum(step)
            if step < 2:
                small_copy(step + 1).start()
            elif step == 2:
                for k in range(nz):
                    small_copy(3 + k).start()
            gradients_here()
        for step in range(3 + nz):
            small_copy(step).wait_send()
        small_out().wait()
        g_end()
        edge_end()

    L = layers
    nzb = max(nz, 1)
    scratch = dict(
        v=[pltpu.VMEM((L, 2, *dims[k]), BF16) for k in KINDS],
        h=pltpu.VMEM((2 * L + 1, HALF, width), BF16),
        nT=pltpu.VMEM((width, HALF), BF16),
        nrm=pltpu.VMEM((HALF, width), BF16),
        ag=pltpu.VMEM((L, width), F32),
        fg=pltpu.VMEM((L, width), F32),
        total=pltpu.VMEM((8, width), F32),
        g=pltpu.VMEM((HALF, width), BF16),
        pj=pltpu.VMEM((L, 2 * heads, HALF, 256), BF16),
        pjT=pltpu.VMEM((L, 2 * heads, 256, HALF), BF16),
        rz=pltpu.VMEM((L, 2 * heads, 64, HALF), F32),
        pr=pltpu.VMEM((L, 2 * heads, 64, HALF), BF16),
        sc=pltpu.VMEM((L, 2 * heads, 64, HALF), BF16),
        mixT=pltpu.VMEM((L, 2 * heads, 64, HALF), BF16),
        lm=pltpu.VMEM((L, 2 * heads, 64, 128), F32),
        before=pltpu.VMEM((L, tiles, HALF, 512), BF16),
        actT=pltpu.VMEM((512, HALF), BF16),
        acc=pltpu.VMEM((HALF, width), F32),
        tmp=pltpu.VMEM((heads, 192, HALF), F32),
        tri=pltpu.VMEM((BLK, BLK), BF16),
        state_out=pltpu.VMEM((2, heads, 256, 128), BF16),
        state_in=pltpu.VMEM((2 * L + 1, heads, 256, 128), BF16),
        sm=pltpu.VMEM((4, 8, width), F32),
        smr=pltpu.VMEM((3 + nzb, 8, width), F32),
        co=pltpu.VMEM((len(TILES), 256, 512), BF16),
        cw=pltpu.VMEM((len(pieces), 256, 512), BF16),
        edge=pltpu.VMEM((2, HALF, 256), BF16),
        yr=pltpu.VMEM((len(pieces), 256, 512), BF16),
        xr=pltpu.VMEM((len(pieces), 128, 512), BF16),
        zr=pltpu.VMEM((len(pieces), nzb, 128 // shards, 512), BF16),
        fin=pltpu.VMEM((len(pieces), 128 // shards, 512), BF16),
        ld_sem=pltpu.SemaphoreType.DMA((5 + 4 * L,)),
        w_send=pltpu.SemaphoreType.DMA((L,)),
        w_recv=pltpu.SemaphoreType.DMA((W_RECV * len(ITEMS),)),
        st_send=pltpu.SemaphoreType.DMA((2 * L,)),
        st_recv=pltpu.SemaphoreType.DMA((2 * L,)),
        o_send=pltpu.SemaphoreType.DMA((1,)),
        o_recv=pltpu.SemaphoreType.DMA((3,)),
        g_send=pltpu.SemaphoreType.DMA((len(pieces),)),
        g_recv=pltpu.SemaphoreType.DMA((len(pieces) * G_RECV + 1,)),
        s_send=pltpu.SemaphoreType.DMA((3 + nzb,)),
        s_recv=pltpu.SemaphoreType.DMA((3 + nzb,)),
    )
    flat, layout = jax.tree.flatten(scratch)
    return kernel, flat


def finish(layers, width, out, ig, small, grads):
    steps = 2 * layers
    own = width // 2

    def kernel(out_in, ig_in, small_in, wi, wo, f1, f2, *results):
        out_to, ig_to, wi_to, wo_to, ag_to, f1_to, f2_to, fg_to, mass_to = results
        out_to[...] = out_in[...]
        ig_to[...] = ig_in[...]
        for source, target in ((wi, wi_to), (wo, wo_to), (f1, f1_to), (f2, f2_to)):
            target[...] = source[...].astype(F32)
        ag_to[...] = small_in[0:layers, :]
        fg_to[...] = small_in[layers : 2 * layers, :]
        mass_to[...] = small_in[2 * layers : 3 * layers, :own]

    edge = pl.BlockSpec((out.shape[0] // steps, out.shape[1]), lambda i: (i, 0))

    def part(v):
        return pl.BlockSpec((1, v.shape[1] // 2, v.shape[2]), lambda i: (i // 2, i % 2, 0))

    def whole(*shape):
        return pl.BlockSpec(shape, lambda i: (0, 0))

    like = [jax.ShapeDtypeStruct(v.shape, F32) for v in grads]
    gain = jax.ShapeDtypeStruct((layers, width), F32)
    mass = jax.ShapeDtypeStruct((layers, own), F32)
    edges = [jax.ShapeDtypeStruct(out.shape, BF16)] * 2
    gain_spec, mass_spec = whole(layers, width), whole(layers, own)
    parts = [part(v) for v in grads]
    return pl.pallas_call(
        kernel,
        grid=(steps,),
        in_specs=[edge, edge, whole(*small.shape), *parts],
        out_specs=[edge, edge, *parts[:2], gain_spec, *parts[2:], gain_spec, mass_spec],
        out_shape=[*edges, *like[:2], gain, *like[2:], gain, mass],
        compiler_params=pltpu.CompilerParams(vmem_limit_bytes=60 * 1024 * 1024),
    )(out, ig, small, *grads)


def solution(mesh):
    n_dp = mesh.shape["dp"]
    dp_inside = n_dp in (2, 4)

    def local(tokens, attn_gain, w_in, w_out, ffn_gain, ffn_in, ffn_out, cotangent):
        layers, width = attn_gain.shape
        arrays = (w_in, w_out, ffn_in, ffn_out)
        dims = [v.shape[1:] for v in arrays]
        kernel, scratch = make_kernel(
            layers, dims, n_dp, dp_inside, tokens.shape[0] * n_dp
        )
        anyspace = pl.BlockSpec(memory_space=pl.ANY)
        vmem = pl.BlockSpec(memory_space=pltpu.VMEM)
        edge = jax.ShapeDtypeStruct((tokens.shape[0], width // 4), BF16)
        results = pl.pallas_call(
            kernel,
            out_shape=[edge, edge]
            + [jax.ShapeDtypeStruct(v.shape, BF16) for v in arrays]
            + [jax.ShapeDtypeStruct((8, width), F32)],
            in_specs=[anyspace] * 8,
            out_specs=[anyspace] * 7,
            scratch_shapes=scratch,
            compiler_params=pltpu.CompilerParams(
                collective_id=0, has_side_effects=True, vmem_limit_bytes=63 * 1024 * 1024
            ),
        )(tokens, attn_gain, ffn_gain, cotangent, *arrays)
        out, ig, *grads, small = results
        if not dp_inside and n_dp > 1:
            grads = [lax.psum(v, "dp") for v in grads]
            small = lax.psum(small, "dp")
        return finish(layers, width, out, ig, small, grads)

    placed = (
        P("dp", None),
        P(),
        P(None, None, "tensor"),
        P(None, "tensor", None),
        P(),
        P(None, None, "tensor"),
        P(None, "tensor", None),
        P("dp", None),
    )
    return jax.shard_map(
        local,
        mesh=mesh,
        in_specs=placed,
        out_specs=(
            P("dp", "section"),
            P("dp", "section"),
            P(None, None, "tensor"),
            P(None, "tensor", None),
            P(),
            P(None, None, "tensor"),
            P(None, "tensor", None),
            P(),
            P(None, "tensor"),
        ),
        check_vma=False,
    )
```
